32 devices in a mesh: cfg: 2 (over x), blk: 4 (over z), uly: 4 (over y, core).
Axes of the slice: x: 2, y: 2, z: 4, core: 2. Of those that a mesh axis runs over, the one named last changes fastest.
Arguments:
- new_queries: bfloat16 [4096, 6144], P(('cfg', 'blk', 'uly')), parts along dimension 0, may hold values from -15 to 15
- new_keys: bfloat16 [4096, 6144], P(('cfg', 'blk', 'uly')), parts along dimension 0, may hold values from -6 to 6
- new_values: bfloat16 [4096, 6144], P(('cfg', 'blk', 'uly')), parts along dimension 0, may hold values from -6 to 6
- context_keys: bfloat16 [8192, 6144], P(('cfg', 'blk'), 'uly'), parts along dimension 0, may hold values from -6 to 6
- context_values: bfloat16 [8192, 6144], P(('cfg', 'blk'), 'uly'), parts along dimension 0, may hold values from -6 to 6
- keep_flags: int32 [16, 48], replicated, may hold values from 0 to 1, as said below
Outputs:
- attended: bfloat16 [4096, 6144], P(('cfg', 'blk', 'uly')), parts along dimension 0
The draws below stay inside these ranges and needn't reach their ends.
There are 2 independent parts, one for each index of `cfg`. The reference program is written for one: setup_inputs(seed, part) draws one part's arguments, and reference() takes and returns one part's arrays. A program takes and returns all parts, laid end to end along the dimension named above; an argument that names none is the same for every part. Nothing has to cross between parts.
Inputs may be any that keep to these rules, and one draw needn't show every extreme that they name: keep_flags[i, 0] and keep_flags[i, 32 + i] are 1 for every query block i; at least one query block keeps every key block.
All inputs are finite; a program needn't handle non-finite values.
Results may differ from the reference program's by a relative error of at most 0.017.
Values may be sent and summed in bfloat16 or wider, within the bound.
No kernel may reach another device: no remote copies, remote signals or barrier semaphores. Data moves between devices by JAX's collectives and lax.ppermute only.
A program may use at most 128 MiB of HBM per device.

```python
import jax
import jax.numpy as jnp
from jax import lax

H = 48
DH = 128
D = 6144
TILE = 128
CH = 2048
CTX = 4096
QT = 16
KT = 48


def draw_new_queries(key, part):
    key = jax.random.fold_in(key, 11)
    base = jnp.clip(2.5 * jax.random.normal(key, (CH, D), jnp.float32), -15.0, 15.0)
    return base.astype(jnp.bfloat16)


def draw_context_keys(key, part):
    key = jax.random.fold_in(key, 12)
    base = jnp.clip(jax.random.normal(key, (CTX, D), jnp.float32), -6.0, 6.0)
    return base.astype(jnp.bfloat16)


def draw_keep_flags(key, part):
    key = jax.random.fold_in(key, 13)
    roll_key, pick_key, extra_key = jax.random.split(key, 3)
    query_tile = jnp.arange(QT)[:, None]
    key_tile = jnp.arange(KT)[None, :]
    distance = jnp.abs(CTX // TILE + query_tile - key_tile)
    threshold = 4096 // (4 + distance)
    rolled = jax.random.randint(roll_key, (QT, KT), 0, 1024)
    chosen = jax.random.randint(pick_key, (), 0, QT)
    extra = jax.random.randint(extra_key, (QT,), 0, 16) == 0
    global_rows = (jnp.arange(QT) == chosen) | extra
    kept = (rolled < threshold) | (key_tile == 0) | (distance == 0) | global_rows[:, None]
    return kept.astype(jnp.int32)


def block_levels(key, extent, pieces, low, largest):
    def one(position, shards_of):
        steps = jax.random.uniform(jax.random.fold_in(jax.random.fold_in(key, 6), position), (shards_of,), jnp.float32, low / len(pieces), largest / len(pieces))
        return jnp.repeat(jnp.exp(steps), extent[position] // shards_of).reshape((-1,) + (1,) * (len(extent) - position - 1))

    loudness = one(*pieces[0])
    for cut in pieces[1:]:
        loudness = loudness * one(*cut)
    return loudness


def noise(rng, extent, scale, limit, shards=(), kind=jnp.bfloat16):
    gain = block_levels(rng, extent, shards, -0.22, 0.18) if shards else 1.0
    array = jax.random.normal(rng, extent, jnp.float32) * scale * gain
    return jnp.minimum(jnp.maximum(array, -limit), limit).astype(kind)


def setup_inputs(seed: int = 0, part: int = 0) -> dict:
    streams_of = jax.random.split(jax.random.key(seed), 7)
    part_keys = jax.random.split(jax.random.fold_in(streams_of[6], part), 7)
    new_queries = draw_new_queries(jax.random.fold_in(jax.random.fold_in(streams_of[6], part), 71), part)
    new_keys = noise(part_keys[1], (CH, D), 1.0, 6.0, ((0, 16),))
    new_values = noise(part_keys[2], (CH, D), 1.0, 6.0, ((0, 16),))
    context_keys = draw_context_keys(jax.random.fold_in(jax.random.fold_in(streams_of[6], part), 71), part)
    context_values = noise(part_keys[4], (CTX, D), 1.0, 6.0, ((0, 4), (1, 4)))
    keep_flags = draw_keep_flags(jax.random.fold_in(streams_of[6], 71), part)
    return dict(new_queries=new_queries, new_keys=new_keys, new_values=new_values, context_keys=context_keys, context_values=context_values, keep_flags=keep_flags)


def reference(new_queries, new_keys, new_values, context_keys, context_values, keep_flags):
    all_keys = jnp.concatenate([context_keys, new_keys], axis=0)
    all_values = jnp.concatenate([context_values, new_values], axis=0)
    query_count = new_queries.shape[0]
    key_count = all_keys.shape[0]
    allowed = jnp.repeat(jnp.repeat(keep_flags > 0, TILE, axis=0), TILE, axis=1)
    query_heads = new_queries.reshape(query_count, H, DH).transpose(1, 0, 2)
    key_heads = all_keys.reshape(key_count, H, DH).transpose(1, 0, 2)
    value_heads = all_values.reshape(key_count, H, DH).transpose(1, 0, 2)

    def one_head(head_items):
        scores = jnp.dot(head_items[0], head_items[1].T, preferred_element_type=jnp.float32) * (DH ** -0.5)
        scores = jnp.where(allowed, scores, -1.0e30)
        row_max = jnp.max(scores, axis=1, keepdims=True)
        probs = jnp.where(allowed, jnp.exp(scores - row_max), 0.0)
        denom = jnp.sum(probs, axis=1, keepdims=True)
        summed = jnp.dot(probs.astype(jnp.bfloat16), head_items[2], preferred_element_type=jnp.float32)
        return (summed / denom).astype(jnp.bfloat16)

    outputs = lax.map(one_head, (query_heads, key_heads, value_heads))
    return outputs.transpose(1, 0, 2).reshape(query_count, H * DH)
```

```python
import functools

import jax
import jax.numpy as jnp
from jax import lax
from jax.experimental import pallas as pl
from jax.experimental.pallas import tpu as pltpu
from jax.sharding import PartitionSpec as P

DH = 128
TILE = 128
PIECES = ((0, 1), (1, 1), (2, 1))
PIECE_UNITS = 3
HALF = 256
CHUNK = 256
LOG2E = 1.4426950408889634
TINY = 1.0e-30
ONES = 16
SCALE2 = DH ** (-0.5) * LOG2E
MASKED = -1.0e30
MIB = 1024 * 1024
QUICK = pl.CostEstimate(flops=1024, bytes_accessed=1024, transcendentals=0)


def split3(x):
    hi = x.astype(jnp.bfloat16).astype(jnp.float32)
    rest = x - hi
    mid = rest.astype(jnp.bfloat16).astype(jnp.float32)
    lo = (rest - mid).astype(jnp.bfloat16).astype(jnp.float32)
    return hi, mid, lo


def stat_rows(width):
    return -(-3 * (width // DH) // 16) * 16


def attend_kernel(deltas, table_ref, kept_ref, *refs):
    count = len(deltas)
    q_refs = refs[:count]
    ck_ref, nk_ref, cv_ref, nv_ref = refs[count : count + 4]
    out_ref, q_s, s0, s1, m0, m1, stat_s = refs[-7:]
    rows = q_s.shape[0]
    width = q_s.shape[1] // 2
    heads = width // DH
    ctx, new = ck_ref.shape[0], nk_ref.shape[0]
    subs = HALF // TILE
    halves = rows // HALF
    slots = ((s0, m0), (s1, m1))
    nt = (((1,), (1,)), ((), ()))
    target = table_ref[1 + pl.program_id(0)]
    first_tile = target * (rows // TILE)
    stat_s[...] = jnp.zeros_like(stat_s)
    for delta, q_ref in zip(deltas, q_refs):

        @pl.when(target - table_ref[0] == delta)
        def _():
            for head in range(heads):
                scaled = q_ref[:, head * DH : (head + 1) * DH].astype(jnp.float32) * SCALE2
                hi = scaled.astype(jnp.bfloat16)
                q_s[:, 2 * head * DH : (2 * head + 1) * DH] = hi
                q_s[:, (2 * head + 1) * DH : (2 * head + 2) * DH] = (scaled - hi.astype(jnp.float32)).astype(jnp.bfloat16)

    def columns(head, size=DH):
        return pl.ds(pl.multiple_of(head * size, size), size)

    chunks = [(k, v, at, base) for k, v, size, base in ((ck_ref, cv_ref, ctx, 0), (nk_ref, nv_ref, new, ctx))
              for at in range(0, size, CHUNK)]

    def kept(half, sub, row):
        return kept_ref[first_tile + half * subs + sub, row // TILE] > 0

    def score(head, half, chunk, q, tops):
        s_ref = slots[half % 2][0]
        k_ref, _, at, base = chunk
        size = min(CHUNK, k_ref.shape[0] - at)
        k = k_ref[at : at + size, columns(head)]
        scores = lax.dot_general(jnp.concatenate([k, k], axis=1), q, nt, preferred_element_type=jnp.float32)
        s_ref[base + at : base + at + size, :] = scores
        for j in range(0, size, TILE):
            for sub in range(subs):
                piece = scores[j : j + TILE, sub * TILE : (sub + 1) * TILE]
                top = jnp.max(piece.reshape(TILE // 8, 8, TILE), axis=0)
                top = jnp.where(kept(half, sub, base + at + j), top, MASKED)
                tops[sub] = top if tops[sub] is None else jnp.maximum(tops[sub], top)

    def weigh(head, half, chunk, high):
        s_ref = slots[half % 2][0]
        _, v_ref, at, base = chunk
        size = min(CHUNK, v_ref.shape[1] - at)
        lows = []
        for j in range(0, size, TILE):
            row = base + at + j
            pieces = []
            for sub in range(subs):
                lanes = slice(sub * TILE, (sub + 1) * TILE)
                less = jnp.where(kept(half, sub, row), high[:, lanes], -MASKED)
                pieces.append(jnp.exp2(s_ref[row : row + TILE, lanes] - less).astype(jnp.bfloat16))
            lows.append(jnp.concatenate(pieces, axis=1))
        low = jnp.concatenate(lows, axis=0)
        values = jnp.concatenate([v_ref[columns(head), at : at + size], jnp.ones((ONES, size), jnp.bfloat16)], axis=0)
        return jnp.dot(values, low, preferred_element_type=jnp.float32)

    def step(head, half, next_head, next_half, both=True):
        q = q_s[next_half * HALF : (next_half + 1) * HALF, columns(next_head, 2 * DH)]
        tops = [None] * subs
        if both:
            high = jnp.max(slots[half % 2][1][...], axis=0, keepdims=True)
            acc = None
        for chunk in chunks:
            score(next_head, next_half, chunk, q, tops)
            if both:
                found = weigh(head, half, chunk, high)
                acc = found if acc is None else acc + found
        for sub in range(subs):
            slots[next_half % 2][1][:, sub * TILE : (sub + 1) * TILE] = tops[sub]
        if both:
            total = jnp.maximum(acc[DH : DH + 1, :], TINY)
            lanes = slice(half * HALF, (half + 1) * HALF)
            out_ref[0, columns(head), lanes] = (acc[:DH, :] * (1.0 / total)).astype(jnp.bfloat16)
            for part, value in enumerate(split3(high + jnp.log2(total))):
                stat_s[pl.ds(3 * head + part, 1), lanes] = value

    step(0, 1, 0, 0, both=False)

    @pl.loop(0, heads)
    def _(head):
        for half in range(halves):
            if half + 1 < halves:
                step(head, half, head, half + 1)
            else:
                step(head, half, jnp.minimum(head + 1, heads - 1), 0)

    out_ref[0, width:, :] = stat_s[...].astype(jnp.bfloat16)


def attend(order, kept, queries, ctx_k, new_k, ctx_v, new_v, piece, blocks, out_blocks, dep):
    deltas = sorted(queries)
    rows, width = queries[deltas[0]].shape
    ctx, new = ctx_k.shape[0], new_k.shape[0]
    heads = width // DH
    keys = ctx + new
    across = lambda i, t, b: (0, piece)
    down = lambda i, t, b: (piece, 0)
    at = (lambda i, t, b: (0, 0, 0)) if out_blocks == 1 else (lambda i, t, b: (t[1 + i], 0, 0))
    prow = width + stat_rows(width)
    return pl.pallas_call(
        functools.partial(attend_kernel, deltas),
        out_shape=jax.ShapeDtypeStruct((out_blocks, prow, rows), jnp.bfloat16),
        grid_spec=pltpu.PrefetchScalarGridSpec(
            num_scalar_prefetch=2,
            grid=(blocks,),
            in_specs=[pl.BlockSpec((rows, width), lambda i, t, b: (0, 0))] * len(deltas)
            + [
                pl.BlockSpec((ctx, width), across),
                pl.BlockSpec((new, width), across),
                pl.BlockSpec((width, ctx), down),
                pl.BlockSpec((width, new), down),
                pl.BlockSpec(memory_space=pl.ANY),
            ],
            out_specs=pl.BlockSpec((1, prow, rows), at),
            scratch_shapes=[
                pltpu.VMEM((rows, 2 * width), jnp.bfloat16),
                pltpu.VMEM((keys, HALF), jnp.float32),
                pltpu.VMEM((keys, HALF), jnp.float32),
                pltpu.VMEM((8, HALF), jnp.float32),
                pltpu.VMEM((8, HALF), jnp.float32),
                pltpu.VMEM((stat_rows(width), rows), jnp.float32),
            ],
        ),
        compiler_params=pltpu.CompilerParams(vmem_limit_bytes=28 * MIB),
        cost_estimate=pl.CostEstimate(
            flops=8 * blocks * rows * keys * DH * heads,
            bytes_accessed=4 * blocks * rows * width + 4 * keys * width,
            transcendentals=blocks * rows * keys * heads,
        ),
        name="attend",
    )(order, kept, *[queries[d] for d in deltas], ctx_k, new_k, ctx_v, new_v, dep)


def load_stats(ref, lead, width):
    terms = ref[lead + (slice(width, None), slice(None))].astype(jnp.float32)
    return [
        terms[3 * h : 3 * h + 1, :] + terms[3 * h + 1 : 3 * h + 2, :] + terms[3 * h + 2 : 3 * h + 3, :]
        for h in range(width // DH)
    ]


def merge_one(own_ref, far_ref, got_ref, out_ref, stat_ref, use_far, got_ok):
    width = out_ref.shape[0] - stat_ref.shape[0]
    own_stats = load_stats(own_ref, (0,), width)
    far_stats = load_stats(far_ref, (0,), width)
    got_stats = load_stats(got_ref, (), width)
    stat_ref[...] = jnp.zeros_like(stat_ref)
    for head in range(width // DH):
        at = slice(head * DH, (head + 1) * DH)
        a = jnp.where(use_far, far_stats[head], own_stats[head])
        g = jnp.where(got_ok, got_stats[head], MASKED)
        top = jnp.maximum(a, g)
        wa = jnp.exp2(a - top)
        wg = jnp.exp2(g - top)
        total = wa + wg
        share = wg / total
        mine = jnp.where(use_far, far_ref[0, at, :], own_ref[0, at, :]).astype(jnp.float32)
        theirs = got_ref[at, :].astype(jnp.float32)
        out_ref[at, :] = (mine + share * (theirs - mine)).astype(jnp.bfloat16)
        for part, value in enumerate(split3(top + jnp.log2(total))):
            stat_ref[3 * head + part : 3 * head + part + 1, :] = value
    out_ref[width:, :] = stat_ref[...].astype(jnp.bfloat16)


def merge_kernel(n, info_ref, own_r, own_l, far_ref, got_r, got_l, dep, out_r, out_l, stat_ref):
    place, ahead, far = info_ref[0], info_ref[1], info_ref[2]

    @pl.when(place + ahead <= n - 1)
    def _():
        merge_one(own_r, far_ref, got_r, out_r, stat_ref, place + ahead == far, place > 0)

    @pl.when(place - ahead >= 0)
    def _():
        merge_one(own_l, far_ref, got_l, out_l, stat_ref, place - ahead == far, place < n - 1)


def merge(info, n, width, own, far, got_r, got_l, dep):
    _, prow, rows = own.shape
    whole = pl.BlockSpec((prow, rows), lambda i, t: (0, 0))
    return pl.pallas_call(
        functools.partial(merge_kernel, n),
        out_shape=[jax.ShapeDtypeStruct((prow, rows), jnp.bfloat16)] * 2,
        grid_spec=pltpu.PrefetchScalarGridSpec(
            num_scalar_prefetch=1,
            grid=(1,),
            in_specs=[
                pl.BlockSpec((1, prow, rows), lambda i, t: (jnp.minimum(t[0] + t[1], n - 1), 0, 0)),
                pl.BlockSpec((1, prow, rows), lambda i, t: (jnp.maximum(t[0] - t[1], 0), 0, 0)),
                pl.BlockSpec((1, prow, rows), lambda i, t: (0, 0, 0)),
                whole,
                whole,
                pl.BlockSpec(memory_space=pl.ANY),
            ],
            out_specs=[whole, whole],
            scratch_shapes=[pltpu.VMEM((prow - width, rows), jnp.float32)],
        ),
        compiler_params=pltpu.CompilerParams(vmem_limit_bytes=16 * MIB),
        cost_estimate=QUICK,
        name="merge",
    )(info, own, own, far, got_r, got_l, dep)


def finish_kernel(n, info_ref, own_ref, got_r, got_l, dep, out_ref):
    place = info_ref[0]
    rows, width = out_ref.shape
    own_stats = load_stats(own_ref, (0,), width)
    r_stats = load_stats(got_r, (), width)
    l_stats = load_stats(got_l, (), width)
    for head in range(width // DH):
        at = slice(head * DH, (head + 1) * DH)
        a = own_stats[head]
        r = jnp.where(place > 0, r_stats[head], MASKED)
        l = jnp.where(place < n - 1, l_stats[head], MASKED)
        top = jnp.maximum(jnp.maximum(a, r), l)
        wa, wr, wl = jnp.exp2(a - top), jnp.exp2(r - top), jnp.exp2(l - top)
        total = wa + wr + wl
        mine = own_ref[0, at, :].astype(jnp.float32)
        from_r = got_r[at, :].astype(jnp.float32)
        from_l = got_l[at, :].astype(jnp.float32)
        value = mine + (wr / total) * (from_r - mine) + (wl / total) * (from_l - mine)
        out_ref[:, at] = jnp.transpose(value).astype(jnp.bfloat16)


def finish(info, n, width, own, got_r, got_l, dep):
    _, prow, rows = own.shape
    whole = pl.BlockSpec((prow, rows), lambda i, t: (0, 0))
    return pl.pallas_call(
        functools.partial(finish_kernel, n),
        out_shape=jax.ShapeDtypeStruct((rows, width), jnp.bfloat16),
        grid_spec=pltpu.PrefetchScalarGridSpec(
            num_scalar_prefetch=1,
            grid=(1,),
            in_specs=[
                pl.BlockSpec((1, prow, rows), lambda i, t: (t[0], 0, 0)),
                whole,
                whole,
                pl.BlockSpec(memory_space=pl.ANY),
            ],
            out_specs=pl.BlockSpec((rows, width), lambda i, t: (0, 0)),
        ),
        compiler_params=pltpu.CompilerParams(vmem_limit_bytes=16 * MIB),
        cost_estimate=QUICK,
        name="finish",
    )(info, own, got_r, got_l, dep)


def part_kernel(peers, peer_ref, *refs):
    rows = refs[0].shape[0]
    for k in range(peers):
        target = refs[k - peers]
        target[:rows, :] = refs[k][...]
        target[rows:, :] = refs[peers + k][...]


def parts_for_peers(peer, upper, lower, peers, dep):
    rows, group = upper.shape[0], upper.shape[1] // peers
    specs = [pl.BlockSpec((rows, group), functools.partial(lambda k, i, t: (0, t[0] ^ k), k)) for k in range(peers)]
    return pl.pallas_call(
        functools.partial(part_kernel, peers),
        out_shape=[jax.ShapeDtypeStruct((2 * rows, group), jnp.bfloat16)] * peers,
        grid_spec=pltpu.PrefetchScalarGridSpec(
            num_scalar_prefetch=1,
            grid=(1,),
            in_specs=specs * 2 + [pl.BlockSpec(memory_space=pl.ANY)],
            out_specs=[pl.BlockSpec((2 * rows, group), lambda i, t: (0, 0))] * peers,
        ),
        compiler_params=pltpu.CompilerParams(vmem_limit_bytes=24 * MIB),
        cost_estimate=QUICK,
        name="parts",
    )(peer.reshape(1), *[upper] * peers, *[lower] * peers, dep)


def join_kernel(*refs):
    pieces, (k_ref, v_ref, v_s) = refs[:-4], refs[-3:]
    rows = pieces[0].shape[0] // 2
    for i, piece in enumerate(pieces):
        k_ref[i * rows : (i + 1) * rows, :] = piece[:rows, :]
        v_s[i * rows : (i + 1) * rows, :] = piece[rows:, :]
    for at in range(0, v_s.shape[0], TILE):
        v_ref[:, at : at + TILE] = jnp.transpose(v_s[at : at + TILE, :])


def joined(pieces, dep):
    rows, group = pieces[0].shape[0] // 2 * len(pieces), pieces[0].shape[1]
    return pl.pallas_call(
        join_kernel,
        out_shape=[
            jax.ShapeDtypeStruct((rows, group), jnp.bfloat16),
            jax.ShapeDtypeStruct((group, rows), jnp.bfloat16),
        ],
        in_specs=[pl.BlockSpec(memory_space=pltpu.VMEM)] * len(pieces) + [pl.BlockSpec(memory_space=pl.ANY)],
        scratch_shapes=[pltpu.VMEM((rows, group), jnp.bfloat16)],
        compiler_params=pltpu.CompilerParams(vmem_limit_bytes=24 * MIB),
        cost_estimate=QUICK,
        name="join",
    )(*pieces, dep)


def hold_kernel(*refs):
    pass


def hold(arrays, dep):
    anywhere = pl.BlockSpec(memory_space=pl.ANY)
    return pl.pallas_call(
        hold_kernel,
        out_shape=[jax.ShapeDtypeStruct(a.shape, a.dtype) for a in arrays],
        in_specs=[anywhere] * (len(arrays) + 1),
        out_specs=[anywhere] * len(arrays),
        input_output_aliases={i: i for i in range(len(arrays))},
        cost_estimate=QUICK,
        name="hold",
    )(*arrays, dep)


def later_kernel(start, x_ref, dep, out_ref):
    out_ref[0] = x_ref[:, start:]


def later_columns(x, peers, start, dep):
    rows, group = x.shape[0], x.shape[1] // peers
    return pl.pallas_call(
        functools.partial(later_kernel, start),
        out_shape=jax.ShapeDtypeStruct((peers, rows, group - start), jnp.bfloat16),
        grid=(peers,),
        in_specs=[pl.BlockSpec((rows, group), lambda p: (0, p)), pl.BlockSpec(memory_space=pl.ANY)],
        out_specs=pl.BlockSpec((1, rows, group - start), lambda p: (p, 0, 0)),
        compiler_params=pltpu.CompilerParams(vmem_limit_bytes=16 * MIB),
        cost_estimate=QUICK,
        name="later",
    )(x, dep)


def shards(new_queries, new_keys, new_values, context_keys, context_values, keep_flags):
    n = lax.axis_size("blk")
    place = lax.axis_index("blk").astype(jnp.int32)
    peers = lax.axis_size("uly")
    own_rows = new_queries.shape[0]
    group = context_keys.shape[1]
    unit = group // PIECE_UNITS
    span_rows = own_rows * peers
    ctx_tiles, new_tiles = context_keys.shape[0] // TILE, span_rows // TILE

    peer = lax.axis_index("uly").astype(jnp.int32)
    new_order = jnp.arange(new_tiles, dtype=jnp.int32) ^ (peer * own_rows // TILE)
    new_kept = lax.dynamic_slice_in_dim(keep_flags, n * ctx_tiles + place * new_tiles, new_tiles, 1)
    kept = jnp.concatenate(
        [
            lax.dynamic_slice_in_dim(keep_flags, place * ctx_tiles, ctx_tiles, 1),
            jnp.sum(jnp.where(new_order[:, None] == jnp.arange(new_tiles), new_kept[:, None, :], 0), axis=2),
        ],
        axis=1,
    )
    kept = (kept == 1).astype(jnp.int32)
    far = jnp.where(place < n // 2, n - 1, 0).astype(jnp.int32)
    others = jnp.arange(n - 1, dtype=jnp.int32)
    others = jnp.where(far == 0, others + 1, n - 2 - others)
    far_order = jnp.stack([place, far])
    others = jnp.concatenate([place.reshape(1), others])

    count = len(PIECES)
    widths = [units * unit for _, units in PIECES]
    found = [None] * count
    fars, owns, got, backs = [None] * count, [None] * count, [None] * count, [None] * count

    def to_heads(pieces):
        moved = lax.all_to_all(pieces, "uly", split_axis=0, concat_axis=0, tiled=False)
        return moved.reshape(span_rows, pieces.shape[2])

    def pass_on(c, step):
        found[c][-step] = lax.ppermute(found[c][1 - step], "blk", [(i, i + 1) for i in range(step - 1, n - 1)])
        found[c][step] = lax.ppermute(found[c][step - 1], "blk", [(i, i - 1) for i in range(n - step, 0, -1)])

    early = widths[0]
    first_span = to_heads(jnp.stack([new_queries[:, p * group : p * group + early] for p in range(peers)]))
    found[0] = {0: first_span}
    pass_on(0, 1)
    rest = to_heads(later_columns(new_queries, peers, early, first_span))
    spans = [rest[:, first * unit - early : (first + units) * unit - early] for first, units in PIECES[1:]]
    spans = dict(zip(range(1, count), spans))
    pieces = parts_for_peers(peer, new_keys, new_values, peers, rest)
    moved = [lax.ppermute(p, "uly", [(i, i ^ k) for i in range(peers)]) if k else p for k, p in enumerate(pieces)]
    context_values_t = context_values.T
    last = [pieces[0]]
    new_kv = []

    def run_forward(*hops):
        keys, arrays = [], []
        for c, step in hops:
            for d in [0] if step == 1 else [1 - step, step - 1]:
                keys.append((c, d))
                arrays.append(spans[c] if step == 1 else found[c][d])
        held = hold(arrays, last[0])
        last[0] = held[0]
        for (c, d), array in zip(keys, held):
            if d == 0:
                found[c] = {}
            found[c][d] = array
        for c, step in hops:
            pass_on(c, step)

    def run_join():
        new_kv.extend(joined(moved, last[0]))
        last[0] = new_kv[0]

    def run_far(c):
        distant = {d: q for d, q in found[c].items() if abs(d) >= n // 2}
        fars[c] = attend(far_order, kept, distant, *work(c), 1, 1, last[0])
        last[0] = fars[c]
        both = lax.ppermute(fars[c][0], "blk", [(0, 1), (n - 1, n - 2)])
        got[c] = (both, both)

    def work(c):
        return context_keys, new_kv[0], context_values_t, new_kv[1], PIECES[c][0] // PIECES[c][1]

    def run_rest(c):
        nearer = {d: q for d, q in found[c].items() if abs(d) < n - 1}
        owns[c] = attend(others, kept, nearer, *work(c), n - 1, n, last[0])
        last[0] = owns[c]

    def run_merge(c, step):
        info = jnp.stack([place, jnp.int32(n - step), far])
        out_r, out_l = merge(info, n, widths[c], owns[c], fars[c], got[c][0], got[c][1], last[0])
        last[0] = out_r
        got[c] = (
            lax.ppermute(out_r, "blk", [(i, i + 1) for i in range(step)]),
            lax.ppermute(out_l, "blk", [(n - 1 - i, n - 2 - i) for i in range(step)]),
        )

    def run_finish(c):
        info = jnp.stack([place, jnp.int32(0), far])
        done = finish(info, n, widths[c], owns[c], got[c][0], got[c][1], last[0])
        last[0] = done
        done = done.reshape(peers, own_rows, widths[c])
        backs[c] = lax.all_to_all(done, "uly", split_axis=0, concat_axis=0, tiled=False)

    if n == 4 and count == 3:
        run_forward((0, 2), (1, 1))
        run_forward((0, 3), (1, 2))
        run_join()
        run_far(0)
        run_forward((1, 3), (2, 1))
        run_rest(0)
        run_merge(0, 2)
        run_forward((2, 2))
        run_far(1)
        run_forward((2, 3))
        run_merge(0, 3)
        run_rest(1)
        run_merge(1, 2)
        run_far(2)
        run_finish(0)
        run_merge(1, 3)
        run_rest(2)
        run_merge(2, 2)
        run_finish(1)
        run_merge(2, 3)
        run_finish(2)
    else:
        run_join()
        for c in range(count):
            for step in range(2 if c == 0 else 1, n):
                run_forward((c, step))
            run_far(c)
            run_rest(c)
            for step in range(2, n):
                run_merge(c, step)
            run_finish(c)

    in_order = [backs[c] for c in sorted(range(count), key=lambda c: PIECES[c][0])]
    together = jnp.concatenate(in_order, axis=2)
    return together.transpose(1, 0, 2).reshape(own_rows, peers * group)


def solution(mesh):
    in_specs = (
        P(("cfg", "blk", "uly"), None),
        P(("cfg", "blk", "uly"), None),
        P(("cfg", "blk", "uly"), None),
        P(("cfg", "blk"), "uly"),
        P(("cfg", "blk"), "uly"),
        P(),
    )
    out_specs = P(("cfg", "blk", "uly"), None)
    return jax.shard_map(shards, mesh=mesh, in_specs=in_specs, out_specs=out_specs, check_vma=False)
```

```python
import functools

import jax
import jax.numpy as jnp
from jax import lax
from jax.experimental import pallas as pl
from jax.experimental.pallas import tpu as pltpu
from jax.sharding import PartitionSpec as P

DH = 128
TILE = 128
PIECES = ((0, 1), (1, 1), (2, 1))
PIECE_UNITS = 3
HALF = 256
CHUNK = 256
LOG2E = 1.4426950408889634
TINY = 1.0e-30
ONES = 16
SCALE2 = DH ** (-0.5) * LOG2E
MASKED = -1.0e30
MIB = 1024 * 1024
QUICK = pl.CostEstimate(flops=1024, bytes_accessed=1024, transcendentals=0)


def split3(x):
    hi = x.astype(jnp.bfloat16).astype(jnp.float32)
    rest = x - hi
    mid = rest.astype(jnp.bfloat16).astype(jnp.float32)
    lo = (rest - mid).astype(jnp.bfloat16).astype(jnp.float32)
    return hi, mid, lo


def stat_rows(width):
    return -(-3 * (width // DH) // 16) * 16


def attend_kernel(distances, place_ref, kept_ref, *refs):
    count = len(distances)
    q_refs = refs[:count]
    ck_ref, nk_ref, cv_ref, nv_ref = refs[count : count + 4]
    out_ref, q_s, s0, s1, m0, m1, stat_s = refs[-7:]
    rows = q_s.shape[0]
    width = q_s.shape[1] // 2
    heads = width // DH
    ctx, new = ck_ref.shape[0], nk_ref.shape[0]
    subs = HALF // TILE
    halves = rows // HALF
    slots = ((s0, m0), (s1, m1))
    nt = (((1,), (1,)), ((), ()))
    distance = distances[0]
    for i in range(1, count):
        distance = jnp.where(pl.program_id(0) == i, distances[i], distance)
    first_tile = (place_ref[0] ^ distance) * (rows // TILE)
    stat_s[...] = jnp.zeros_like(stat_s)
    for i, q_ref in enumerate(q_refs):

        @pl.when(pl.program_id(0) == i)
        def _():
            for head in range(heads):
                scaled = q_ref[:, head * DH : (head + 1) * DH].astype(jnp.float32) * SCALE2
                hi = scaled.astype(jnp.bfloat16)
                q_s[:, 2 * head * DH : (2 * head + 1) * DH] = hi
                q_s[:, (2 * head + 1) * DH : (2 * head + 2) * DH] = (scaled - hi.astype(jnp.float32)).astype(jnp.bfloat16)

    def columns(head, size=DH):
        return pl.ds(pl.multiple_of(head * size, size), size)

    chunks = [(k, v, at, base) for k, v, size, base in ((ck_ref, cv_ref, ctx, 0), (nk_ref, nv_ref, new, ctx))
              for at in range(0, size, CHUNK)]

    def kept(half, sub, row):
        return kept_ref[first_tile + half * subs + sub, row // TILE] > 0

    def score(head, half, chunk, q, tops):
        s_ref = slots[half % 2][0]
        k_ref, _, at, base = chunk
        size = min(CHUNK, k_ref.shape[0] - at)
        k = k_ref[at : at + size, columns(head)]
        scores = lax.dot_general(jnp.concatenate([k, k], axis=1), q, nt, preferred_element_type=jnp.float32)
        s_ref[base + at : base + at + size, :] = scores
        for j in range(0, size, TILE):
            for sub in range(subs):
                piece = scores[j : j + TILE, sub * TILE : (sub + 1) * TILE]
                top = jnp.max(piece.reshape(TILE // 8, 8, TILE), axis=0)
                top = jnp.where(kept(half, sub, base + at + j), top, MASKED)
                tops[sub] = top if tops[sub] is None else jnp.maximum(tops[sub], top)

    def weigh(head, half, chunk, high):
        s_ref = slots[half % 2][0]
        _, v_ref, at, base = chunk
        size = min(CHUNK, v_ref.shape[1] - at)
        lows = []
        for j in range(0, size, TILE):
            row = base + at + j
            pieces = []
            for sub in range(subs):
                lanes = slice(sub * TILE, (sub + 1) * TILE)
                less = jnp.where(kept(half, sub, row), high[:, lanes], -MASKED)
                pieces.append(jnp.exp2(s_ref[row : row + TILE, lanes] - less).astype(jnp.bfloat16))
            lows.append(jnp.concatenate(pieces, axis=1))
        low = jnp.concatenate(lows, axis=0)
        values = jnp.concatenate([v_ref[columns(head), at : at + size], jnp.ones((ONES, size), jnp.bfloat16)], axis=0)
        return jnp.dot(values, low, preferred_element_type=jnp.float32)

    def step(head, half, next_head, next_half, both=True):
        q = q_s[next_half * HALF : (next_half + 1) * HALF, columns(next_head, 2 * DH)]
        tops = [None] * subs
        if both:
            high = jnp.max(slots[half % 2][1][...], axis=0, keepdims=True)
            acc = None
        for chunk in chunks:
            score(next_head, next_half, chunk, q, tops)
            if both:
                found = weigh(head, half, chunk, high)
                acc = found if acc is None else acc + found
        for sub in range(subs):
            slots[next_half % 2][1][:, sub * TILE : (sub + 1) * TILE] = tops[sub]
        if both:
            total = jnp.maximum(acc[DH : DH + 1, :], TINY)
            lanes = slice(half * HALF, (half + 1) * HALF)
            out_ref[0, columns(head), lanes] = (acc[:DH, :] * (1.0 / total)).astype(jnp.bfloat16)
            for part, value in enumerate(split3(high + jnp.log2(total))):
                stat_s[pl.ds(3 * head + part, 1), lanes] = value

    step(0, 1, 0, 0, both=False)

    @pl.loop(0, heads)
    def _(head):
        for half in range(halves):
            if half + 1 < halves:
                step(head, half, head, half + 1)
            else:
                step(head, half, jnp.minimum(head + 1, heads - 1), 0)

    out_ref[0, width:, :] = stat_s[...].astype(jnp.bfloat16)


def attend(place, kept, queries, distances, ctx_k, new_k, ctx_v, new_v, piece, dep):
    rows, width = queries[distances[0]].shape
    ctx, new = ctx_k.shape[0], new_k.shape[0]
    heads = width // DH
    keys = ctx + new
    blocks = len(distances)
    across = lambda i, t, b: (0, piece)
    down = lambda i, t, b: (piece, 0)
    prow = width + stat_rows(width)
    return pl.pallas_call(
        functools.partial(attend_kernel, distances),
        out_shape=jax.ShapeDtypeStruct((blocks, prow, rows), jnp.bfloat16),
        grid_spec=pltpu.PrefetchScalarGridSpec(
            num_scalar_prefetch=2,
            grid=(blocks,),
            in_specs=[pl.BlockSpec((rows, width), lambda i, t, b: (0, 0))] * blocks
            + [
                pl.BlockSpec((ctx, width), across),
                pl.BlockSpec((new, width), across),
                pl.BlockSpec((width, ctx), down),
                pl.BlockSpec((width, new), down),
                pl.BlockSpec(memory_space=pl.ANY),
            ],
            out_specs=pl.BlockSpec((1, prow, rows), lambda i, t, b: (i, 0, 0)),
            scratch_shapes=[
                pltpu.VMEM((rows, 2 * width), jnp.bfloat16),
                pltpu.VMEM((keys, HALF), jnp.float32),
                pltpu.VMEM((keys, HALF), jnp.float32),
                pltpu.VMEM((8, HALF), jnp.float32),
                pltpu.VMEM((8, HALF), jnp.float32),
                pltpu.VMEM((stat_rows(width), rows), jnp.float32),
            ],
        ),
        compiler_params=pltpu.CompilerParams(vmem_limit_bytes=28 * MIB),
        cost_estimate=pl.CostEstimate(
            flops=8 * blocks * rows * keys * DH * heads,
            bytes_accessed=4 * blocks * rows * width + 4 * keys * width,
            transcendentals=blocks * rows * keys * heads,
        ),
        name="attend",
    )(place, kept, *[queries[d] for d in distances], ctx_k, new_k, ctx_v, new_v, dep)


def combine(refs, width, emit):
    stats = []
    for ref in refs:
        terms = ref[0, width:, :].astype(jnp.float32)
        stats.append([terms[3 * h : 3 * h + 1] + terms[3 * h + 1 : 3 * h + 2] + terms[3 * h + 2 : 3 * h + 3]
                      for h in range(width // DH)])
    for head in range(width // DH):
        logs = [s[head] for s in stats]
        top = functools.reduce(jnp.maximum, logs)
        weights = [jnp.exp2(l - top) for l in logs]
        total = functools.reduce(jnp.add, weights)
        value = None
        for ref, weight in zip(refs, weights):
            part = ref[0, head * DH : (head + 1) * DH, :].astype(jnp.float32) * (weight / total)
            value = part if value is None else value + part
        emit(head, value, top + jnp.log2(total))


def merge_kernel(*refs):
    sources, (out_ref, stat_ref) = refs[:-3], refs[-2:]
    width = out_ref.shape[1] - stat_ref.shape[0]
    stat_ref[...] = jnp.zeros_like(stat_ref)

    def emit(head, value, log):
        out_ref[0, head * DH : (head + 1) * DH, :] = value.astype(jnp.bfloat16)
        for part, term in enumerate(split3(log)):
            stat_ref[3 * head + part : 3 * head + part + 1, :] = term

    combine(sources, width, emit)
    out_ref[0, width:, :] = stat_ref[...].astype(jnp.bfloat16)


def finish_kernel(*refs):
    sources, out_ref = refs[:-2], refs[-1]

    def emit(head, value, log):
        out_ref[:, head * DH : (head + 1) * DH] = jnp.transpose(value).astype(jnp.bfloat16)

    combine(sources, out_ref.shape[1], emit)


def join_parts(parts, width, dep, final):
    _, prow, rows = parts[0][0].shape
    specs = [pl.BlockSpec((1, prow, rows), functools.partial(lambda slot, i: (slot, 0, 0), slot)) for _, slot in parts]
    shape = (rows, width) if final else (1, prow, rows)
    return pl.pallas_call(
        finish_kernel if final else merge_kernel,
        out_shape=jax.ShapeDtypeStruct(shape, jnp.bfloat16),
        grid=(1,),
        in_specs=specs + [pl.BlockSpec(memory_space=pl.ANY)],
        out_specs=pl.BlockSpec(shape, lambda i: (0,) * len(shape)),
        scratch_shapes=[] if final else [pltpu.VMEM((prow - width, rows), jnp.float32)],
        compiler_params=pltpu.CompilerParams(vmem_limit_bytes=16 * MIB),
        cost_estimate=QUICK,
        name="finish" if final else "merge",
    )(*[array for array, _ in parts], dep)


def part_kernel(peers, count, start, peer_ref, *refs):
    rows = refs[0].shape[0]
    outs = refs[-peers:]
    for i, ref in enumerate(refs[: count * peers]):
        outs[i % peers][i // peers * rows : (i // peers + 1) * rows, :] = ref[:, start:]


def parts_for_peers(peer, arrays, start, peers, deps):
    rows, group = arrays[0].shape[0], arrays[0].shape[1] // peers
    specs = [pl.BlockSpec((rows, group), functools.partial(lambda k, i, t: (0, t[0] ^ k), k)) for k in range(peers)]
    shape = (len(arrays) * rows, group - start)
    return pl.pallas_call(
        functools.partial(part_kernel, peers, len(arrays), start),
        out_shape=[jax.ShapeDtypeStruct(shape, jnp.bfloat16)] * peers,
        grid_spec=pltpu.PrefetchScalarGridSpec(
            num_scalar_prefetch=1,
            grid=(1,),
            in_specs=specs * len(arrays) + [pl.BlockSpec(memory_space=pl.ANY)] * len(deps),
            out_specs=[pl.BlockSpec(shape, lambda i, t: (0, 0))] * peers,
        ),
        compiler_params=pltpu.CompilerParams(vmem_limit_bytes=28 * MIB),
        cost_estimate=QUICK,
        name="parts",
    )(peer.reshape(1), *[a for a in arrays for _ in range(peers)], *deps)


def regroup_kernel(peers, peer_ref, *refs):
    rows = refs[0].shape[0]
    for k in range(peers):
        here = pl.ds(pl.multiple_of((peer_ref[0] ^ k) * rows, rows), rows)
        start = 0
        for out_ref in refs[peers + 1 :]:
            width = out_ref.shape[1]
            out_ref[here, :] = refs[k][:, start : start + width]
            start += width


def regrouped(peer, pieces, widths, dep):
    peers, rows = len(pieces), pieces[0].shape[0]
    whole = lambda i, t: (0, 0)
    shapes = [(peers * rows, width) for width in widths]
    return pl.pallas_call(
        functools.partial(regroup_kernel, peers),
        out_shape=[jax.ShapeDtypeStruct(shape, jnp.bfloat16) for shape in shapes],
        grid_spec=pltpu.PrefetchScalarGridSpec(
            num_scalar_prefetch=1,
            grid=(1,),
            in_specs=[pl.BlockSpec(p.shape, whole) for p in pieces] + [pl.BlockSpec(memory_space=pl.ANY)],
            out_specs=[pl.BlockSpec(shape, whole) for shape in shapes],
        ),
        compiler_params=pltpu.CompilerParams(vmem_limit_bytes=16 * MIB),
        cost_estimate=QUICK,
        name="regroup",
    )(peer.reshape(1), *pieces, dep)


def join_kernel(*refs):
    pieces, (k_ref, v_ref, v_s) = refs[:-4], refs[-3:]
    rows = pieces[0].shape[0] // 2
    for i, piece in enumerate(pieces):
        k_ref[i * rows : (i + 1) * rows, :] = piece[:rows, :]
        v_s[i * rows : (i + 1) * rows, :] = piece[rows:, :]
    for at in range(0, v_s.shape[0], TILE):
        v_ref[:, at : at + TILE] = jnp.transpose(v_s[at : at + TILE, :])


def joined(pieces, dep):
    rows, group = pieces[0].shape[0] // 2 * len(pieces), pieces[0].shape[1]
    return pl.pallas_call(
        join_kernel,
        out_shape=[
            jax.ShapeDtypeStruct((rows, group), jnp.bfloat16),
            jax.ShapeDtypeStruct((group, rows), jnp.bfloat16),
        ],
        in_specs=[pl.BlockSpec(memory_space=pltpu.VMEM)] * len(pieces) + [pl.BlockSpec(memory_space=pl.ANY)],
        scratch_shapes=[pltpu.VMEM((rows, group), jnp.bfloat16)],
        compiler_params=pltpu.CompilerParams(vmem_limit_bytes=24 * MIB),
        cost_estimate=QUICK,
        name="join",
    )(*pieces, dep)


def shards(new_queries, new_keys, new_values, context_keys, context_values, keep_flags):
    n = lax.axis_size("blk")
    place = lax.axis_index("blk").astype(jnp.int32)
    peers = lax.axis_size("uly")
    own_rows = new_queries.shape[0]
    group = context_keys.shape[1]
    unit = group // PIECE_UNITS
    span_rows = own_rows * peers
    ctx_tiles, new_tiles = context_keys.shape[0] // TILE, span_rows // TILE

    peer = lax.axis_index("uly").astype(jnp.int32)
    new_order = jnp.arange(new_tiles, dtype=jnp.int32) ^ (peer * own_rows // TILE)
    new_kept = lax.dynamic_slice_in_dim(keep_flags, n * ctx_tiles + place * new_tiles, new_tiles, 1)
    kept = jnp.concatenate(
        [
            lax.dynamic_slice_in_dim(keep_flags, place * ctx_tiles, ctx_tiles, 1),
            jnp.sum(jnp.where(new_order[:, None] == jnp.arange(new_tiles), new_kept[:, None, :], 0), axis=2),
        ],
        axis=1,
    )
    kept = (kept == 1).astype(jnp.int32)
    count = len(PIECES)
    widths = [units * unit for _, units in PIECES]
    bits = [1 << k for k in range((n - 1).bit_length())]
    where = place.reshape(1)
    parts = [{d: [] for d in range(n)} for _ in range(count)]
    sent, backs = [None] * count, [None] * count

    def to_heads(pieces):
        moved = lax.all_to_all(pieces, "uly", split_axis=0, concat_axis=0, tiled=False)
        return moved.reshape(span_rows, pieces.shape[2])

    def to_peers(pieces):
        return [lax.ppermute(p, "uly", [(i, i ^ k) for i in range(peers)]) if k else p for k, p in enumerate(pieces)]

    def across(x, bit):
        return lax.ppermute(x, "blk", [(i, i ^ bit) for i in range(n)])

    def spread(span):
        found = {0: span}
        for bit in reversed(bits):
            for d in list(found):
                found[d ^ bit] = across(found[d], bit)
        return found

    early = widths[0]
    first_span = to_heads(jnp.stack([new_queries[:, p * group : p * group + early] for p in range(peers)]))
    found = [spread(first_span)]
    both = parts_for_peers(peer, [new_keys, new_values], 0, peers, [first_span])
    span_k, span_v_t = joined(to_peers(both), first_span)
    later = parts_for_peers(peer, [new_queries], early, peers, [both[0]])
    found += [spread(span) for span in regrouped(peer, to_peers(later), widths[1:], span_k)]
    context_values_t = context_values.T
    last = [span_k]

    def run_attend(c, distances):
        own = attend(
            where, kept, found[c], distances, context_keys, span_k, context_values_t, span_v_t,
            PIECES[c][0] // PIECES[c][1], last[0],
        )
        last[0] = own
        for slot, d in enumerate(distances):
            parts[c][d] = [(own, slot)]
        return own

    def run_sent(c):
        sent[c] = across(run_attend(c, list(range(1, n, 2))), 1)

    def run_kept(c):
        run_attend(c, list(range(0, n, 2)))
        for d in range(0, n, 2):
            parts[c][d].append((sent[c], d // 2))

    def run_merge(c):
        for bit in bits[1:]:
            for d in range(bit, n, 2 * bit):
                joint = join_parts(parts[c][d], widths[c], last[0], False)
                last[0] = joint
                parts[c][d ^ bit].append((across(joint, bit), 0))

    def run_finish(c):
        done = join_parts(parts[c][0], widths[c], last[0], True)
        last[0] = done
        done = done.reshape(peers, own_rows, widths[c])
        backs[c] = lax.all_to_all(done, "uly", split_axis=0, concat_axis=0, tiled=False)

    for c in range(count):
        run_sent(c)
        if c > 0:
            run_merge(c - 1)
        run_kept(c)
        if c > 0:
            run_finish(c - 1)
    run_merge(count - 1)
    run_finish(count - 1)

    in_order = [backs[c] for c in sorted(range(count), key=lambda c: PIECES[c][0])]
    together = jnp.concatenate(in_order, axis=2)
    return together.transpose(1, 0, 2).reshape(own_rows, peers * group)


def solution(mesh):
    in_specs = (
        P(("cfg", "blk", "uly"), None),
        P(("cfg", "blk", "uly"), None),
        P(("cfg", "blk", "uly"), None),
        P(("cfg", "blk"), "uly"),
        P(("cfg", "blk"), "uly"),
        P(),
    )
    out_specs = P(("cfg", "blk", "uly"), None)
    return jax.shard_map(shards, mesh=mesh, in_specs=in_specs, out_specs=out_specs, check_vma=False)
```

```python
import functools

import jax
import jax.numpy as jnp
from jax import lax
from jax.experimental import pallas as pl
from jax.experimental.pallas import tpu as pltpu
from jax.sharding import PartitionSpec as P

DH = 128
TILE = 128
PIECES = ((0, 1), (1, 1), (2, 1))
PIECE_UNITS = 3
HALF = 256
CHUNK = 256
LOG2E = 1.4426950408889634
TINY = 1.0e-30
ONES = 16
SCALE2 = DH ** (-0.5) * LOG2E
MASKED = -1.0e30
MIB = 1024 * 1024
QUICK = pl.CostEstimate(flops=1024, bytes_accessed=1024, transcendentals=0)


def split3(x):
    hi = x.astype(jnp.bfloat16).astype(jnp.float32)
    rest = x - hi
    mid = rest.astype(jnp.bfloat16).astype(jnp.float32)
    lo = (rest - mid).astype(jnp.bfloat16).astype(jnp.float32)
    return hi, mid, lo


def stat_rows(width):
    return -(-3 * (width // DH) // 16) * 16


def attend_kernel(distances, place_ref, kept_ref, *refs):
    count = len(distances)
    q_refs = refs[:count]
    ck_ref, nk_ref, cv_ref, nv_ref = refs[count : count + 4]
    out_ref, q_s, s0, s1, m0, m1, stat_s = refs[-7:]
    rows = q_s.shape[0]
    width = q_s.shape[1] // 2
    heads = width // DH
    ctx, new = ck_ref.shape[0], nk_ref.shape[0]
    subs = HALF // TILE
    halves = rows // HALF
    slots = ((s0, m0), (s1, m1))
    nt = (((1,), (1,)), ((), ()))
    distance = distances[0]
    for i in range(1, count):
        distance = jnp.where(pl.program_id(0) == i, distances[i], distance)
    first_tile = (place_ref[0] ^ distance) * (rows // TILE)
    stat_s[...] = jnp.zeros_like(stat_s)
    for i, q_ref in enumerate(q_refs):

        @pl.when(pl.program_id(0) == i)
        def _():
            for head in range(heads):
                scaled = q_ref[:, head * DH : (head + 1) * DH].astype(jnp.float32) * SCALE2
                hi = scaled.astype(jnp.bfloat16)
                q_s[:, 2 * head * DH : (2 * head + 1) * DH] = hi
                q_s[:, (2 * head + 1) * DH : (2 * head + 2) * DH] = (scaled - hi.astype(jnp.float32)).astype(jnp.bfloat16)

    def columns(head, size=DH):
        return pl.ds(pl.multiple_of(head * size, size), size)

    chunks = [(k, v, at, base) for k, v, size, base in ((ck_ref, cv_ref, ctx, 0), (nk_ref, nv_ref, new, ctx))
              for at in range(0, size, CHUNK)]

    def kept(half, sub, row):
        return kept_ref[first_tile + half * subs + sub, row // TILE] > 0

    def score(head, half, chunk, q, tops):
        s_ref = slots[half % 2][0]
        k_ref, _, at, base = chunk
        size = min(CHUNK, k_ref.shape[0] - at)
        k = k_ref[at : at + size, columns(head)]
        scores = lax.dot_general(jnp.concatenate([k, k], axis=1), q, nt, preferred_element_type=jnp.float32)
        s_ref[base + at : base + at + size, :] = scores
        for j in range(0, size, TILE):
            for sub in range(subs):
                piece = scores[j : j + TILE, sub * TILE : (sub + 1) * TILE]
                top = jnp.max(piece.reshape(TILE // 8, 8, TILE), axis=0)
                top = jnp.where(kept(half, sub, base + at + j), top, MASKED)
                tops[sub] = top if tops[sub] is None else jnp.maximum(tops[sub], top)

    def weigh(head, half, chunk, high):
        s_ref = slots[half % 2][0]
        _, v_ref, at, base = chunk
        size = min(CHUNK, v_ref.shape[1] - at)
        lows = []
        for j in range(0, size, TILE):
            row = base + at + j
            pieces = []
            for sub in range(subs):
                lanes = slice(sub * TILE, (sub + 1) * TILE)
                less = jnp.where(kept(half, sub, row), high[:, lanes], -MASKED)
                pieces.append(jnp.exp2(s_ref[row : row + TILE, lanes] - less).astype(jnp.bfloat16))
            lows.append(jnp.concatenate(pieces, axis=1))
        low = jnp.concatenate(lows, axis=0)
        values = jnp.concatenate([v_ref[columns(head), at : at + size], jnp.ones((ONES, size), jnp.bfloat16)], axis=0)
        return jnp.dot(values, low, preferred_element_type=jnp.float32)

    def step(head, half, next_head, next_half, both=True):
        q = q_s[next_half * HALF : (next_half + 1) * HALF, columns(next_head, 2 * DH)]
        tops = [None] * subs
        if both:
            high = jnp.max(slots[half % 2][1][...], axis=0, keepdims=True)
            acc = None
        for chunk in chunks:
            score(next_head, next_half, chunk, q, tops)
            if both:
                found = weigh(head, half, chunk, high)
                acc = found if acc is None else acc + found
        for sub in range(subs):
            slots[next_half % 2][1][:, sub * TILE : (sub + 1) * TILE] = tops[sub]
        if both:
            total = jnp.maximum(acc[DH : DH + 1, :], TINY)
            lanes = slice(half * HALF, (half + 1) * HALF)
            out_ref[0, columns(head), lanes] = (acc[:DH, :] * (1.0 / total)).astype(jnp.bfloat16)
            for part, value in enumerate(split3(high + jnp.log2(total))):
                stat_s[pl.ds(3 * head + part, 1), lanes] = value

    step(0, 1, 0, 0, both=False)

    @pl.loop(0, heads)
    def _(head):
        for half in range(halves):
            if half + 1 < halves:
                step(head, half, head, half + 1)
            else:
                step(head, half, jnp.minimum(head + 1, heads - 1), 0)

    out_ref[0, width:, :] = stat_s[...].astype(jnp.bfloat16)


def attend(place, kept, queries, distances, ctx_k, new_k, ctx_v, new_v, piece, dep):
    rows, width = queries[distances[0]].shape
    ctx, new = ctx_k.shape[0], new_k.shape[0]
    heads = width // DH
    keys = ctx + new
    blocks = len(distances)
    across = lambda i, t, b: (0, piece)
    down = lambda i, t, b: (piece, 0)
    prow = width + stat_rows(width)
    return pl.pallas_call(
        functools.partial(attend_kernel, distances),
        out_shape=jax.ShapeDtypeStruct((blocks, prow, rows), jnp.bfloat16),
        grid_spec=pltpu.PrefetchScalarGridSpec(
            num_scalar_prefetch=2,
            grid=(blocks,),
            in_specs=[pl.BlockSpec((rows, width), lambda i, t, b: (0, 0))] * blocks
            + [
                pl.BlockSpec((ctx, width), across),
                pl.BlockSpec((new, width), across),
                pl.BlockSpec((width, ctx), down),
                pl.BlockSpec((width, new), down),
                pl.BlockSpec(memory_space=pl.ANY),
            ],
            out_specs=pl.BlockSpec((1, prow, rows), lambda i, t, b: (i, 0, 0)),
            scratch_shapes=[
                pltpu.VMEM((rows, 2 * width), jnp.bfloat16),
                pltpu.VMEM((keys, HALF), jnp.float32),
                pltpu.VMEM((keys, HALF), jnp.float32),
                pltpu.VMEM((8, HALF), jnp.float32),
                pltpu.VMEM((8, HALF), jnp.float32),
                pltpu.VMEM((stat_rows(width), rows), jnp.float32),
            ],
        ),
        compiler_params=pltpu.CompilerParams(vmem_limit_bytes=28 * MIB),
        cost_estimate=pl.CostEstimate(
            flops=8 * blocks * rows * keys * DH * heads,
            bytes_accessed=4 * blocks * rows * width + 4 * keys * width,
            transcendentals=blocks * rows * keys * heads,
        ),
        name="attend",
    )(place, kept, *[queries[d] for d in distances], ctx_k, new_k, ctx_v, new_v, dep)


def combine(refs, width, emit):
    stats = []
    for ref in refs:
        terms = ref[0, width:, :].astype(jnp.float32)
        stats.append([terms[3 * h : 3 * h + 1] + terms[3 * h + 1 : 3 * h + 2] + terms[3 * h + 2 : 3 * h + 3]
                      for h in range(width // DH)])
    for head in range(width // DH):
        logs = [s[head] for s in stats]
        top = functools.reduce(jnp.maximum, logs)
        weights = [jnp.exp2(l - top) for l in logs]
        total = functools.reduce(jnp.add, weights)
        value = None
        for ref, weight in zip(refs, weights):
            part = ref[0, head * DH : (head + 1) * DH, :].astype(jnp.float32) * (weight / total)
            value = part if value is None else value + part
        emit(head, value, top + jnp.log2(total))


def merge_kernel(*refs):
    sources, (out_ref, stat_ref) = refs[:-3], refs[-2:]
    width = out_ref.shape[1] - stat_ref.shape[0]
    stat_ref[...] = jnp.zeros_like(stat_ref)

    def emit(head, value, log):
        out_ref[0, head * DH : (head + 1) * DH, :] = value.astype(jnp.bfloat16)
        for part, term in enumerate(split3(log)):
            stat_ref[3 * head + part : 3 * head + part + 1, :] = term

    combine(sources, width, emit)
    out_ref[0, width:, :] = stat_ref[...].astype(jnp.bfloat16)


def finish_kernel(*refs):
    sources, out_ref = refs[:-2], refs[-1]

    def emit(head, value, log):
        out_ref[:, head * DH : (head + 1) * DH] = jnp.transpose(value).astype(jnp.bfloat16)

    combine(sources, out_ref.shape[1], emit)


def join_parts(parts, width, dep, final):
    _, prow, rows = parts[0][0].shape
    specs = [pl.BlockSpec((1, prow, rows), functools.partial(lambda slot, i: (slot, 0, 0), slot)) for _, slot in parts]
    shape = (rows, width) if final else (1, prow, rows)
    return pl.pallas_call(
        finish_kernel if final else merge_kernel,
        out_shape=jax.ShapeDtypeStruct(shape, jnp.bfloat16),
        grid=(1,),
        in_specs=specs + [pl.BlockSpec(memory_space=pl.ANY)],
        out_specs=pl.BlockSpec(shape, lambda i: (0,) * len(shape)),
        scratch_shapes=[] if final else [pltpu.VMEM((prow - width, rows), jnp.float32)],
        compiler_params=pltpu.CompilerParams(vmem_limit_bytes=16 * MIB),
        cost_estimate=QUICK,
        name="finish" if final else "merge",
    )(*[array for array, _ in parts], dep)


def part_kernel(peers, count, start, peer_ref, *refs):
    rows = refs[0].shape[0]
    outs = refs[-peers:]
    for i, ref in enumerate(refs[: count * peers]):
        outs[i % peers][i // peers * rows : (i // peers + 1) * rows, :] = ref[:, start:]


def parts_for_peers(peer, arrays, start, peers, deps):
    rows, group = arrays[0].shape[0], arrays[0].shape[1] // peers
    specs = [pl.BlockSpec((rows, group), functools.partial(lambda k, i, t: (0, t[0] ^ k), k)) for k in range(peers)]
    shape = (len(arrays) * rows, group - start)
    return pl.pallas_call(
        functools.partial(part_kernel, peers, len(arrays), start),
        out_shape=[jax.ShapeDtypeStruct(shape, jnp.bfloat16)] * peers,
        grid_spec=pltpu.PrefetchScalarGridSpec(
            num_scalar_prefetch=1,
            grid=(1,),
            in_specs=specs * len(arrays) + [pl.BlockSpec(memory_space=pl.ANY)] * len(deps),
            out_specs=[pl.BlockSpec(shape, lambda i, t: (0, 0))] * peers,
        ),
        compiler_params=pltpu.CompilerParams(vmem_limit_bytes=28 * MIB),
        cost_estimate=QUICK,
        name="parts",
    )(peer.reshape(1), *[a for a in arrays for _ in range(peers)], *deps)


def regroup_kernel(peers, start, peer_ref, *refs):
    out_ref = refs[-1]
    rows, width = refs[0].shape[0], out_ref.shape[1]
    for k in range(peers):
        here = pl.ds(pl.multiple_of((peer_ref[0] ^ k) * rows, rows), rows)
        out_ref[here, :] = refs[k][:, start : start + width]


def regrouped(peer, pieces, start, width, deps):
    peers, rows = len(pieces), pieces[0].shape[0]
    whole = lambda i, t: (0, 0)
    shape = (peers * rows, width)
    return pl.pallas_call(
        functools.partial(regroup_kernel, peers, start),
        out_shape=jax.ShapeDtypeStruct(shape, jnp.bfloat16),
        grid_spec=pltpu.PrefetchScalarGridSpec(
            num_scalar_prefetch=1,
            grid=(1,),
            in_specs=[pl.BlockSpec(p.shape, whole) for p in pieces] + [pl.BlockSpec(memory_space=pl.ANY)] * len(deps),
            out_specs=pl.BlockSpec(shape, whole),
        ),
        compiler_params=pltpu.CompilerParams(vmem_limit_bytes=16 * MIB),
        cost_estimate=QUICK,
        name="regroup",
    )(peer.reshape(1), *pieces, *deps)


def join_kernel(*refs):
    pieces, (k_ref, v_ref, v_s) = refs[:-4], refs[-3:]
    rows = pieces[0].shape[0] // 2
    for i, piece in enumerate(pieces):
        k_ref[i * rows : (i + 1) * rows, :] = piece[:rows, :]
        v_s[i * rows : (i + 1) * rows, :] = piece[rows:, :]
    for at in range(0, v_s.shape[0], TILE):
        v_ref[:, at : at + TILE] = jnp.transpose(v_s[at : at + TILE, :])


def joined(pieces, dep):
    rows, group = pieces[0].shape[0] // 2 * len(pieces), pieces[0].shape[1]
    return pl.pallas_call(
        join_kernel,
        out_shape=[
            jax.ShapeDtypeStruct((rows, group), jnp.bfloat16),
            jax.ShapeDtypeStruct((group, rows), jnp.bfloat16),
        ],
        in_specs=[pl.BlockSpec(memory_space=pltpu.VMEM)] * len(pieces) + [pl.BlockSpec(memory_space=pl.ANY)],
        scratch_shapes=[pltpu.VMEM((rows, group), jnp.bfloat16)],
        compiler_params=pltpu.CompilerParams(vmem_limit_bytes=24 * MIB),
        cost_estimate=QUICK,
        name="join",
    )(*pieces, dep)


def shards(new_queries, new_keys, new_values, context_keys, context_values, keep_flags):
    n = lax.axis_size("blk")
    place = lax.axis_index("blk").astype(jnp.int32)
    peers = lax.axis_size("uly")
    own_rows = new_queries.shape[0]
    group = context_keys.shape[1]
    unit = group // PIECE_UNITS
    span_rows = own_rows * peers
    ctx_tiles, new_tiles = context_keys.shape[0] // TILE, span_rows // TILE

    peer = lax.axis_index("uly").astype(jnp.int32)
    new_order = jnp.arange(new_tiles, dtype=jnp.int32) ^ (peer * own_rows // TILE)
    new_kept = lax.dynamic_slice_in_dim(keep_flags, n * ctx_tiles + place * new_tiles, new_tiles, 1)
    kept = jnp.concatenate(
        [
            lax.dynamic_slice_in_dim(keep_flags, place * ctx_tiles, ctx_tiles, 1),
            jnp.sum(jnp.where(new_order[:, None] == jnp.arange(new_tiles), new_kept[:, None, :], 0), axis=2),
        ],
        axis=1,
    )
    kept = (kept == 1).astype(jnp.int32)
    count = len(PIECES)
    widths = [units * unit for _, units in PIECES]
    bits = [1 << k for k in range((n - 1).bit_length())]
    where = place.reshape(1)
    parts = [{d: [] for d in range(n)} for _ in range(count)]
    sent, backs = [None] * count, [None] * count

    def to_heads(pieces):
        moved = lax.all_to_all(pieces, "uly", split_axis=0, concat_axis=0, tiled=False)
        return moved.reshape(span_rows, pieces.shape[2])

    def to_peers(pieces):
        return [lax.ppermute(p, "uly", [(i, i ^ k) for i in range(peers)]) if k else p for k, p in enumerate(pieces)]

    def across(x, bit):
        return lax.ppermute(x, "blk", [(i, i ^ bit) for i in range(n)])

    def spread(span):
        found = {0: span}
        for bit in reversed(bits):
            for d in list(found):
                found[d ^ bit] = across(found[d], bit)
        return found

    early = widths[0]
    first_span = to_heads(jnp.stack([new_queries[:, p * group : p * group + early] for p in range(peers)]))
    found = [spread(first_span)]
    parts_q = parts_for_peers(peer, [new_queries], early, peers, [first_span])
    later = to_peers(parts_q)
    parts_kv = parts_for_peers(peer, [new_keys, new_values], 0, peers, [*later, found[0][n // 2]])

    def run_spread(c, deps):
        span = regrouped(peer, later, PIECES[c][0] * unit - early, widths[c], deps)
        found.append(spread(span))
        return span

    for c in range(1, count):
        latest = run_spread(c, [found[c - 1][n // 2]])
    span_k, span_v_t = joined(to_peers(parts_kv), latest)
    context_values_t = context_values.T
    last = [span_k]

    def run_attend(c, distances):
        own = attend(
            where, kept, found[c], distances, context_keys, span_k, context_values_t, span_v_t,
            PIECES[c][0] // PIECES[c][1], last[0],
        )
        last[0] = own
        for slot, d in enumerate(distances):
            parts[c][d] = [(own, slot)]
        return own

    def run_sent(c):
        sent[c] = across(run_attend(c, list(range(1, n, 2))), 1)

    def run_kept(c):
        run_attend(c, list(range(0, n, 2)))
        for d in range(0, n, 2):
            parts[c][d].append((sent[c], d // 2))

    def run_merge(c):
        for bit in bits[1:]:
            for d in range(bit, n, 2 * bit):
                joint = join_parts(parts[c][d], widths[c], last[0], False)
                last[0] = joint
                parts[c][d ^ bit].append((across(joint, bit), 0))

    def run_finish(c):
        done = join_parts(parts[c][0], widths[c], last[0], True)
        last[0] = done
        done = done.reshape(peers, own_rows, widths[c])
        backs[c] = lax.all_to_all(done, "uly", split_axis=0, concat_axis=0, tiled=False)

    for c in range(count):
        run_sent(c)
        if c > 0:
            run_merge(c - 1)
        run_kept(c)
        if 0 < c < count - 1:
            run_finish(c - 1)
    run_merge(count - 1)
    run_finish(count - 2)
    run_finish(count - 1)

    in_order = [backs[c] for c in sorted(range(count), key=lambda c: PIECES[c][0])]
    together = jnp.concatenate(in_order, axis=2)
    return together.transpose(1, 0, 2).reshape(own_rows, peers * group)


def solution(mesh):
    in_specs = (
        P(("cfg", "blk", "uly"), None),
        P(("cfg", "blk", "uly"), None),
        P(("cfg", "blk", "uly"), None),
        P(("cfg", "blk"), "uly"),
        P(("cfg", "blk"), "uly"),
        P(),
    )
    out_specs = P(("cfg", "blk", "uly"), None)
    return jax.shard_map(shards, mesh=mesh, in_specs=in_specs, out_specs=out_specs, check_vma=False)
```

```python
import functools

import jax
import jax.numpy as jnp
from jax import lax
from jax.experimental import pallas as pl
from jax.experimental.pallas import tpu as pltpu
from jax.sharding import PartitionSpec as P

DH = 128
TILE = 128
PIECES = ((0, 1), (1, 1), (2, 1))
PIECE_UNITS = 3
HALF = 256
CHUNK = 256
LOG2E = 1.4426950408889634
TINY = 1.0e-30
ONES = 16
SCALE2 = DH ** (-0.5) * LOG2E
MASKED = -1.0e30
MIB = 1024 * 1024
QUICK = pl.CostEstimate(flops=1024, bytes_accessed=1024, transcendentals=0)


def split3(x):
    hi = x.astype(jnp.bfloat16).astype(jnp.float32)
    rest = x - hi
    mid = rest.astype(jnp.bfloat16).astype(jnp.float32)
    lo = (rest - mid).astype(jnp.bfloat16).astype(jnp.float32)
    return hi, mid, lo


def stat_rows(width):
    return -(-3 * (width // DH) // 16) * 16


def attend_kernel(choices, table_ref, kept_ref, *refs):
    count = sum(len(c) for c in choices)
    sources, at = [], 0
    for c in choices:
        sources.append(refs[at : at + len(c)])
        at += len(c)
    ck_ref, nk_ref, cv_ref, nv_ref = refs[count : count + 4]
    out_ref, q_s, s0, s1, m0, m1, stat_s = refs[-7:]
    rows = q_s.shape[0]
    width = q_s.shape[1] // 2
    heads = width // DH
    ctx, new = ck_ref.shape[0], nk_ref.shape[0]
    subs = HALF // TILE
    halves = rows // HALF
    slots = ((s0, m0), (s1, m1))
    nt = (((1,), (1,)), ((), ()))
    step_no = pl.program_id(0)
    first_tile = table_ref[1 + step_no] * (rows // TILE)
    stat_s[...] = jnp.zeros_like(stat_s)
    for c, q_refs in enumerate(sources):
        for i, q_ref in enumerate(q_refs):

            @pl.when((step_no == i) & (table_ref[0] == c))
            def _():
                for head in range(heads):
                    scaled = q_ref[:, head * DH : (head + 1) * DH].astype(jnp.float32) * SCALE2
                    hi = scaled.astype(jnp.bfloat16)
                    lo = (scaled - hi.astype(jnp.float32)).astype(jnp.bfloat16)
                    q_s[:, 2 * head * DH : (2 * head + 1) * DH] = hi
                    q_s[:, (2 * head + 1) * DH : (2 * head + 2) * DH] = lo

    def columns(head, size=DH):
        return pl.ds(pl.multiple_of(head * size, size), size)

    chunks = [(k, v, at, base) for k, v, size, base in ((ck_ref, cv_ref, ctx, 0), (nk_ref, nv_ref, new, ctx))
              for at in range(0, size, CHUNK)]

    def kept(half, sub, row):
        return kept_ref[first_tile + half * subs + sub, row // TILE] > 0

    def score(head, half, chunk, q, tops):
        s_ref = slots[half % 2][0]
        k_ref, _, at, base = chunk
        size = min(CHUNK, k_ref.shape[0] - at)
        k = k_ref[at : at + size, columns(head)]
        scores = lax.dot_general(jnp.concatenate([k, k], axis=1), q, nt, preferred_element_type=jnp.float32)
        s_ref[base + at : base + at + size, :] = scores
        for j in range(0, size, TILE):
            for sub in range(subs):
                piece = scores[j : j + TILE, sub * TILE : (sub + 1) * TILE]
                top = jnp.max(piece.reshape(TILE // 8, 8, TILE), axis=0)
                top = jnp.where(kept(half, sub, base + at + j), top, MASKED)
                tops[sub] = top if tops[sub] is None else jnp.maximum(tops[sub], top)

    def weigh(head, half, chunk, high):
        s_ref = slots[half % 2][0]
        _, v_ref, at, base = chunk
        size = min(CHUNK, v_ref.shape[1] - at)
        lows = []
        for j in range(0, size, TILE):
            row = base + at + j
            pieces = []
            for sub in range(subs):
                lanes = slice(sub * TILE, (sub + 1) * TILE)
                less = jnp.where(kept(half, sub, row), high[:, lanes], -MASKED)
                pieces.append(jnp.exp2(s_ref[row : row + TILE, lanes] - less).astype(jnp.bfloat16))
            lows.append(jnp.concatenate(pieces, axis=1))
        low = jnp.concatenate(lows, axis=0)
        values = jnp.concatenate([v_ref[columns(head), at : at + size], jnp.ones((ONES, size), jnp.bfloat16)], axis=0)
        return jnp.dot(values, low, preferred_element_type=jnp.float32)

    def step(head, half, next_head, next_half, both=True):
        q = q_s[next_half * HALF : (next_half + 1) * HALF, columns(next_head, 2 * DH)]
        tops = [None] * subs
        if both:
            high = jnp.max(slots[half % 2][1][...], axis=0, keepdims=True)
            acc = None
        for chunk in chunks:
            score(next_head, next_half, chunk, q, tops)
            if both:
                found = weigh(head, half, chunk, high)
                acc = found if acc is None else acc + found
        for sub in range(subs):
            slots[next_half % 2][1][:, sub * TILE : (sub + 1) * TILE] = tops[sub]
        if both:
            total = jnp.maximum(acc[DH : DH + 1, :], TINY)
            lanes = slice(half * HALF, (half + 1) * HALF)
            out_ref[0, columns(head), lanes] = (acc[:DH, :] * (1.0 / total)).astype(jnp.bfloat16)
            for part, value in enumerate(split3(high + jnp.log2(total))):
                stat_s[pl.ds(3 * head + part, 1), lanes] = value

    step(0, 1, 0, 0, both=False)

    @pl.loop(0, heads)
    def _(head):
        for half in range(halves):
            if half + 1 < halves:
                step(head, half, head, half + 1)
            else:
                step(head, half, jnp.minimum(head + 1, heads - 1), 0)

    out_ref[0, width:, :] = stat_s[...].astype(jnp.bfloat16)


def attend(table, kept, choices, ctx_k, new_k, ctx_v, new_v, piece, dep):
    queries = [q for choice in choices for q in choice]
    rows, width = queries[0].shape
    ctx, new = ctx_k.shape[0], new_k.shape[0]
    heads = width // DH
    keys = ctx + new
    blocks = len(choices[0])
    across = lambda i, t, b: (0, piece)
    down = lambda i, t, b: (piece, 0)
    prow = width + stat_rows(width)
    return pl.pallas_call(
        functools.partial(attend_kernel, [[None] * len(c) for c in choices]),
        out_shape=jax.ShapeDtypeStruct((blocks, prow, rows), jnp.bfloat16),
        grid_spec=pltpu.PrefetchScalarGridSpec(
            num_scalar_prefetch=2,
            grid=(blocks,),
            in_specs=[pl.BlockSpec((rows, width), lambda i, t, b: (0, 0))] * len(queries)
            + [
                pl.BlockSpec((ctx, width), across),
                pl.BlockSpec((new, width), across),
                pl.BlockSpec((width, ctx), down),
                pl.BlockSpec((width, new), down),
                pl.BlockSpec(memory_space=pl.ANY),
            ],
            out_specs=pl.BlockSpec((1, prow, rows), lambda i, t, b: (i, 0, 0)),
            scratch_shapes=[
                pltpu.VMEM((rows, 2 * width), jnp.bfloat16),
                pltpu.VMEM((keys, HALF), jnp.float32),
                pltpu.VMEM((keys, HALF), jnp.float32),
                pltpu.VMEM((8, HALF), jnp.float32),
                pltpu.VMEM((8, HALF), jnp.float32),
                pltpu.VMEM((stat_rows(width), rows), jnp.float32),
            ],
        ),
        compiler_params=pltpu.CompilerParams(vmem_limit_bytes=28 * MIB),
        cost_estimate=pl.CostEstimate(
            flops=8 * blocks * rows * keys * DH * heads,
            bytes_accessed=4 * blocks * rows * width + 4 * keys * width,
            transcendentals=blocks * rows * keys * heads,
        ),
        name="attend",
    )(table, kept, *queries, ctx_k, new_k, ctx_v, new_v, dep)


def combine(refs, width, emit):
    stats = []
    for ref in refs:
        terms = ref[0, width:, :].astype(jnp.float32)
        stats.append([terms[3 * h : 3 * h + 1] + terms[3 * h + 1 : 3 * h + 2] + terms[3 * h + 2 : 3 * h + 3]
                      for h in range(width // DH)])
    for head in range(width // DH):
        logs = [s[head] for s in stats]
        top = functools.reduce(jnp.maximum, logs)
        weights = [jnp.exp2(l - top) for l in logs]
        total = functools.reduce(jnp.add, weights)
        value = None
        for ref, weight in zip(refs, weights):
            part = ref[0, head * DH : (head + 1) * DH, :].astype(jnp.float32) * (weight / total)
            value = part if value is None else value + part
        emit(head, value, top + jnp.log2(total))


def join_kernel_of(sizes, final, table_ref, *refs):
    sources, at = [], 0
    for size in sizes:
        sources.append(refs[at : at + size])
        at += size
    if final:
        out_ref = refs[-1]
        width = out_ref.shape[1]
    else:
        out_ref, stat_ref = refs[-2:]
        width = out_ref.shape[1] - stat_ref.shape[0]

    def emit(head, value, log):
        at = slice(head * DH, (head + 1) * DH)
        if final:
            out_ref[:, at] = jnp.transpose(value).astype(jnp.bfloat16)
            return
        out_ref[0, at, :] = value.astype(jnp.bfloat16)
        for part, term in enumerate(split3(log)):
            stat_ref[3 * head + part : 3 * head + part + 1, :] = term

    for c, chosen in enumerate(sources):
        if chosen:

            @pl.when(table_ref[0] == c)
            def _():
                if not final:
                    stat_ref[...] = jnp.zeros_like(stat_ref)
                combine(chosen, width, emit)
                if not final:
                    out_ref[0, width:, :] = stat_ref[...].astype(jnp.bfloat16)


def join_parts(table, choices, width, dep, final, blocks=1):
    parts = [part for choice in choices for part in choice]
    _, prow, rows = parts[0][0].shape
    specs = [
        pl.BlockSpec((1, prow, rows), functools.partial(lambda slot, i, t: (slot + i, 0, 0), slot)) for _, slot in parts
    ]
    shape = (rows, width) if final else (blocks, prow, rows)
    out_spec = pl.BlockSpec(shape, lambda i, t: (0, 0)) if final else pl.BlockSpec((1, prow, rows), lambda i, t: (i, 0, 0))
    return pl.pallas_call(
        functools.partial(join_kernel_of, [len(c) for c in choices], final),
        out_shape=jax.ShapeDtypeStruct(shape, jnp.bfloat16),
        grid_spec=pltpu.PrefetchScalarGridSpec(
            num_scalar_prefetch=1,
            grid=(blocks,),
            in_specs=specs + [pl.BlockSpec(memory_space=pl.ANY)],
            out_specs=out_spec,
            scratch_shapes=[] if final else [pltpu.VMEM((prow - width, rows), jnp.float32)],
        ),
        compiler_params=pltpu.CompilerParams(vmem_limit_bytes=16 * MIB),
        cost_estimate=QUICK,
        name="finish" if final else "merge",
    )(table, *[array for array, _ in parts], dep)


def part_kernel(peers, count, start, peer_ref, *refs):
    rows = refs[0].shape[0]
    outs = refs[-peers:]
    for i, ref in enumerate(refs[: count * peers]):
        outs[i % peers][i // peers * rows : (i // peers + 1) * rows, :] = ref[:, start:]


def parts_for_peers(peer, arrays, start, peers, deps):
    rows, group = arrays[0].shape[0], arrays[0].shape[1] // peers
    specs = [pl.BlockSpec((rows, group), functools.partial(lambda k, i, t: (0, t[0] ^ k), k)) for k in range(peers)]
    shape = (len(arrays) * rows, group - start)
    return pl.pallas_call(
        functools.partial(part_kernel, peers, len(arrays), start),
        out_shape=[jax.ShapeDtypeStruct(shape, jnp.bfloat16)] * peers,
        grid_spec=pltpu.PrefetchScalarGridSpec(
            num_scalar_prefetch=1,
            grid=(1,),
            in_specs=specs * len(arrays) + [pl.BlockSpec(memory_space=pl.ANY)] * len(deps),
            out_specs=[pl.BlockSpec(shape, lambda i, t: (0, 0))] * peers,
        ),
        compiler_params=pltpu.CompilerParams(vmem_limit_bytes=28 * MIB),
        cost_estimate=QUICK,
        name="parts",
    )(peer.reshape(1), *[a for a in arrays for _ in range(peers)], *deps)


def regroup_kernel(peers, start, peer_ref, *refs):
    out_ref = refs[-1]
    rows, width = refs[0].shape[0], out_ref.shape[1]
    for k in range(peers):
        here = pl.ds(pl.multiple_of((peer_ref[0] ^ k) * rows, rows), rows)
        out_ref[here, :] = refs[k][:, start : start + width]


def regrouped(peer, pieces, start, width, deps):
    peers, rows = len(pieces), pieces[0].shape[0]
    whole = lambda i, t: (0, 0)
    shape = (peers * rows, width)
    return pl.pallas_call(
        functools.partial(regroup_kernel, peers, start),
        out_shape=jax.ShapeDtypeStruct(shape, jnp.bfloat16),
        grid_spec=pltpu.PrefetchScalarGridSpec(
            num_scalar_prefetch=1,
            grid=(1,),
            in_specs=[pl.BlockSpec(p.shape, whole) for p in pieces] + [pl.BlockSpec(memory_space=pl.ANY)] * len(deps),
            out_specs=pl.BlockSpec(shape, whole),
        ),
        compiler_params=pltpu.CompilerParams(vmem_limit_bytes=16 * MIB),
        cost_estimate=QUICK,
        name="regroup",
    )(peer.reshape(1), *pieces, *deps)


def join_kernel(*refs):
    pieces, (k_ref, v_ref, v_s) = refs[:-4], refs[-3:]
    rows = pieces[0].shape[0] // 2
    for i, piece in enumerate(pieces):
        k_ref[i * rows : (i + 1) * rows, :] = piece[:rows, :]
        v_s[i * rows : (i + 1) * rows, :] = piece[rows:, :]
    for at in range(0, v_s.shape[0], TILE):
        v_ref[:, at : at + TILE] = jnp.transpose(v_s[at : at + TILE, :])


def joined(pieces, dep):
    rows, group = pieces[0].shape[0] // 2 * len(pieces), pieces[0].shape[1]
    return pl.pallas_call(
        join_kernel,
        out_shape=[
            jax.ShapeDtypeStruct((rows, group), jnp.bfloat16),
            jax.ShapeDtypeStruct((group, rows), jnp.bfloat16),
        ],
        in_specs=[pl.BlockSpec(memory_space=pltpu.VMEM)] * len(pieces) + [pl.BlockSpec(memory_space=pl.ANY)],
        scratch_shapes=[pltpu.VMEM((rows, group), jnp.bfloat16)],
        compiler_params=pltpu.CompilerParams(vmem_limit_bytes=24 * MIB),
        cost_estimate=QUICK,
        name="join",
    )(*pieces, dep)


def shards(new_queries, new_keys, new_values, context_keys, context_values, keep_flags):
    n = lax.axis_size("blk")
    place = lax.axis_index("blk").astype(jnp.int32)
    peers = lax.axis_size("uly")
    own_rows = new_queries.shape[0]
    group = context_keys.shape[1]
    unit = group // PIECE_UNITS
    span_rows = own_rows * peers
    ctx_tiles, new_tiles = context_keys.shape[0] // TILE, span_rows // TILE

    peer = lax.axis_index("uly").astype(jnp.int32)
    new_order = jnp.arange(new_tiles, dtype=jnp.int32) ^ (peer * own_rows // TILE)
    new_kept = lax.dynamic_slice_in_dim(keep_flags, n * ctx_tiles + place * new_tiles, new_tiles, 1)
    kept = jnp.concatenate(
        [
            lax.dynamic_slice_in_dim(keep_flags, place * ctx_tiles, ctx_tiles, 1),
            jnp.sum(jnp.where(new_order[:, None] == jnp.arange(new_tiles), new_kept[:, None, :], 0), axis=2),
        ],
        axis=1,
    )
    kept = (kept == 1).astype(jnp.int32)
    count = len(PIECES)
    widths = [units * unit for _, units in PIECES]
    backs = [None] * count

    def to_heads(pieces):
        moved = lax.all_to_all(pieces, "uly", split_axis=0, concat_axis=0, tiled=False)
        return moved.reshape(span_rows, pieces.shape[2])

    def to_peers(pieces):
        return [lax.ppermute(p, "uly", [(i, i ^ k) for i in range(peers)]) if k else p for k, p in enumerate(pieces)]

    def send(x, *pairs):
        return lax.ppermute(x, "blk", pairs)

    def spread_line(span):
        near = send(span, (0, 1), (1, 0), (2, 3), (3, 2))
        third = send(span, (1, 2), (2, 1))
        far = send(near, (1, 2), (2, 1))
        third_out = send(third, (1, 0), (2, 3))
        far_out = send(far, (1, 0), (2, 3))
        return dict(own=span, near=near, sent=[[far, third], [far_out, third_out]], early=third, mid=third_out)

    def spread_cube(span):
        found = {0: span}
        for bit in reversed(bits):
            for d in list(found):
                found[d ^ bit] = send(found[d], *[(i, i ^ bit) for i in range(n)])
        return dict(found=found, early=found[n // 2], mid=found[n // 2])

    bits = [1 << k for k in range((n - 1).bit_length())]
    line = n == 4
    spread = spread_line if line else spread_cube
    early = widths[0]
    first_span = to_heads(jnp.stack([new_queries[:, p * group : p * group + early] for p in range(peers)]))
    found = [spread(first_span)]
    parts_q = parts_for_peers(peer, [new_queries], early, peers, [first_span])
    later = to_peers(parts_q)
    parts_kv = parts_for_peers(peer, [new_keys, new_values], 0, peers, [*later, found[0]["early"]])

    def run_spread(c, deps):
        span = regrouped(peer, later, PIECES[c][0] * unit - early, widths[c], deps)
        found.append(spread(span))
        return span

    latest = parts_kv[0]
    for c in range(1, count):
        latest = run_spread(c, [found[c - 1]["early"], latest])
    span_k, span_v_t = joined(to_peers(parts_kv), latest)
    context_values_t = context_values.T
    last = [span_k]
    outer = ((place == 0) | (place == n - 1)).astype(jnp.int32)
    low = place < n // 2

    def run_attend(c, choices, targets):
        table = jnp.stack([outer, *targets]).astype(jnp.int32)
        own = attend(
            table, kept, choices, context_keys, span_k, context_values_t, span_v_t, PIECES[c][0] // PIECES[c][1], last[0]
        )
        last[0] = own
        return own

    def run_join(c, choices, final=False, blocks=1):
        last[0] = join_parts(outer.reshape(1), choices, widths[c], last[0], final, blocks)
        return last[0]

    def run_back(c, choices):
        done = run_join(c, choices, True).reshape(peers, own_rows, widths[c])
        backs[c] = lax.all_to_all(done, "uly", split_axis=0, concat_axis=0, tiled=False)

    state = [dict() for _ in range(count)]

    def run_sent(c):
        mine = run_attend(c, found[c]["sent"], [jnp.where(low, 3, 0), jnp.where(low, 2, 1)])
        state[c].update(far=mine, edge=send(mine, (0, 1), (3, 2)))

    def run_kept(c):
        blocks = [found[c]["near"], found[c]["own"]]
        mine = run_attend(c, [blocks, blocks], [place ^ 1, place])
        state[c].update(kept=mine, edge_near=send(mine[:1], (0, 1), (3, 2)))

    def run_cross(c):
        joint = run_join(c, [[(state[c]["far"], 0), (state[c]["edge"], 0)], []], blocks=2)
        state[c]["cross"] = send(joint, (1, 2), (2, 1))

    def run_outward(c):
        joint = run_join(c, [[(state[c]["kept"], 0), (state[c]["cross"], 0)], []])
        state[c]["outward"] = send(joint, (1, 0), (2, 3))

    def run_finish(c):
        inner = [(state[c]["kept"], 1), (state[c]["edge_near"], 0), (state[c]["cross"], 1)]
        run_back(c, [inner, [(state[c]["kept"], 1), (state[c]["outward"], 0)]])

    if line:
        run_sent(0)
        run_kept(0)
        run_sent(1)
        run_cross(0)
        run_kept(1)
        run_sent(2)
        run_outward(0)
        run_cross(1)
        run_kept(2)
        run_cross(2)
        run_finish(0)
        run_outward(1)
        run_outward(2)
        run_finish(1)
        run_finish(2)
    else:
        for c in range(count):
            parts = {d: [] for d in range(n)}
            for distances in (range(1, n, 2), range(0, n, 2)):
                blocks = [found[c]["found"][d] for d in distances]
                mine = run_attend(c, [blocks, blocks], [place ^ d for d in distances])
                for slot, d in enumerate(distances):
                    parts[d].append((mine, slot))
                if 1 in distances:
                    moved = send(mine, *[(i, i ^ 1) for i in range(n)])
            for slot, d in enumerate(range(0, n, 2)):
                parts[d].append((moved, slot))
            for bit in bits[1:]:
                for d in range(bit, n, 2 * bit):
                    joint = run_join(c, [parts[d], parts[d]])
                    parts[d ^ bit].append((send(joint, *[(i, i ^ bit) for i in range(n)]), 0))
            run_back(c, [parts[0], parts[0]])

    in_order = [backs[c] for c in sorted(range(count), key=lambda c: PIECES[c][0])]
    together = jnp.concatenate(in_order, axis=2)
    return together.transpose(1, 0, 2).reshape(own_rows, peers * group)


def solution(mesh):
    in_specs = (
        P(("cfg", "blk", "uly"), None),
        P(("cfg", "blk", "uly"), None),
        P(("cfg", "blk", "uly"), None),
        P(("cfg", "blk"), "uly"),
        P(("cfg", "blk"), "uly"),
        P(),
    )
    out_specs = P(("cfg", "blk", "uly"), None)
    return jax.shard_map(shards, mesh=mesh, in_specs=in_specs, out_specs=out_specs, check_vma=False)
```

```python
import functools

import jax
import jax.numpy as jnp
from jax import lax
from jax.experimental import pallas as pl
from jax.experimental.pallas import tpu as pltpu
from jax.sharding import PartitionSpec as P

DH = 128
TILE = 128
PIECES = ((0, 1), (1, 1), (2, 1))
PIECE_UNITS = 3
HALF = 256
CHUNK = 256
LOG2E = 1.4426950408889634
TINY = 1.0e-30
ONES = 16
SCALE2 = DH ** (-0.5) * LOG2E
MASKED = -1.0e30
MIB = 1024 * 1024
QUICK = pl.CostEstimate(flops=1024, bytes_accessed=1024, transcendentals=0)


def split3(x):
    hi = x.astype(jnp.bfloat16).astype(jnp.float32)
    rest = x - hi
    mid = rest.astype(jnp.bfloat16).astype(jnp.float32)
    lo = (rest - mid).astype(jnp.bfloat16).astype(jnp.float32)
    return hi, mid, lo


def stat_rows(width):
    return -(-3 * (width // DH) // 16) * 16


def attend_kernel(choices, table_ref, kept_ref, *refs):
    count = sum(len(c) for c in choices)
    sources, at = [], 0
    for c in choices:
        sources.append(refs[at : at + len(c)])
        at += len(c)
    ck_ref, nk_ref, cv_ref, nv_ref = refs[count : count + 4]
    out_ref, q_s, s0, s1, m0, m1, stat_s = refs[-7:]
    rows = q_s.shape[0]
    width = q_s.shape[1] // 2
    heads = width // DH
    ctx, new = ck_ref.shape[0], nk_ref.shape[0]
    subs = HALF // TILE
    halves = rows // HALF
    slots = ((s0, m0), (s1, m1))
    nt = (((1,), (1,)), ((), ()))
    step_no = pl.program_id(0)
    first_tile = table_ref[1 + step_no] * (rows // TILE)
    stat_s[...] = jnp.zeros_like(stat_s)
    for c, q_refs in enumerate(sources):
        for i, q_ref in enumerate(q_refs):

            @pl.when((step_no == i) & (table_ref[0] == c))
            def _():
                for head in range(heads):
                    scaled = q_ref[:, head * DH : (head + 1) * DH].astype(jnp.float32) * SCALE2
                    hi = scaled.astype(jnp.bfloat16)
                    lo = (scaled - hi.astype(jnp.float32)).astype(jnp.bfloat16)
                    q_s[:, 2 * head * DH : (2 * head + 1) * DH] = hi
                    q_s[:, (2 * head + 1) * DH : (2 * head + 2) * DH] = lo

    def columns(head, size=DH):
        return pl.ds(pl.multiple_of(head * size, size), size)

    chunks = [(k, v, at, base) for k, v, size, base in ((ck_ref, cv_ref, ctx, 0), (nk_ref, nv_ref, new, ctx))
              for at in range(0, size, CHUNK)]

    def kept(half, sub, row):
        return kept_ref[first_tile + half * subs + sub, row // TILE] > 0

    def score(head, half, chunk, q, tops):
        s_ref = slots[half % 2][0]
        k_ref, _, at, base = chunk
        size = min(CHUNK, k_ref.shape[0] - at)
        k = k_ref[at : at + size, columns(head)]
        scores = lax.dot_general(jnp.concatenate([k, k], axis=1), q, nt, preferred_element_type=jnp.float32)
        s_ref[base + at : base + at + size, :] = scores
        for j in range(0, size, TILE):
            for sub in range(subs):
                piece = scores[j : j + TILE, sub * TILE : (sub + 1) * TILE]
                top = jnp.max(piece.reshape(TILE // 8, 8, TILE), axis=0)
                top = jnp.where(kept(half, sub, base + at + j), top, MASKED)
                tops[sub] = top if tops[sub] is None else jnp.maximum(tops[sub], top)

    def weigh(head, half, chunk, high):
        s_ref = slots[half % 2][0]
        _, v_ref, at, base = chunk
        size = min(CHUNK, v_ref.shape[1] - at)
        lows = []
        for j in range(0, size, TILE):
            row = base + at + j
            pieces = []
            for sub in range(subs):
                lanes = slice(sub * TILE, (sub + 1) * TILE)
                less = jnp.where(kept(half, sub, row), high[:, lanes], -MASKED)
                pieces.append(jnp.exp2(s_ref[row : row + TILE, lanes] - less).astype(jnp.bfloat16))
            lows.append(jnp.concatenate(pieces, axis=1))
        low = jnp.concatenate(lows, axis=0)
        values = jnp.concatenate([v_ref[columns(head), at : at + size], jnp.ones((ONES, size), jnp.bfloat16)], axis=0)
        return jnp.dot(values, low, preferred_element_type=jnp.float32)

    def step(head, half, next_head, next_half, both=True):
        q = q_s[next_half * HALF : (next_half + 1) * HALF, columns(next_head, 2 * DH)]
        tops = [None] * subs
        if both:
            high = jnp.max(slots[half % 2][1][...], axis=0, keepdims=True)
            acc = None
        for chunk in chunks:
            score(next_head, next_half, chunk, q, tops)
            if both:
                found = weigh(head, half, chunk, high)
                acc = found if acc is None else acc + found
        for sub in range(subs):
            slots[next_half % 2][1][:, sub * TILE : (sub + 1) * TILE] = tops[sub]
        if both:
            total = jnp.maximum(acc[DH : DH + 1, :], TINY)
            lanes = slice(half * HALF, (half + 1) * HALF)
            out_ref[0, columns(head), lanes] = (acc[:DH, :] * (1.0 / total)).astype(jnp.bfloat16)
            for part, value in enumerate(split3(high + jnp.log2(total))):
                stat_s[pl.ds(3 * head + part, 1), lanes] = value

    step(0, 1, 0, 0, both=False)

    @pl.loop(0, heads)
    def _(head):
        for half in range(halves):
            if half + 1 < halves:
                step(head, half, head, half + 1)
            else:
                step(head, half, jnp.minimum(head + 1, heads - 1), 0)

    out_ref[0, width:, :] = stat_s[...].astype(jnp.bfloat16)


def attend(table, kept, choices, ctx_k, new_k, ctx_v, new_v, piece, dep):
    queries = [q for choice in choices for q in choice]
    rows, width = queries[0].shape
    ctx, new = ctx_k.shape[0], new_k.shape[0]
    heads = width // DH
    keys = ctx + new
    blocks = len(choices[0])
    across = lambda i, t, b: (0, piece)
    down = lambda i, t, b: (piece, 0)
    prow = width + stat_rows(width)
    return pl.pallas_call(
        functools.partial(attend_kernel, [[None] * len(c) for c in choices]),
        out_shape=jax.ShapeDtypeStruct((blocks, prow, rows), jnp.bfloat16),
        grid_spec=pltpu.PrefetchScalarGridSpec(
            num_scalar_prefetch=2,
            grid=(blocks,),
            in_specs=[pl.BlockSpec((rows, width), lambda i, t, b: (0, 0))] * len(queries)
            + [
                pl.BlockSpec((ctx, width), across),
                pl.BlockSpec((new, width), across),
                pl.BlockSpec((width, ctx), down),
                pl.BlockSpec((width, new), down),
                pl.BlockSpec(memory_space=pl.ANY),
            ],
            out_specs=pl.BlockSpec((1, prow, rows), lambda i, t, b: (i, 0, 0)),
            scratch_shapes=[
                pltpu.VMEM((rows, 2 * width), jnp.bfloat16),
                pltpu.VMEM((keys, HALF), jnp.float32),
                pltpu.VMEM((keys, HALF), jnp.float32),
                pltpu.VMEM((8, HALF), jnp.float32),
                pltpu.VMEM((8, HALF), jnp.float32),
                pltpu.VMEM((stat_rows(width), rows), jnp.float32),
            ],
        ),
        compiler_params=pltpu.CompilerParams(vmem_limit_bytes=28 * MIB),
        cost_estimate=pl.CostEstimate(
            flops=8 * blocks * rows * keys * DH * heads,
            bytes_accessed=4 * blocks * rows * width + 4 * keys * width,
            transcendentals=blocks * rows * keys * heads,
        ),
        name="attend",
    )(table, kept, *queries, ctx_k, new_k, ctx_v, new_v, dep)


def combine(refs, width, emit):
    stats = []
    for ref in refs:
        terms = ref[0, width:, :].astype(jnp.float32)
        stats.append([terms[3 * h : 3 * h + 1] + terms[3 * h + 1 : 3 * h + 2] + terms[3 * h + 2 : 3 * h + 3]
                      for h in range(width // DH)])
    for head in range(width // DH):
        logs = [s[head] for s in stats]
        top = functools.reduce(jnp.maximum, logs)
        weights = [jnp.exp2(l - top) for l in logs]
        total = functools.reduce(jnp.add, weights)
        value = None
        for ref, weight in zip(refs, weights):
            part = ref[0, head * DH : (head + 1) * DH, :].astype(jnp.float32) * (weight / total)
            value = part if value is None else value + part
        emit(head, value, top + jnp.log2(total))


def join_kernel_of(sizes, final, table_ref, *refs):
    sources, at = [], 0
    for size in sizes:
        sources.append(refs[at : at + size])
        at += size
    if final:
        out_ref = refs[-1]
        width = out_ref.shape[1]
    else:
        out_ref, stat_ref = refs[-2:]
        width = out_ref.shape[1] - stat_ref.shape[0]

    def emit(head, value, log):
        at = slice(head * DH, (head + 1) * DH)
        if final:
            out_ref[:, at] = jnp.transpose(value).astype(jnp.bfloat16)
            return
        out_ref[0, at, :] = value.astype(jnp.bfloat16)
        for part, term in enumerate(split3(log)):
            stat_ref[3 * head + part : 3 * head + part + 1, :] = term

    for c, chosen in enumerate(sources):
        if chosen:

            @pl.when(table_ref[0] == c)
            def _():
                if not final:
                    stat_ref[...] = jnp.zeros_like(stat_ref)
                combine(chosen, width, emit)
                if not final:
                    out_ref[0, width:, :] = stat_ref[...].astype(jnp.bfloat16)


def join_parts(table, choices, width, dep, final, blocks=1):
    parts = [part for choice in choices for part in choice]
    _, prow, rows = parts[0][0].shape
    specs = [
        pl.BlockSpec((1, prow, rows), functools.partial(lambda slot, i, t: (slot + i, 0, 0), slot)) for _, slot in parts
    ]
    shape = (rows, width) if final else (blocks, prow, rows)
    out_spec = pl.BlockSpec(shape, lambda i, t: (0, 0)) if final else pl.BlockSpec((1, prow, rows), lambda i, t: (i, 0, 0))
    return pl.pallas_call(
        functools.partial(join_kernel_of, [len(c) for c in choices], final),
        out_shape=jax.ShapeDtypeStruct(shape, jnp.bfloat16),
        grid_spec=pltpu.PrefetchScalarGridSpec(
            num_scalar_prefetch=1,
            grid=(blocks,),
            in_specs=specs + [pl.BlockSpec(memory_space=pl.ANY)],
            out_specs=out_spec,
            scratch_shapes=[] if final else [pltpu.VMEM((prow - width, rows), jnp.float32)],
        ),
        compiler_params=pltpu.CompilerParams(vmem_limit_bytes=16 * MIB),
        cost_estimate=QUICK,
        name="finish" if final else "merge",
    )(table, *[array for array, _ in parts], dep)


def part_kernel(peers, starts, peer_ref, *refs):
    outs = refs[-peers:]
    at = 0
    for i, start in enumerate(starts):
        for k in range(peers):
            ref = refs[i * peers + k]
            outs[k][:, at : at + ref.shape[1] - start] = ref[:, start:]
        at += ref.shape[1] - start


def parts_for_peers(peer, arrays, starts, peers, dep):
    rows, group = arrays[0].shape[0], arrays[0].shape[1] // peers
    specs = [pl.BlockSpec((rows, group), functools.partial(lambda k, i, t: (0, t[0] ^ k), k)) for k in range(peers)]
    shape = (rows, len(arrays) * group - sum(starts))
    return pl.pallas_call(
        functools.partial(part_kernel, peers, starts),
        out_shape=[jax.ShapeDtypeStruct(shape, jnp.bfloat16)] * peers,
        grid_spec=pltpu.PrefetchScalarGridSpec(
            num_scalar_prefetch=1,
            grid=(1,),
            in_specs=specs * len(arrays) + [pl.BlockSpec(memory_space=pl.ANY)],
            out_specs=[pl.BlockSpec(shape, lambda i, t: (0, 0))] * peers,
        ),
        compiler_params=pltpu.CompilerParams(vmem_limit_bytes=28 * MIB),
        cost_estimate=QUICK,
        name="parts",
    )(peer.reshape(1), *[a for a in arrays for _ in range(peers)], dep)


def regroup_kernel(peers, start, peer_ref, *refs):
    out_ref = refs[-1]
    rows, width = refs[0].shape[0], out_ref.shape[1]
    for k in range(peers):
        here = pl.ds(pl.multiple_of((peer_ref[0] ^ k) * rows, rows), rows)
        out_ref[here, :] = refs[k][:, start : start + width]


def regrouped(peer, pieces, start, width, deps):
    peers, rows = len(pieces), pieces[0].shape[0]
    whole = lambda i, t: (0, 0)
    shape = (peers * rows, width)
    return pl.pallas_call(
        functools.partial(regroup_kernel, peers, start),
        out_shape=jax.ShapeDtypeStruct(shape, jnp.bfloat16),
        grid_spec=pltpu.PrefetchScalarGridSpec(
            num_scalar_prefetch=1,
            grid=(1,),
            in_specs=[pl.BlockSpec(p.shape, whole) for p in pieces] + [pl.BlockSpec(memory_space=pl.ANY)] * len(deps),
            out_specs=pl.BlockSpec(shape, whole),
        ),
        compiler_params=pltpu.CompilerParams(vmem_limit_bytes=16 * MIB),
        cost_estimate=QUICK,
        name="regroup",
    )(peer.reshape(1), *pieces, *deps)


def join_kernel(*refs):
    pieces, (k_ref, v_ref, v_s) = refs[:-4], refs[-3:]
    rows, group = pieces[0].shape[0], k_ref.shape[1]
    for i, piece in enumerate(pieces):
        k_ref[i * rows : (i + 1) * rows, :] = piece[:, :group]
        v_s[i * rows : (i + 1) * rows, :] = piece[:, group : 2 * group]
    for at in range(0, v_s.shape[0], TILE):
        v_ref[:, at : at + TILE] = jnp.transpose(v_s[at : at + TILE, :])


def joined(pieces, group, dep):
    rows = pieces[0].shape[0] * len(pieces)
    return pl.pallas_call(
        join_kernel,
        out_shape=[
            jax.ShapeDtypeStruct((rows, group), jnp.bfloat16),
            jax.ShapeDtypeStruct((group, rows), jnp.bfloat16),
        ],
        in_specs=[pl.BlockSpec(memory_space=pltpu.VMEM)] * len(pieces) + [pl.BlockSpec(memory_space=pl.ANY)],
        scratch_shapes=[pltpu.VMEM((rows, group), jnp.bfloat16)],
        compiler_params=pltpu.CompilerParams(vmem_limit_bytes=24 * MIB),
        cost_estimate=QUICK,
        name="join",
    )(*pieces, dep)


def shards(new_queries, new_keys, new_values, context_keys, context_values, keep_flags):
    n = lax.axis_size("blk")
    place = lax.axis_index("blk").astype(jnp.int32)
    peers = lax.axis_size("uly")
    own_rows = new_queries.shape[0]
    group = context_keys.shape[1]
    unit = group // PIECE_UNITS
    span_rows = own_rows * peers
    ctx_tiles, new_tiles = context_keys.shape[0] // TILE, span_rows // TILE

    peer = lax.axis_index("uly").astype(jnp.int32)
    new_order = jnp.arange(new_tiles, dtype=jnp.int32) ^ (peer * own_rows // TILE)
    new_kept = lax.dynamic_slice_in_dim(keep_flags, n * ctx_tiles + place * new_tiles, new_tiles, 1)
    kept = jnp.concatenate(
        [
            lax.dynamic_slice_in_dim(keep_flags, place * ctx_tiles, ctx_tiles, 1),
            jnp.sum(jnp.where(new_order[:, None] == jnp.arange(new_tiles), new_kept[:, None, :], 0), axis=2),
        ],
        axis=1,
    )
    kept = (kept == 1).astype(jnp.int32)
    count = len(PIECES)
    widths = [units * unit for _, units in PIECES]
    backs = [None] * count

    def to_heads(pieces):
        moved = lax.all_to_all(pieces, "uly", split_axis=0, concat_axis=0, tiled=False)
        return moved.reshape(span_rows, pieces.shape[2])

    def to_peers(pieces):
        return [lax.ppermute(p, "uly", [(i, i ^ k) for i in range(peers)]) if k else p for k, p in enumerate(pieces)]

    def send(x, *pairs):
        return lax.ppermute(x, "blk", pairs)

    def spread_line(span):
        near = send(span, (0, 1), (1, 0), (2, 3), (3, 2))
        third = send(span, (1, 2), (2, 1))
        far = send(near, (1, 2), (2, 1))
        third_out = send(third, (1, 0), (2, 3))
        far_out = send(far, (1, 0), (2, 3))
        return dict(own=span, near=near, sent=[[far, third], [far_out, third_out]], early=third, mid=third_out)

    def spread_cube(span):
        found = {0: span}
        for bit in reversed(bits):
            for d in list(found):
                found[d ^ bit] = send(found[d], *[(i, i ^ bit) for i in range(n)])
        return dict(found=found, early=found[n // 2], mid=found[n // 2])

    bits = [1 << k for k in range((n - 1).bit_length())]
    line = n == 4
    spread = spread_line if line else spread_cube
    early = widths[0]
    first_span = to_heads(jnp.stack([new_queries[:, p * group : p * group + early] for p in range(peers)]))
    found = [spread(first_span)]
    moved = to_peers(parts_for_peers(peer, [new_keys, new_values, new_queries], [0, 0, early], peers, first_span))

    def run_spread(c, deps):
        span = regrouped(peer, moved, 2 * group + PIECES[c][0] * unit - early, widths[c], deps)
        found.append(spread(span))
        return span

    span_k, span_v_t = joined(moved, group, run_spread(1, [first_span]))
    context_values_t = context_values.T
    last = [span_k]
    outer = ((place == 0) | (place == n - 1)).astype(jnp.int32)
    low = place < n // 2

    def run_attend(c, choices, targets):
        table = jnp.stack([outer, *targets]).astype(jnp.int32)
        own = attend(
            table, kept, choices, context_keys, span_k, context_values_t, span_v_t, PIECES[c][0] // PIECES[c][1], last[0]
        )
        last[0] = own
        return own

    def run_join(c, choices, final=False, blocks=1):
        last[0] = join_parts(outer.reshape(1), choices, widths[c], last[0], final, blocks)
        return last[0]

    def run_back(c, choices):
        backs[c] = run_join(c, choices, True).reshape(peers, own_rows, widths[c])

    def run_return(first, last_one):
        those = range(first, last_one + 1)
        moved = lax.all_to_all(jnp.concatenate([backs[c] for c in those], axis=2), "uly", split_axis=0, concat_axis=0, tiled=False)
        at = 0
        for c in those:
            backs[c] = moved[:, :, at : at + widths[c]]
            at += widths[c]

    state = [dict() for _ in range(count)]

    def run_sent(c):
        mine = run_attend(c, found[c]["sent"], [jnp.where(low, 3, 0), jnp.where(low, 2, 1)])
        state[c].update(far=mine, edge=send(mine, (0, 1), (3, 2)))

    def run_kept(c):
        blocks = [found[c]["near"], found[c]["own"]]
        mine = run_attend(c, [blocks, blocks], [place ^ 1, place])
        state[c].update(kept=mine, edge_near=send(mine[:1], (0, 1), (3, 2)))

    def run_cross(c):
        joint = run_join(c, [[(state[c]["far"], 0), (state[c]["edge"], 0)], []], blocks=2)
        state[c]["cross"] = send(joint, (1, 2), (2, 1))

    def run_outward(c):
        joint = run_join(c, [[(state[c]["kept"], 0), (state[c]["cross"], 0)], []])
        state[c]["outward"] = send(joint, (1, 0), (2, 3))

    def run_finish(c):
        inner = [(state[c]["kept"], 1), (state[c]["edge_near"], 0), (state[c]["cross"], 1)]
        run_back(c, [inner, [(state[c]["kept"], 1), (state[c]["outward"], 0)]])

    if line:
        run_sent(0)
        last[0] = run_spread(2, [found[1]["early"], last[0]])
        run_kept(0)
        run_sent(1)
        run_cross(0)
        run_kept(1)
        run_sent(2)
        run_outward(0)
        run_cross(1)
        run_kept(2)
        run_cross(2)
        run_finish(0)
        run_return(0, 0)
        run_outward(1)
        run_outward(2)
        run_finish(1)
        run_finish(2)
        run_return(1, 2)
    else:
        for c in range(count):
            if c > 1:
                last[0] = run_spread(c, [last[0]])
            parts = {d: [] for d in range(n)}
            for distances in (range(1, n, 2), range(0, n, 2)):
                blocks = [found[c]["found"][d] for d in distances]
                mine = run_attend(c, [blocks, blocks], [place ^ d for d in distances])
                for slot, d in enumerate(distances):
                    parts[d].append((mine, slot))
                if 1 in distances:
                    swapped = send(mine, *[(i, i ^ 1) for i in range(n)])
            for slot, d in enumerate(range(0, n, 2)):
                parts[d].append((swapped, slot))
            for bit in bits[1:]:
                for d in range(bit, n, 2 * bit):
                    joint = run_join(c, [parts[d], parts[d]])
                    parts[d ^ bit].append((send(joint, *[(i, i ^ bit) for i in range(n)]), 0))
            run_back(c, [parts[0], parts[0]])
            run_return(c, c)

    in_order = [backs[c] for c in sorted(range(count), key=lambda c: PIECES[c][0])]
    together = jnp.concatenate(in_order, axis=2)
    return together.transpose(1, 0, 2).reshape(own_rows, peers * group)


def solution(mesh):
    in_specs = (
        P(("cfg", "blk", "uly"), None),
        P(("cfg", "blk", "uly"), None),
        P(("cfg", "blk", "uly"), None),
        P(("cfg", "blk"), "uly"),
        P(("cfg", "blk"), "uly"),
        P(),
    )
    out_specs = P(("cfg", "blk", "uly"), None)
    return jax.shard_map(shards, mesh=mesh, in_specs=in_specs, out_specs=out_specs, check_vma=False)
```

```python
import functools

import jax
import jax.numpy as jnp
from jax import lax
from jax.experimental import pallas as pl
from jax.experimental.pallas import tpu as pltpu
from jax.sharding import PartitionSpec as P

DH = 128
TILE = 128
PIECES = ((0, 1), (1, 1), (2, 1))
PIECE_UNITS = 3
HALF = 256
CHUNK = 256
LOG2E = 1.4426950408889634
TINY = 1.0e-30
ONES = 16
SCALE2 = DH ** (-0.5) * LOG2E
MASKED = -1.0e30
MIB = 1024 * 1024
QUICK = pl.CostEstimate(flops=1024, bytes_accessed=1024, transcendentals=0)


def split3(x):
    hi = x.astype(jnp.bfloat16).astype(jnp.float32)
    rest = x - hi
    mid = rest.astype(jnp.bfloat16).astype(jnp.float32)
    lo = (rest - mid).astype(jnp.bfloat16).astype(jnp.float32)
    return hi, mid, lo


def stat_rows(width):
    return -(-3 * (width // DH) // 16) * 16


def attend_kernel(choices, table_ref, kept_ref, *refs):
    count = sum(len(c) for c in choices)
    sources, at = [], 0
    for c in choices:
        sources.append(refs[at : at + len(c)])
        at += len(c)
    ck_ref, nk_ref, cv_ref, nv_ref = refs[count : count + 4]
    out_ref, q_s, s0, s1, m0, m1, stat_s = refs[-7:]
    rows = q_s.shape[0]
    width = q_s.shape[1] // 2
    heads = width // DH
    ctx, new = ck_ref.shape[0], nk_ref.shape[0]
    subs = HALF // TILE
    halves = rows // HALF
    slots = ((s0, m0), (s1, m1))
    nt = (((1,), (1,)), ((), ()))
    step_no = pl.program_id(0)
    first_tile = table_ref[1 + step_no] * (rows // TILE)
    stat_s[...] = jnp.zeros_like(stat_s)
    for c, q_refs in enumerate(sources):
        for i, q_ref in enumerate(q_refs):

            @pl.when((step_no == i) & (table_ref[0] == c))
            def _():
                for head in range(heads):
                    scaled = q_ref[:, head * DH : (head + 1) * DH].astype(jnp.float32) * SCALE2
                    hi = scaled.astype(jnp.bfloat16)
                    lo = (scaled - hi.astype(jnp.float32)).astype(jnp.bfloat16)
                    q_s[:, 2 * head * DH : (2 * head + 1) * DH] = hi
                    q_s[:, (2 * head + 1) * DH : (2 * head + 2) * DH] = lo

    def columns(head, size=DH):
        return pl.ds(pl.multiple_of(head * size, size), size)

    chunks = [(k, v, at, base) for k, v, size, base in ((ck_ref, cv_ref, ctx, 0), (nk_ref, nv_ref, new, ctx))
              for at in range(0, size, CHUNK)]

    def kept(half, sub, row):
        return kept_ref[first_tile + half * subs + sub, row // TILE] > 0

    def score(head, half, chunk, q, tops):
        s_ref = slots[half % 2][0]
        k_ref, _, at, base = chunk
        size = min(CHUNK, k_ref.shape[0] - at)
        k = k_ref[at : at + size, columns(head)]
        scores = lax.dot_general(jnp.concatenate([k, k], axis=1), q, nt, preferred_element_type=jnp.float32)
        s_ref[base + at : base + at + size, :] = scores
        for j in range(0, size, TILE):
            for sub in range(subs):
                piece = scores[j : j + TILE, sub * TILE : (sub + 1) * TILE]
                top = jnp.max(piece.reshape(TILE // 8, 8, TILE), axis=0)
                top = jnp.where(kept(half, sub, base + at + j), top, MASKED)
                tops[sub] = top if tops[sub] is None else jnp.maximum(tops[sub], top)

    def weigh(head, half, chunk, high):
        s_ref = slots[half % 2][0]
        _, v_ref, at, base = chunk
        size = min(CHUNK, v_ref.shape[1] - at)
        lows = []
        for j in range(0, size, TILE):
            row = base + at + j
            pieces = []
            for sub in range(subs):
                lanes = slice(sub * TILE, (sub + 1) * TILE)
                less = jnp.where(kept(half, sub, row), high[:, lanes], -MASKED)
                pieces.append(jnp.exp2(s_ref[row : row + TILE, lanes] - less).astype(jnp.bfloat16))
            lows.append(jnp.concatenate(pieces, axis=1))
        low = jnp.concatenate(lows, axis=0)
        values = jnp.concatenate([v_ref[columns(head), at : at + size], jnp.ones((ONES, size), jnp.bfloat16)], axis=0)
        return jnp.dot(values, low, preferred_element_type=jnp.float32)

    def step(head, half, next_head, next_half, both=True):
        q = q_s[next_half * HALF : (next_half + 1) * HALF, columns(next_head, 2 * DH)]
        tops = [None] * subs
        if both:
            high = jnp.max(slots[half % 2][1][...], axis=0, keepdims=True)
            acc = None
        for chunk in chunks:
            score(next_head, next_half, chunk, q, tops)
            if both:
                found = weigh(head, half, chunk, high)
                acc = found if acc is None else acc + found
        for sub in range(subs):
            slots[next_half % 2][1][:, sub * TILE : (sub + 1) * TILE] = tops[sub]
        if both:
            total = jnp.maximum(acc[DH : DH + 1, :], TINY)
            lanes = slice(half * HALF, (half + 1) * HALF)
            out_ref[0, columns(head), lanes] = (acc[:DH, :] * (1.0 / total)).astype(jnp.bfloat16)
            for part, value in enumerate(split3(high + jnp.log2(total))):
                stat_s[pl.ds(3 * head + part, 1), lanes] = value

    step(0, 1, 0, 0, both=False)

    @pl.loop(0, heads)
    def _(head):
        for half in range(halves):
            if half + 1 < halves:
                step(head, half, head, half + 1)
            else:
                step(head, half, jnp.minimum(head + 1, heads - 1), 0)

    out_ref[0, width:, :] = stat_s[...].astype(jnp.bfloat16)


def attend(table, kept, choices, ctx_k, new_k, ctx_v, new_v, piece, dep):
    queries = [q for choice in choices for q in choice]
    rows, width = queries[0].shape
    ctx, new = ctx_k.shape[0], new_k.shape[0]
    heads = width // DH
    keys = ctx + new
    blocks = len(choices[0])
    across = lambda i, t, b: (0, piece)
    down = lambda i, t, b: (piece, 0)
    prow = width + stat_rows(width)
    return pl.pallas_call(
        functools.partial(attend_kernel, [[None] * len(c) for c in choices]),
        out_shape=jax.ShapeDtypeStruct((blocks, prow, rows), jnp.bfloat16),
        grid_spec=pltpu.PrefetchScalarGridSpec(
            num_scalar_prefetch=2,
            grid=(blocks,),
            in_specs=[pl.BlockSpec((rows, width), lambda i, t, b: (0, 0))] * len(queries)
            + [
                pl.BlockSpec((ctx, width), across),
                pl.BlockSpec((new, width), across),
                pl.BlockSpec((width, ctx), down),
                pl.BlockSpec((width, new), down),
                pl.BlockSpec(memory_space=pl.ANY),
            ],
            out_specs=pl.BlockSpec((1, prow, rows), lambda i, t, b: (i, 0, 0)),
            scratch_shapes=[
                pltpu.VMEM((rows, 2 * width), jnp.bfloat16),
                pltpu.VMEM((keys, HALF), jnp.float32),
                pltpu.VMEM((keys, HALF), jnp.float32),
                pltpu.VMEM((8, HALF), jnp.float32),
                pltpu.VMEM((8, HALF), jnp.float32),
                pltpu.VMEM((stat_rows(width), rows), jnp.float32),
            ],
        ),
        compiler_params=pltpu.CompilerParams(vmem_limit_bytes=28 * MIB),
        cost_estimate=pl.CostEstimate(
            flops=16 * blocks * rows * keys * DH * heads,
            bytes_accessed=4 * blocks * rows * width + 4 * keys * width,
            transcendentals=blocks * rows * keys * heads,
        ),
        name="attend",
    )(table, kept, *queries, ctx_k, new_k, ctx_v, new_v, dep)


def combine(refs, width, emit):
    stats = []
    for ref in refs:
        terms = ref[0, width:, :].astype(jnp.float32)
        stats.append([terms[3 * h : 3 * h + 1] + terms[3 * h + 1 : 3 * h + 2] + terms[3 * h + 2 : 3 * h + 3]
                      for h in range(width // DH)])
    for head in range(width // DH):
        logs = [s[head] for s in stats]
        top = functools.reduce(jnp.maximum, logs)
        weights = [jnp.exp2(l - top) for l in logs]
        total = functools.reduce(jnp.add, weights)
        value = None
        for ref, weight in zip(refs, weights):
            part = ref[0, head * DH : (head + 1) * DH, :].astype(jnp.float32) * (weight / total)
            value = part if value is None else value + part
        emit(head, value, top + jnp.log2(total))


def join_kernel_of(sizes, final, table_ref, *refs):
    sources, at = [], 0
    for size in sizes:
        sources.append(refs[at : at + size])
        at += size
    if final:
        out_ref = refs[-1]
        width = out_ref.shape[1]
    else:
        out_ref, stat_ref = refs[-2:]
        width = out_ref.shape[1] - stat_ref.shape[0]

    def emit(head, value, log):
        at = slice(head * DH, (head + 1) * DH)
        if final:
            out_ref[:, at] = jnp.transpose(value).astype(jnp.bfloat16)
            return
        out_ref[0, at, :] = value.astype(jnp.bfloat16)
        for part, term in enumerate(split3(log)):
            stat_ref[3 * head + part : 3 * head + part + 1, :] = term

    for c, chosen in enumerate(sources):
        if chosen:

            @pl.when(table_ref[0] == c)
            def _():
                if not final:
                    stat_ref[...] = jnp.zeros_like(stat_ref)
                combine(chosen, width, emit)
                if not final:
                    out_ref[0, width:, :] = stat_ref[...].astype(jnp.bfloat16)


def join_parts(table, choices, width, dep, final, blocks=1):
    parts = [part for choice in choices for part in choice]
    _, prow, rows = parts[0][0].shape
    specs = [
        pl.BlockSpec((1, prow, rows), functools.partial(lambda slot, i, t: (slot + i, 0, 0), slot)) for _, slot in parts
    ]
    shape = (rows, width) if final else (blocks, prow, rows)
    out_spec = pl.BlockSpec(shape, lambda i, t: (0, 0)) if final else pl.BlockSpec((1, prow, rows), lambda i, t: (i, 0, 0))
    return pl.pallas_call(
        functools.partial(join_kernel_of, [len(c) for c in choices], final),
        out_shape=jax.ShapeDtypeStruct(shape, jnp.bfloat16),
        grid_spec=pltpu.PrefetchScalarGridSpec(
            num_scalar_prefetch=1,
            grid=(blocks,),
            in_specs=specs + [pl.BlockSpec(memory_space=pl.ANY)],
            out_specs=out_spec,
            scratch_shapes=[] if final else [pltpu.VMEM((prow - width, rows), jnp.float32)],
        ),
        compiler_params=pltpu.CompilerParams(vmem_limit_bytes=16 * MIB),
        cost_estimate=QUICK,
        name="finish" if final else "merge",
    )(table, *[array for array, _ in parts], dep)


def part_kernel(peers, starts, peer_ref, *refs):
    outs = refs[-peers:]
    at = 0
    for i, start in enumerate(starts):
        for k in range(peers):
            ref = refs[i * peers + k]
            outs[k][:, at : at + ref.shape[1] - start] = ref[:, start:]
        at += ref.shape[1] - start


def parts_for_peers(peer, arrays, starts, peers, dep):
    rows, group = arrays[0].shape[0], arrays[0].shape[1] // peers
    specs = [pl.BlockSpec((rows, group), functools.partial(lambda k, i, t: (0, t[0] ^ k), k)) for k in range(peers)]
    shape = (rows, len(arrays) * group - sum(starts))
    return pl.pallas_call(
        functools.partial(part_kernel, peers, starts),
        out_shape=[jax.ShapeDtypeStruct(shape, jnp.bfloat16)] * peers,
        grid_spec=pltpu.PrefetchScalarGridSpec(
            num_scalar_prefetch=1,
            grid=(1,),
            in_specs=specs * len(arrays) + [pl.BlockSpec(memory_space=pl.ANY)],
            out_specs=[pl.BlockSpec(shape, lambda i, t: (0, 0))] * peers,
        ),
        compiler_params=pltpu.CompilerParams(vmem_limit_bytes=28 * MIB),
        cost_estimate=QUICK,
        name="parts",
    )(peer.reshape(1), *[a for a in arrays for _ in range(peers)], dep)


def regroup_kernel(peers, start, peer_ref, *refs):
    out_ref = refs[-1]
    rows, width = refs[0].shape[0], out_ref.shape[1]
    for k in range(peers):
        here = pl.ds(pl.multiple_of((peer_ref[0] ^ k) * rows, rows), rows)
        out_ref[here, :] = refs[k][:, start : start + width]


def regrouped(peer, pieces, start, width, deps):
    peers, rows = len(pieces), pieces[0].shape[0]
    whole = lambda i, t: (0, 0)
    shape = (peers * rows, width)
    return pl.pallas_call(
        functools.partial(regroup_kernel, peers, start),
        out_shape=jax.ShapeDtypeStruct(shape, jnp.bfloat16),
        grid_spec=pltpu.PrefetchScalarGridSpec(
            num_scalar_prefetch=1,
            grid=(1,),
            in_specs=[pl.BlockSpec(p.shape, whole) for p in pieces] + [pl.BlockSpec(memory_space=pl.ANY)] * len(deps),
            out_specs=pl.BlockSpec(shape, whole),
        ),
        compiler_params=pltpu.CompilerParams(vmem_limit_bytes=16 * MIB),
        cost_estimate=QUICK,
        name="regroup",
    )(peer.reshape(1), *pieces, *deps)


def join_kernel(*refs):
    pieces, (k_ref, v_ref, v_s) = refs[:-4], refs[-3:]
    rows, group = pieces[0].shape[0], k_ref.shape[1]
    for i, piece in enumerate(pieces):
        k_ref[i * rows : (i + 1) * rows, :] = piece[:, :group]
        v_s[i * rows : (i + 1) * rows, :] = piece[:, group : 2 * group]
    for at in range(0, v_s.shape[0], TILE):
        v_ref[:, at : at + TILE] = jnp.transpose(v_s[at : at + TILE, :])


def joined(pieces, group, dep):
    rows = pieces[0].shape[0] * len(pieces)
    return pl.pallas_call(
        join_kernel,
        out_shape=[
            jax.ShapeDtypeStruct((rows, group), jnp.bfloat16),
            jax.ShapeDtypeStruct((group, rows), jnp.bfloat16),
        ],
        in_specs=[pl.BlockSpec(memory_space=pltpu.VMEM)] * len(pieces) + [pl.BlockSpec(memory_space=pl.ANY)],
        scratch_shapes=[pltpu.VMEM((rows, group), jnp.bfloat16)],
        compiler_params=pltpu.CompilerParams(vmem_limit_bytes=24 * MIB),
        cost_estimate=QUICK,
        name="join",
    )(*pieces, dep)


def shards(new_queries, new_keys, new_values, context_keys, context_values, keep_flags):
    n = lax.axis_size("blk")
    place = lax.axis_index("blk").astype(jnp.int32)
    peers = lax.axis_size("uly")
    own_rows = new_queries.shape[0]
    group = context_keys.shape[1]
    unit = group // PIECE_UNITS
    span_rows = own_rows * peers
    ctx_tiles, new_tiles = context_keys.shape[0] // TILE, span_rows // TILE

    peer = lax.axis_index("uly").astype(jnp.int32)
    new_order = jnp.arange(new_tiles, dtype=jnp.int32) ^ (peer * own_rows // TILE)
    new_kept = lax.dynamic_slice_in_dim(keep_flags, n * ctx_tiles + place * new_tiles, new_tiles, 1)
    kept = jnp.concatenate(
        [
            lax.dynamic_slice_in_dim(keep_flags, place * ctx_tiles, ctx_tiles, 1),
            jnp.sum(jnp.where(new_order[:, None] == jnp.arange(new_tiles), new_kept[:, None, :], 0), axis=2),
        ],
        axis=1,
    )
    kept = (kept == 1).astype(jnp.int32)
    count = len(PIECES)
    widths = [units * unit for _, units in PIECES]
    backs = [None] * count

    def to_heads(pieces):
        moved = lax.all_to_all(pieces, "uly", split_axis=0, concat_axis=0, tiled=False)
        return moved.reshape(span_rows, pieces.shape[2])

    def to_peers(pieces):
        return [lax.ppermute(p, "uly", [(i, i ^ k) for i in range(peers)]) if k else p for k, p in enumerate(pieces)]

    def send(x, *pairs):
        return lax.ppermute(x, "blk", pairs)

    def spread_line(span):
        near = send(span, (0, 1), (1, 0), (2, 3), (3, 2))
        third = send(span, (1, 2), (2, 1))
        far = send(near, (1, 2), (2, 1))
        third_out = send(third, (1, 0), (2, 3))
        far_out = send(far, (1, 0), (2, 3))
        return dict(own=span, near=near, sent=[[far, third], [far_out, third_out]], early=third, end=far_out)

    def spread_cube(span):
        found = {0: span}
        for bit in reversed(bits):
            for d in list(found):
                found[d ^ bit] = send(found[d], *[(i, i ^ bit) for i in range(n)])
        return dict(found=found, early=found[n // 2], end=found[n - 1])

    bits = [1 << k for k in range((n - 1).bit_length())]
    line = n == 4
    spread = spread_line if line else spread_cube
    early = widths[0]
    first_span = to_heads(jnp.stack([new_queries[:, p * group : p * group + early] for p in range(peers)]))
    found = [spread(first_span)]
    moved = to_peers(parts_for_peers(peer, [new_keys, new_values, new_queries], [0, 0, early], peers, first_span))

    def run_spread(c, deps):
        span = regrouped(peer, moved, 2 * group + PIECES[c][0] * unit - early, widths[c], deps)
        found.append(spread(span))
        return span

    span_k, span_v_t = joined(moved, group, run_spread(1, [found[0]["end"]]))
    context_values_t = context_values.T
    last = [span_k]
    outer = ((place == 0) | (place == n - 1)).astype(jnp.int32)
    low = place < n // 2

    def run_attend(c, choices, targets):
        table = jnp.stack([outer, *targets]).astype(jnp.int32)
        own = attend(
            table, kept, choices, context_keys, span_k, context_values_t, span_v_t, PIECES[c][0] // PIECES[c][1], last[0]
        )
        last[0] = own
        return own

    def run_join(c, choices, final=False, blocks=1):
        last[0] = join_parts(outer.reshape(1), choices, widths[c], last[0], final, blocks)
        return last[0]

    def run_back(c, choices):
        backs[c] = run_join(c, choices, True).reshape(peers, own_rows, widths[c])

    def run_return(first, last_one):
        those = range(first, last_one + 1)
        moved = lax.all_to_all(jnp.concatenate([backs[c] for c in those], axis=2), "uly", split_axis=0, concat_axis=0, tiled=False)
        at = 0
        for c in those:
            backs[c] = moved[:, :, at : at + widths[c]]
            at += widths[c]

    state = [dict() for _ in range(count)]

    def run_sent(c):
        mine = run_attend(c, found[c]["sent"], [jnp.where(low, 3, 0), jnp.where(low, 2, 1)])
        state[c].update(far=mine, edge=send(mine, (0, 1), (3, 2)))

    def run_kept(c):
        blocks = [found[c]["near"], found[c]["own"]]
        mine = run_attend(c, [blocks, blocks], [place ^ 1, place])
        state[c].update(kept=mine, edge_near=send(mine[:1], (0, 1), (3, 2)))

    def run_cross(c):
        joint = run_join(c, [[(state[c]["far"], 0), (state[c]["edge"], 0)], []], blocks=2)
        state[c]["cross"] = send(joint, (1, 2), (2, 1))

    def run_outward(c):
        joint = run_join(c, [[(state[c]["kept"], 0), (state[c]["cross"], 0)], []])
        state[c]["outward"] = send(joint, (1, 0), (2, 3))

    def run_finish(c):
        inner = [(state[c]["kept"], 1), (state[c]["edge_near"], 0), (state[c]["cross"], 1)]
        run_back(c, [inner, [(state[c]["kept"], 1), (state[c]["outward"], 0)]])

    if line:
        run_sent(0)
        last[0] = run_spread(2, [found[1]["early"], last[0]])
        run_kept(0)
        run_sent(1)
        run_cross(0)
        run_kept(1)
        run_sent(2)
        run_outward(0)
        run_cross(1)
        run_kept(2)
        run_cross(2)
        run_finish(0)
        run_return(0, 0)
        run_outward(1)
        run_outward(2)
        run_finish(1)
        run_finish(2)
        run_return(1, 2)
    else:
        for c in range(count):
            if c > 1:
                last[0] = run_spread(c, [last[0]])
            parts = {d: [] for d in range(n)}
            for distances in (range(1, n, 2), range(0, n, 2)):
                blocks = [found[c]["found"][d] for d in distances]
                mine = run_attend(c, [blocks, blocks], [place ^ d for d in distances])
                for slot, d in enumerate(distances):
                    parts[d].append((mine, slot))
                if 1 in distances:
                    swapped = send(mine, *[(i, i ^ 1) for i in range(n)])
            for slot, d in enumerate(range(0, n, 2)):
                parts[d].append((swapped, slot))
            for bit in bits[1:]:
                for d in range(bit, n, 2 * bit):
                    joint = run_join(c, [parts[d], parts[d]])
                    parts[d ^ bit].append((send(joint, *[(i, i ^ bit) for i in range(n)]), 0))
            run_back(c, [parts[0], parts[0]])
            run_return(c, c)

    in_order = [backs[c] for c in sorted(range(count), key=lambda c: PIECES[c][0])]
    together = jnp.concatenate(in_order, axis=2)
    return together.transpose(1, 0, 2).reshape(own_rows, peers * group)


def solution(mesh):
    in_specs = (
        P(("cfg", "blk", "uly"), None),
        P(("cfg", "blk", "uly"), None),
        P(("cfg", "blk", "uly"), None),
        P(("cfg", "blk"), "uly"),
        P(("cfg", "blk"), "uly"),
        P(),
    )
    out_specs = P(("cfg", "blk", "uly"), None)
    return jax.shard_map(shards, mesh=mesh, in_specs=in_specs, out_specs=out_specs, check_vma=False)
```

```python
import functools

import jax
import jax.numpy as jnp
from jax import lax
from jax.experimental import pallas as pl
from jax.experimental.pallas import tpu as pltpu
from jax.sharding import PartitionSpec as P

DH = 128
TILE = 128
PIECES = ((0, 1), (1, 1), (2, 1))
PIECE_UNITS = 3
HALF = 256
CHUNK = 256
LOG2E = 1.4426950408889634
TINY = 1.0e-30
ONES = 16
SCALE2 = DH ** (-0.5) * LOG2E
MASKED = -1.0e30
MIB = 1024 * 1024
QUICK = pl.CostEstimate(flops=1024, bytes_accessed=1024, transcendentals=0)


def split3(x):
    hi = x.astype(jnp.bfloat16).astype(jnp.float32)
    rest = x - hi
    mid = rest.astype(jnp.bfloat16).astype(jnp.float32)
    lo = (rest - mid).astype(jnp.bfloat16).astype(jnp.float32)
    return hi, mid, lo


def stat_rows(width):
    return -(-3 * (width // DH) // 16) * 16


def attend_kernel(choices, table_ref, kept_ref, *refs):
    count = sum(len(c) for c in choices)
    sources, at = [], 0
    for c in choices:
        sources.append(refs[at : at + len(c)])
        at += len(c)
    ck_ref, nk_ref, cv_ref, nv_ref = refs[count : count + 4]
    out_ref, q_s, s0, s1, m0, m1, stat_s = refs[-7:]
    rows = q_s.shape[0]
    width = q_s.shape[1] // 2
    heads = width // DH
    ctx, new = ck_ref.shape[0], nk_ref.shape[0]
    subs = HALF // TILE
    halves = rows // HALF
    slots = ((s0, m0), (s1, m1))
    nt = (((1,), (1,)), ((), ()))
    step_no = pl.program_id(0)
    first_tile = table_ref[1 + step_no] * (rows // TILE)
    stat_s[...] = jnp.zeros_like(stat_s)
    for c, q_refs in enumerate(sources):
        for i, q_ref in enumerate(q_refs):

            @pl.when((step_no == i) & (table_ref[0] == c))
            def _():
                for head in range(heads):
                    scaled = q_ref[:, head * DH : (head + 1) * DH].astype(jnp.float32) * SCALE2
                    hi = scaled.astype(jnp.bfloat16)
                    lo = (scaled - hi.astype(jnp.float32)).astype(jnp.bfloat16)
                    q_s[:, 2 * head * DH : (2 * head + 1) * DH] = hi
                    q_s[:, (2 * head + 1) * DH : (2 * head + 2) * DH] = lo

    def columns(head, size=DH):
        return pl.ds(pl.multiple_of(head * size, size), size)

    chunks = [(k, v, at, base) for k, v, size, base in ((ck_ref, cv_ref, ctx, 0), (nk_ref, nv_ref, new, ctx))
              for at in range(0, size, CHUNK)]

    def kept(half, sub, row):
        return kept_ref[first_tile + half * subs + sub, row // TILE] > 0

    def score(head, half, chunk, q, tops):
        s_ref = slots[half % 2][0]
        k_ref, _, at, base = chunk
        size = min(CHUNK, k_ref.shape[0] - at)
        k = k_ref[at : at + size, columns(head)]
        scores = lax.dot_general(jnp.concatenate([k, k], axis=1), q, nt, preferred_element_type=jnp.float32)
        s_ref[base + at : base + at + size, :] = scores
        for j in range(0, size, TILE):
            for sub in range(subs):
                piece = scores[j : j + TILE, sub * TILE : (sub + 1) * TILE]
                top = jnp.max(piece.reshape(TILE // 8, 8, TILE), axis=0)
                top = jnp.where(kept(half, sub, base + at + j), top, MASKED)
                tops[sub] = top if tops[sub] is None else jnp.maximum(tops[sub], top)

    def weigh(head, half, chunk, high):
        s_ref = slots[half % 2][0]
        _, v_ref, at, base = chunk
        size = min(CHUNK, v_ref.shape[1] - at)
        lows = []
        for j in range(0, size, TILE):
            row = base + at + j
            pieces = []
            for sub in range(subs):
                lanes = slice(sub * TILE, (sub + 1) * TILE)
                less = jnp.where(kept(half, sub, row), high[:, lanes], -MASKED)
                pieces.append(jnp.exp2(s_ref[row : row + TILE, lanes] - less).astype(jnp.bfloat16))
            lows.append(jnp.concatenate(pieces, axis=1))
        low = jnp.concatenate(lows, axis=0)
        values = jnp.concatenate([v_ref[columns(head), at : at + size], jnp.ones((ONES, size), jnp.bfloat16)], axis=0)
        return jnp.dot(values, low, preferred_element_type=jnp.float32)

    def step(head, half, next_head, next_half, both=True):
        q = q_s[next_half * HALF : (next_half + 1) * HALF, columns(next_head, 2 * DH)]
        tops = [None] * subs
        if both:
            high = jnp.max(slots[half % 2][1][...], axis=0, keepdims=True)
            acc = None
        for chunk in chunks:
            score(next_head, next_half, chunk, q, tops)
            if both:
                found = weigh(head, half, chunk, high)
                acc = found if acc is None else acc + found
        for sub in range(subs):
            slots[next_half % 2][1][:, sub * TILE : (sub + 1) * TILE] = tops[sub]
        if both:
            total = jnp.maximum(acc[DH : DH + 1, :], TINY)
            lanes = slice(half * HALF, (half + 1) * HALF)
            out_ref[0, columns(head), lanes] = (acc[:DH, :] * (1.0 / total)).astype(jnp.bfloat16)
            for part, value in enumerate(split3(high + jnp.log2(total))):
                stat_s[pl.ds(3 * head + part, 1), lanes] = value

    step(0, 1, 0, 0, both=False)

    @pl.loop(0, heads)
    def _(head):
        for half in range(halves):
            if half + 1 < halves:
                step(head, half, head, half + 1)
            else:
                step(head, half, jnp.minimum(head + 1, heads - 1), 0)

    out_ref[0, width:, :] = stat_s[...].astype(jnp.bfloat16)


def attend(table, kept, choices, ctx_k, new_k, ctx_v, new_v, piece, dep):
    queries = [q for choice in choices for q in choice]
    rows, width = queries[0].shape
    ctx, new = ctx_k.shape[0], new_k.shape[0]
    heads = width // DH
    keys = ctx + new
    blocks = len(choices[0])
    across = lambda i, t, b: (0, piece)
    down = lambda i, t, b: (piece, 0)
    prow = width + stat_rows(width)
    return pl.pallas_call(
        functools.partial(attend_kernel, [[None] * len(c) for c in choices]),
        out_shape=jax.ShapeDtypeStruct((blocks, prow, rows), jnp.bfloat16),
        grid_spec=pltpu.PrefetchScalarGridSpec(
            num_scalar_prefetch=2,
            grid=(blocks,),
            in_specs=[pl.BlockSpec((rows, width), lambda i, t, b: (0, 0))] * len(queries)
            + [
                pl.BlockSpec((ctx, width), across),
                pl.BlockSpec((new, width), across),
                pl.BlockSpec((width, ctx), down),
                pl.BlockSpec((width, new), down),
                pl.BlockSpec(memory_space=pl.ANY),
            ],
            out_specs=pl.BlockSpec((1, prow, rows), lambda i, t, b: (i, 0, 0)),
            scratch_shapes=[
                pltpu.VMEM((rows, 2 * width), jnp.bfloat16),
                pltpu.VMEM((keys, HALF), jnp.float32),
                pltpu.VMEM((keys, HALF), jnp.float32),
                pltpu.VMEM((8, HALF), jnp.float32),
                pltpu.VMEM((8, HALF), jnp.float32),
                pltpu.VMEM((stat_rows(width), rows), jnp.float32),
            ],
        ),
        compiler_params=pltpu.CompilerParams(vmem_limit_bytes=28 * MIB),
        cost_estimate=pl.CostEstimate(
            flops=8 * blocks * rows * keys * DH * heads,
            bytes_accessed=4 * blocks * rows * width + 4 * keys * width,
            transcendentals=blocks * rows * keys * heads,
        ),
        name="attend",
    )(table, kept, *queries, ctx_k, new_k, ctx_v, new_v, dep)


def combine(refs, width, emit):
    stats = []
    for ref in refs:
        terms = ref[0, width:, :].astype(jnp.float32)
        stats.append([terms[3 * h : 3 * h + 1] + terms[3 * h + 1 : 3 * h + 2] + terms[3 * h + 2 : 3 * h + 3]
                      for h in range(width // DH)])
    for head in range(width // DH):
        logs = [s[head] for s in stats]
        top = functools.reduce(jnp.maximum, logs)
        weights = [jnp.exp2(l - top) for l in logs]
        total = functools.reduce(jnp.add, weights)
        value = None
        for ref, weight in zip(refs, weights):
            part = ref[0, head * DH : (head + 1) * DH, :].astype(jnp.float32) * (weight / total)
            value = part if value is None else value + part
        emit(head, value, top + jnp.log2(total))


def join_kernel_of(sizes, final, table_ref, *refs):
    sources, at = [], 0
    for size in sizes:
        sources.append(refs[at : at + size])
        at += size
    if final:
        out_ref = refs[-1]
        width = out_ref.shape[1]
    else:
        out_ref, stat_ref = refs[-2:]
        width = out_ref.shape[1] - stat_ref.shape[0]

    def emit(head, value, log):
        at = slice(head * DH, (head + 1) * DH)
        if final:
            out_ref[:, at] = jnp.transpose(value).astype(jnp.bfloat16)
            return
        out_ref[0, at, :] = value.astype(jnp.bfloat16)
        for part, term in enumerate(split3(log)):
            stat_ref[3 * head + part : 3 * head + part + 1, :] = term

    for c, chosen in enumerate(sources):
        if chosen:

            @pl.when(table_ref[0] == c)
            def _():
                if not final:
                    stat_ref[...] = jnp.zeros_like(stat_ref)
                combine(chosen, width, emit)
                if not final:
                    out_ref[0, width:, :] = stat_ref[...].astype(jnp.bfloat16)


def join_parts(table, choices, width, dep, final, blocks=1):
    parts = [part for choice in choices for part in choice]
    _, prow, rows = parts[0][0].shape
    specs = [
        pl.BlockSpec((1, prow, rows), functools.partial(lambda slot, i, t: (slot + i, 0, 0), slot)) for _, slot in parts
    ]
    shape = (rows, width) if final else (blocks, prow, rows)
    out_spec = pl.BlockSpec(shape, lambda i, t: (0, 0)) if final else pl.BlockSpec((1, prow, rows), lambda i, t: (i, 0, 0))
    return pl.pallas_call(
        functools.partial(join_kernel_of, [len(c) for c in choices], final),
        out_shape=jax.ShapeDtypeStruct(shape, jnp.bfloat16),
        grid_spec=pltpu.PrefetchScalarGridSpec(
            num_scalar_prefetch=1,
            grid=(blocks,),
            in_specs=specs + [pl.BlockSpec(memory_space=pl.ANY)],
            out_specs=out_spec,
            scratch_shapes=[] if final else [pltpu.VMEM((prow - width, rows), jnp.float32)],
        ),
        compiler_params=pltpu.CompilerParams(vmem_limit_bytes=16 * MIB),
        cost_estimate=QUICK,
        name="finish" if final else "merge",
    )(table, *[array for array, _ in parts], dep)


def part_kernel(peers, count, start, peer_ref, *refs):
    rows = refs[0].shape[0]
    outs = refs[-peers:]
    for i, ref in enumerate(refs[: count * peers]):
        outs[i % peers][i // peers * rows : (i // peers + 1) * rows, :] = ref[:, start:]


def parts_for_peers(peer, arrays, start, peers, deps):
    rows, group = arrays[0].shape[0], arrays[0].shape[1] // peers
    specs = [pl.BlockSpec((rows, group), functools.partial(lambda k, i, t: (0, t[0] ^ k), k)) for k in range(peers)]
    shape = (len(arrays) * rows, group - start)
    return pl.pallas_call(
        functools.partial(part_kernel, peers, len(arrays), start),
        out_shape=[jax.ShapeDtypeStruct(shape, jnp.bfloat16)] * peers,
        grid_spec=pltpu.PrefetchScalarGridSpec(
            num_scalar_prefetch=1,
            grid=(1,),
            in_specs=specs * len(arrays) + [pl.BlockSpec(memory_space=pl.ANY)] * len(deps),
            out_specs=[pl.BlockSpec(shape, lambda i, t: (0, 0))] * peers,
        ),
        compiler_params=pltpu.CompilerParams(vmem_limit_bytes=28 * MIB),
        cost_estimate=QUICK,
        name="parts",
    )(peer.reshape(1), *[a for a in arrays for _ in range(peers)], *deps)


def regroup_kernel(peers, start, peer_ref, *refs):
    out_ref = refs[-1]
    rows, width = refs[0].shape[0], out_ref.shape[1]
    for k in range(peers):
        here = pl.ds(pl.multiple_of((peer_ref[0] ^ k) * rows, rows), rows)
        out_ref[here, :] = refs[k][:, start : start + width]


def regrouped(peer, pieces, start, width, deps):
    peers, rows = len(pieces), pieces[0].shape[0]
    whole = lambda i, t: (0, 0)
    shape = (peers * rows, width)
    return pl.pallas_call(
        functools.partial(regroup_kernel, peers, start),
        out_shape=jax.ShapeDtypeStruct(shape, jnp.bfloat16),
        grid_spec=pltpu.PrefetchScalarGridSpec(
            num_scalar_prefetch=1,
            grid=(1,),
            in_specs=[pl.BlockSpec(p.shape, whole) for p in pieces] + [pl.BlockSpec(memory_space=pl.ANY)] * len(deps),
            out_specs=pl.BlockSpec(shape, whole),
        ),
        compiler_params=pltpu.CompilerParams(vmem_limit_bytes=16 * MIB),
        cost_estimate=QUICK,
        name="regroup",
    )(peer.reshape(1), *pieces, *deps)


def join_kernel(*refs):
    pieces, (k_ref, v_ref, v_s) = refs[:-4], refs[-3:]
    rows = pieces[0].shape[0] // 2
    for i, piece in enumerate(pieces):
        k_ref[i * rows : (i + 1) * rows, :] = piece[:rows, :]
        v_s[i * rows : (i + 1) * rows, :] = piece[rows:, :]
    for at in range(0, v_s.shape[0], TILE):
        v_ref[:, at : at + TILE] = jnp.transpose(v_s[at : at + TILE, :])


def joined(pieces, dep):
    rows, group = pieces[0].shape[0] // 2 * len(pieces), pieces[0].shape[1]
    return pl.pallas_call(
        join_kernel,
        out_shape=[
            jax.ShapeDtypeStruct((rows, group), jnp.bfloat16),
            jax.ShapeDtypeStruct((group, rows), jnp.bfloat16),
        ],
        in_specs=[pl.BlockSpec(memory_space=pltpu.VMEM)] * len(pieces) + [pl.BlockSpec(memory_space=pl.ANY)],
        scratch_shapes=[pltpu.VMEM((rows, group), jnp.bfloat16)],
        compiler_params=pltpu.CompilerParams(vmem_limit_bytes=24 * MIB),
        cost_estimate=QUICK,
        name="join",
    )(*pieces, dep)


def shards(new_queries, new_keys, new_values, context_keys, context_values, keep_flags):
    n = lax.axis_size("blk")
    place = lax.axis_index("blk").astype(jnp.int32)
    peers = lax.axis_size("uly")
    own_rows = new_queries.shape[0]
    group = context_keys.shape[1]
    unit = group // PIECE_UNITS
    span_rows = own_rows * peers
    ctx_tiles, new_tiles = context_keys.shape[0] // TILE, span_rows // TILE

    peer = lax.axis_index("uly").astype(jnp.int32)
    new_order = jnp.arange(new_tiles, dtype=jnp.int32) ^ (peer * own_rows // TILE)
    new_kept = lax.dynamic_slice_in_dim(keep_flags, n * ctx_tiles + place * new_tiles, new_tiles, 1)
    kept = jnp.concatenate(
        [
            lax.dynamic_slice_in_dim(keep_flags, place * ctx_tiles, ctx_tiles, 1),
            jnp.sum(jnp.where(new_order[:, None] == jnp.arange(new_tiles), new_kept[:, None, :], 0), axis=2),
        ],
        axis=1,
    )
    kept = (kept == 1).astype(jnp.int32)
    count = len(PIECES)
    widths = [units * unit for _, units in PIECES]
    backs = [None] * count

    def to_heads(pieces):
        moved = lax.all_to_all(pieces, "uly", split_axis=0, concat_axis=0, tiled=False)
        return moved.reshape(span_rows, pieces.shape[2])

    def to_peers(pieces):
        return [lax.ppermute(p, "uly", [(i, i ^ k) for i in range(peers)]) if k else p for k, p in enumerate(pieces)]

    def send(x, *pairs):
        return lax.ppermute(x, "blk", pairs)

    def spread_line(span):
        near = send(span, (0, 1), (1, 0), (2, 3), (3, 2))
        third = send(span, (1, 2), (2, 1))
        far = send(near, (1, 2), (2, 1))
        third_out = send(third, (1, 0), (2, 3))
        far_out = send(far, (1, 0), (2, 3))
        return dict(own=span, near=near, sent=[[far, third], [far_out, third_out]], early=third, mid=third_out)

    def spread_cube(span):
        found = {0: span}
        for bit in reversed(bits):
            for d in list(found):
                found[d ^ bit] = send(found[d], *[(i, i ^ bit) for i in range(n)])
        return dict(found=found, early=found[n // 2], mid=found[n // 2])

    bits = [1 << k for k in range((n - 1).bit_length())]
    line = n == 4
    spread = spread_line if line else spread_cube
    early = widths[0]
    first_span = to_heads(jnp.stack([new_queries[:, p * group : p * group + early] for p in range(peers)]))
    found = [spread(first_span)]
    parts_q = parts_for_peers(peer, [new_queries], early, peers, [first_span])
    later = to_peers(parts_q)
    parts_kv = parts_for_peers(peer, [new_keys, new_values], 0, peers, [*later, found[0]["early"]])

    def run_spread(c, deps):
        span = regrouped(peer, later, PIECES[c][0] * unit - early, widths[c], deps)
        found.append(spread(span))
        return span

    latest = parts_kv[0]
    for c in range(1, count):
        latest = run_spread(c, [found[c - 1]["early"], latest])
    span_k, span_v_t = joined(to_peers(parts_kv), latest)
    context_values_t = context_values.T
    last = [span_k]
    outer = ((place == 0) | (place == n - 1)).astype(jnp.int32)
    low = place < n // 2

    def run_attend(c, choices, targets):
        table = jnp.stack([outer, *targets]).astype(jnp.int32)
        own = attend(
            table, kept, choices, context_keys, span_k, context_values_t, span_v_t, PIECES[c][0] // PIECES[c][1], last[0]
        )
        last[0] = own
        return own

    def run_join(c, choices, final=False, blocks=1):
        last[0] = join_parts(outer.reshape(1), choices, widths[c], last[0], final, blocks)
        return last[0]

    def run_back(c, choices):
        backs[c] = run_join(c, choices, True).reshape(peers, own_rows, widths[c])

    def run_return(*those):
        joint = jnp.concatenate([backs[c] for c in those], axis=2)
        joint = lax.all_to_all(joint, "uly", split_axis=0, concat_axis=0, tiled=False)
        at = 0
        for c in those:
            backs[c] = joint[:, :, at : at + widths[c]]
            at += widths[c]

    state = [dict() for _ in range(count)]

    def run_sent(c):
        mine = run_attend(c, found[c]["sent"], [jnp.where(low, 3, 0), jnp.where(low, 2, 1)])
        state[c].update(far=mine, edge=send(mine, (0, 1), (3, 2)))

    def run_kept(c):
        blocks = [found[c]["near"], found[c]["own"]]
        mine = run_attend(c, [blocks, blocks], [place ^ 1, place])
        state[c].update(kept=mine, edge_near=send(mine[:1], (0, 1), (3, 2)))

    def run_cross(c):
        joint = run_join(c, [[(state[c]["far"], 0), (state[c]["edge"], 0)], []], blocks=2)
        state[c]["cross"] = send(joint, (1, 2), (2, 1))

    def run_outward(c):
        joint = run_join(c, [[(state[c]["kept"], 0), (state[c]["cross"], 0)], []])
        state[c]["outward"] = send(joint, (1, 0), (2, 3))

    def run_finish(c):
        inner = [(state[c]["kept"], 1), (state[c]["edge_near"], 0), (state[c]["cross"], 1)]
        run_back(c, [inner, [(state[c]["kept"], 1), (state[c]["outward"], 0)]])

    def run_halves(c):
        inner, outer_ones = found[c]["sent"]
        near, own = found[c]["near"], found[c]["own"]
        mine = run_attend(c, [[near, inner[1]], [near, outer_ones[0]]], [place ^ 1, place ^ 3])
        state[c].update(swap=send(mine, (0, 1), (1, 0), (2, 3), (3, 2)), rest=[[own, inner[0]], [own, outer_ones[1]]])

    def run_halves_kept(c):
        state[c]["kept"] = run_attend(c, state[c]["rest"], [place, place ^ 2])

    def run_halves_join(c):
        pair = [(state[c]["kept"], 1), (state[c]["swap"], 1)]
        state[c]["across"] = send(run_join(c, [pair, pair]), (0, 2), (2, 0), (1, 3), (3, 1))

    def run_halves_finish(c):
        three = [(state[c]["kept"], 0), (state[c]["swap"], 0), (state[c]["across"], 0)]
        run_back(c, [three, three])

    if line:
        run_sent(0)
        run_kept(0)
        run_sent(1)
        run_cross(0)
        run_kept(1)
        run_halves(2)
        run_outward(0)
        run_cross(1)
        run_halves_kept(2)
        run_halves_join(2)
        run_outward(1)
        run_finish(0)
        run_return(0)
        run_finish(1)
        run_halves_finish(2)
        run_return(1, 2)
    else:
        for c in range(count):
            parts = {d: [] for d in range(n)}
            for distances in (range(1, n, 2), range(0, n, 2)):
                blocks = [found[c]["found"][d] for d in distances]
                mine = run_attend(c, [blocks, blocks], [place ^ d for d in distances])
                for slot, d in enumerate(distances):
                    parts[d].append((mine, slot))
                if 1 in distances:
                    moved = send(mine, *[(i, i ^ 1) for i in range(n)])
            for slot, d in enumerate(range(0, n, 2)):
                parts[d].append((moved, slot))
            for bit in bits[1:]:
                for d in range(bit, n, 2 * bit):
                    joint = run_join(c, [parts[d], parts[d]])
                    parts[d ^ bit].append((send(joint, *[(i, i ^ bit) for i in range(n)]), 0))
            run_back(c, [parts[0], parts[0]])
            run_return(c)

    in_order = [backs[c] for c in sorted(range(count), key=lambda c: PIECES[c][0])]
    together = jnp.concatenate(in_order, axis=2)
    return together.transpose(1, 0, 2).reshape(own_rows, peers * group)


def solution(mesh):
    in_specs = (
        P(("cfg", "blk", "uly"), None),
        P(("cfg", "blk", "uly"), None),
        P(("cfg", "blk", "uly"), None),
        P(("cfg", "blk"), "uly"),
        P(("cfg", "blk"), "uly"),
        P(),
    )
    out_specs = P(("cfg", "blk", "uly"), None)
    return jax.shard_map(shards, mesh=mesh, in_specs=in_specs, out_specs=out_specs, check_vma=False)
```

```python
import functools

import jax
import jax.numpy as jnp
from jax import lax
from jax.experimental import pallas as pl
from jax.experimental.pallas import tpu as pltpu
from jax.sharding import PartitionSpec as P

DH = 128
TILE = 128
PIECES = ((0, 1), (1, 1), (2, 1))
PIECE_UNITS = 3
HALF = 256
CHUNK = 256
LOG2E = 1.4426950408889634
TINY = 1.0e-30
ONES = 16
SCALE2 = DH ** (-0.5) * LOG2E
MASKED = -1.0e30
MIB = 1024 * 1024
QUICK = pl.CostEstimate(flops=1024, bytes_accessed=1024, transcendentals=0)


def split3(x):
    hi = x.astype(jnp.bfloat16).astype(jnp.float32)
    rest = x - hi
    mid = rest.astype(jnp.bfloat16).astype(jnp.float32)
    lo = (rest - mid).astype(jnp.bfloat16).astype(jnp.float32)
    return hi, mid, lo


def stat_rows(width):
    return -(-3 * (width // DH) // 16) * 16


def attend_kernel(choices, table_ref, kept_ref, *refs):
    count = sum(len(c) for c in choices)
    sources, at = [], 0
    for c in choices:
        sources.append(refs[at : at + len(c)])
        at += len(c)
    ck_ref, nk_ref, cv_ref, nv_ref = refs[count : count + 4]
    out_ref, q_s, s0, s1, m0, m1, stat_s = refs[-7:]
    rows = q_s.shape[0]
    width = q_s.shape[1] // 2
    heads = width // DH
    ctx, new = ck_ref.shape[0], nk_ref.shape[0]
    subs = HALF // TILE
    halves = rows // HALF
    slots = ((s0, m0), (s1, m1))
    nt = (((1,), (1,)), ((), ()))
    step_no = pl.program_id(0)
    first_tile = table_ref[1 + step_no] * (rows // TILE)
    stat_s[...] = jnp.zeros_like(stat_s)
    for c, q_refs in enumerate(sources):
        for i, q_ref in enumerate(q_refs):

            @pl.when((step_no == i) & (table_ref[0] == c))
            def _():
                for head in range(heads):
                    scaled = q_ref[:, head * DH : (head + 1) * DH].astype(jnp.float32) * SCALE2
                    hi = scaled.astype(jnp.bfloat16)
                    lo = (scaled - hi.astype(jnp.float32)).astype(jnp.bfloat16)
                    q_s[:, 2 * head * DH : (2 * head + 1) * DH] = hi
                    q_s[:, (2 * head + 1) * DH : (2 * head + 2) * DH] = lo

    def columns(head, size=DH):
        return pl.ds(pl.multiple_of(head * size, size), size)

    chunks = [(k, v, at, base) for k, v, size, base in ((ck_ref, cv_ref, ctx, 0), (nk_ref, nv_ref, new, ctx))
              for at in range(0, size, CHUNK)]

    def kept(half, sub, row):
        return kept_ref[first_tile + half * subs + sub, row // TILE] > 0

    def score(head, half, chunk, q, tops):
        s_ref = slots[half % 2][0]
        k_ref, _, at, base = chunk
        size = min(CHUNK, k_ref.shape[0] - at)
        k = k_ref[at : at + size, columns(head)]
        scores = lax.dot_general(jnp.concatenate([k, k], axis=1), q, nt, preferred_element_type=jnp.float32)
        s_ref[base + at : base + at + size, :] = scores
        for j in range(0, size, TILE):
            for sub in range(subs):
                piece = scores[j : j + TILE, sub * TILE : (sub + 1) * TILE]
                top = jnp.max(piece.reshape(TILE // 8, 8, TILE), axis=0)
                top = jnp.where(kept(half, sub, base + at + j), top, MASKED)
                tops[sub] = top if tops[sub] is None else jnp.maximum(tops[sub], top)

    def weigh(head, half, chunk, high):
        s_ref = slots[half % 2][0]
        _, v_ref, at, base = chunk
        size = min(CHUNK, v_ref.shape[1] - at)
        lows = []
        for j in range(0, size, TILE):
            row = base + at + j
            pieces = []
            for sub in range(subs):
                lanes = slice(sub * TILE, (sub + 1) * TILE)
                less = jnp.where(kept(half, sub, row), high[:, lanes], -MASKED)
                pieces.append(jnp.exp2(s_ref[row : row + TILE, lanes] - less).astype(jnp.bfloat16))
            lows.append(jnp.concatenate(pieces, axis=1))
        low = jnp.concatenate(lows, axis=0)
        values = jnp.concatenate([v_ref[columns(head), at : at + size], jnp.ones((ONES, size), jnp.bfloat16)], axis=0)
        return jnp.dot(values, low, preferred_element_type=jnp.float32)

    def step(head, half, next_head, next_half, both=True):
        q = q_s[next_half * HALF : (next_half + 1) * HALF, columns(next_head, 2 * DH)]
        tops = [None] * subs
        if both:
            high = jnp.max(slots[half % 2][1][...], axis=0, keepdims=True)
            acc = None
        for chunk in chunks:
            score(next_head, next_half, chunk, q, tops)
            if both:
                found = weigh(head, half, chunk, high)
                acc = found if acc is None else acc + found
        for sub in range(subs):
            slots[next_half % 2][1][:, sub * TILE : (sub + 1) * TILE] = tops[sub]
        if both:
            total = jnp.maximum(acc[DH : DH + 1, :], TINY)
            lanes = slice(half * HALF, (half + 1) * HALF)
            out_ref[0, columns(head), lanes] = (acc[:DH, :] * (1.0 / total)).astype(jnp.bfloat16)
            for part, value in enumerate(split3(high + jnp.log2(total))):
                stat_s[pl.ds(3 * head + part, 1), lanes] = value

    step(0, 1, 0, 0, both=False)

    @pl.loop(0, heads)
    def _(head):
        for half in range(halves):
            if half + 1 < halves:
                step(head, half, head, half + 1)
            else:
                step(head, half, jnp.minimum(head + 1, heads - 1), 0)

    out_ref[0, width:, :] = stat_s[...].astype(jnp.bfloat16)


def attend(table, kept, choices, ctx_k, new_k, ctx_v, new_v, piece, dep):
    queries = [q for choice in choices for q in choice]
    rows, width = queries[0].shape
    ctx, new = ctx_k.shape[0], new_k.shape[0]
    heads = width // DH
    keys = ctx + new
    blocks = len(choices[0])
    across = lambda i, t, b: (0, piece)
    down = lambda i, t, b: (piece, 0)
    prow = width + stat_rows(width)
    return pl.pallas_call(
        functools.partial(attend_kernel, [[None] * len(c) for c in choices]),
        out_shape=jax.ShapeDtypeStruct((blocks, prow, rows), jnp.bfloat16),
        grid_spec=pltpu.PrefetchScalarGridSpec(
            num_scalar_prefetch=2,
            grid=(blocks,),
            in_specs=[pl.BlockSpec((rows, width), lambda i, t, b: (0, 0))] * len(queries)
            + [
                pl.BlockSpec((ctx, width), across),
                pl.BlockSpec((new, width), across),
                pl.BlockSpec((width, ctx), down),
                pl.BlockSpec((width, new), down),
                pl.BlockSpec(memory_space=pl.ANY),
            ],
            out_specs=pl.BlockSpec((1, prow, rows), lambda i, t, b: (i, 0, 0)),
            scratch_shapes=[
                pltpu.VMEM((rows, 2 * width), jnp.bfloat16),
                pltpu.VMEM((keys, HALF), jnp.float32),
                pltpu.VMEM((keys, HALF), jnp.float32),
                pltpu.VMEM((8, HALF), jnp.float32),
                pltpu.VMEM((8, HALF), jnp.float32),
                pltpu.VMEM((stat_rows(width), rows), jnp.float32),
            ],
        ),
        compiler_params=pltpu.CompilerParams(vmem_limit_bytes=22 * MIB),
        cost_estimate=pl.CostEstimate(
            flops=8 * blocks * rows * keys * DH * heads,
            bytes_accessed=4 * blocks * rows * width + 4 * keys * width,
            transcendentals=blocks * rows * keys * heads,
        ),
        name="attend",
    )(table, kept, *queries, ctx_k, new_k, ctx_v, new_v, dep)


def combine(refs, width, emit):
    stats = []
    for ref in refs:
        terms = ref[0, width:, :].astype(jnp.float32)
        stats.append([terms[3 * h : 3 * h + 1] + terms[3 * h + 1 : 3 * h + 2] + terms[3 * h + 2 : 3 * h + 3]
                      for h in range(width // DH)])
    for head in range(width // DH):
        logs = [s[head] for s in stats]
        top = functools.reduce(jnp.maximum, logs)
        weights = [jnp.exp2(l - top) for l in logs]
        total = functools.reduce(jnp.add, weights)
        value = None
        for ref, weight in zip(refs, weights):
            part = ref[0, head * DH : (head + 1) * DH, :].astype(jnp.float32) * (weight / total)
            value = part if value is None else value + part
        emit(head, value, top + jnp.log2(total))


def join_kernel_of(sizes, final, table_ref, *refs):
    sources, at = [], 0
    for size in sizes:
        sources.append(refs[at : at + size])
        at += size
    if final:
        out_ref = refs[-1]
        width = out_ref.shape[1]
    else:
        out_ref, stat_ref = refs[-2:]
        width = out_ref.shape[1] - stat_ref.shape[0]

    def emit(head, value, log):
        at = slice(head * DH, (head + 1) * DH)
        if final:
            out_ref[:, at] = jnp.transpose(value).astype(jnp.bfloat16)
            return
        out_ref[0, at, :] = value.astype(jnp.bfloat16)
        for part, term in enumerate(split3(log)):
            stat_ref[3 * head + part : 3 * head + part + 1, :] = term

    for c, chosen in enumerate(sources):
        if chosen:

            @pl.when(table_ref[0] == c)
            def _():
                if not final:
                    stat_ref[...] = jnp.zeros_like(stat_ref)
                combine(chosen, width, emit)
                if not final:
                    out_ref[0, width:, :] = stat_ref[...].astype(jnp.bfloat16)


def join_parts(table, choices, width, dep, final, blocks=1):
    parts = [part for choice in choices for part in choice]
    _, prow, rows = parts[0][0].shape
    specs = [
        pl.BlockSpec((1, prow, rows), functools.partial(lambda slot, i, t: (slot + i, 0, 0), slot)) for _, slot in parts
    ]
    shape = (rows, width) if final else (blocks, prow, rows)
    out_spec = pl.BlockSpec(shape, lambda i, t: (0, 0)) if final else pl.BlockSpec((1, prow, rows), lambda i, t: (i, 0, 0))
    return pl.pallas_call(
        functools.partial(join_kernel_of, [len(c) for c in choices], final),
        out_shape=jax.ShapeDtypeStruct(shape, jnp.bfloat16),
        grid_spec=pltpu.PrefetchScalarGridSpec(
            num_scalar_prefetch=1,
            grid=(blocks,),
            in_specs=specs + [pl.BlockSpec(memory_space=pl.ANY)],
            out_specs=out_spec,
            scratch_shapes=[] if final else [pltpu.VMEM((prow - width, rows), jnp.float32)],
        ),
        compiler_params=pltpu.CompilerParams(vmem_limit_bytes=16 * MIB),
        cost_estimate=QUICK,
        name="finish" if final else "merge",
    )(table, *[array for array, _ in parts], dep)


def part_kernel(peers, count, start, peer_ref, *refs):
    rows = refs[0].shape[0]
    outs = refs[-peers:]
    for i, ref in enumerate(refs[: count * peers]):
        outs[i % peers][i // peers * rows : (i // peers + 1) * rows, :] = ref[:, start:]


def parts_for_peers(peer, arrays, start, peers, deps):
    rows, group = arrays[0].shape[0], arrays[0].shape[1] // peers
    specs = [pl.BlockSpec((rows, group), functools.partial(lambda k, i, t: (0, t[0] ^ k), k)) for k in range(peers)]
    shape = (len(arrays) * rows, group - start)
    return pl.pallas_call(
        functools.partial(part_kernel, peers, len(arrays), start),
        out_shape=[jax.ShapeDtypeStruct(shape, jnp.bfloat16)] * peers,
        grid_spec=pltpu.PrefetchScalarGridSpec(
            num_scalar_prefetch=1,
            grid=(1,),
            in_specs=specs * len(arrays) + [pl.BlockSpec(memory_space=pl.ANY)] * len(deps),
            out_specs=[pl.BlockSpec(shape, lambda i, t: (0, 0))] * peers,
        ),
        compiler_params=pltpu.CompilerParams(vmem_limit_bytes=28 * MIB),
        cost_estimate=QUICK,
        name="parts",
    )(peer.reshape(1), *[a for a in arrays for _ in range(peers)], *deps)


def regroup_kernel(peers, start, peer_ref, *refs):
    out_ref = refs[-1]
    rows, width = refs[0].shape[0], out_ref.shape[1]
    for k in range(peers):
        here = pl.ds(pl.multiple_of((peer_ref[0] ^ k) * rows, rows), rows)
        out_ref[here, :] = refs[k][:, start : start + width]


def regrouped(peer, pieces, start, width, deps):
    peers, rows = len(pieces), pieces[0].shape[0]
    whole = lambda i, t: (0, 0)
    shape = (peers * rows, width)
    return pl.pallas_call(
        functools.partial(regroup_kernel, peers, start),
        out_shape=jax.ShapeDtypeStruct(shape, jnp.bfloat16),
        grid_spec=pltpu.PrefetchScalarGridSpec(
            num_scalar_prefetch=1,
            grid=(1,),
            in_specs=[pl.BlockSpec(p.shape, whole) for p in pieces] + [pl.BlockSpec(memory_space=pl.ANY)] * len(deps),
            out_specs=pl.BlockSpec(shape, whole),
        ),
        compiler_params=pltpu.CompilerParams(vmem_limit_bytes=16 * MIB),
        cost_estimate=QUICK,
        name="regroup",
    )(peer.reshape(1), *pieces, *deps)


def join_kernel(*refs):
    pieces, (k_ref, v_ref, v_s) = refs[:-4], refs[-3:]
    rows = pieces[0].shape[0] // 2
    for i, piece in enumerate(pieces):
        k_ref[i * rows : (i + 1) * rows, :] = piece[:rows, :]
        v_s[i * rows : (i + 1) * rows, :] = piece[rows:, :]
    for at in range(0, v_s.shape[0], TILE):
        v_ref[:, at : at + TILE] = jnp.transpose(v_s[at : at + TILE, :])


def joined(pieces, dep):
    rows, group = pieces[0].shape[0] // 2 * len(pieces), pieces[0].shape[1]
    return pl.pallas_call(
        join_kernel,
        out_shape=[
            jax.ShapeDtypeStruct((rows, group), jnp.bfloat16),
            jax.ShapeDtypeStruct((group, rows), jnp.bfloat16),
        ],
        in_specs=[pl.BlockSpec(memory_space=pltpu.VMEM)] * len(pieces) + [pl.BlockSpec(memory_space=pl.ANY)],
        scratch_shapes=[pltpu.VMEM((rows, group), jnp.bfloat16)],
        compiler_params=pltpu.CompilerParams(vmem_limit_bytes=24 * MIB),
        cost_estimate=QUICK,
        name="join",
    )(*pieces, dep)


def shards(new_queries, new_keys, new_values, context_keys, context_values, keep_flags):
    n = lax.axis_size("blk")
    place = lax.axis_index("blk").astype(jnp.int32)
    peers = lax.axis_size("uly")
    own_rows = new_queries.shape[0]
    group = context_keys.shape[1]
    unit = group // PIECE_UNITS
    span_rows = own_rows * peers
    ctx_tiles, new_tiles = context_keys.shape[0] // TILE, span_rows // TILE

    peer = lax.axis_index("uly").astype(jnp.int32)
    new_order = jnp.arange(new_tiles, dtype=jnp.int32) ^ (peer * own_rows // TILE)
    new_kept = lax.dynamic_slice_in_dim(keep_flags, n * ctx_tiles + place * new_tiles, new_tiles, 1)
    kept = jnp.concatenate(
        [
            lax.dynamic_slice_in_dim(keep_flags, place * ctx_tiles, ctx_tiles, 1),
            jnp.sum(jnp.where(new_order[:, None] == jnp.arange(new_tiles), new_kept[:, None, :], 0), axis=2),
        ],
        axis=1,
    )
    kept = (kept == 1).astype(jnp.int32)
    count = len(PIECES)
    widths = [units * unit for _, units in PIECES]
    backs = [None] * count

    def to_heads(pieces):
        moved = lax.all_to_all(pieces, "uly", split_axis=0, concat_axis=0, tiled=False)
        return moved.reshape(span_rows, pieces.shape[2])

    def to_peers(pieces):
        return [lax.ppermute(p, "uly", [(i, i ^ k) for i in range(peers)]) if k else p for k, p in enumerate(pieces)]

    def send(x, *pairs):
        return lax.ppermute(x, "blk", pairs)

    def spread_line(span):
        near = send(span, (0, 1), (1, 0), (2, 3), (3, 2))
        third = send(span, (1, 2), (2, 1))
        far = send(near, (1, 2), (2, 1))
        third_out = send(third, (1, 0), (2, 3))
        far_out = send(far, (1, 0), (2, 3))
        return dict(own=span, near=near, sent=[[far, third], [far_out, third_out]], early=third, mid=third_out)

    def spread_cube(span):
        found = {0: span}
        for bit in reversed(bits):
            for d in list(found):
                found[d ^ bit] = send(found[d], *[(i, i ^ bit) for i in range(n)])
        return dict(found=found, early=found[n // 2], mid=found[n // 2])

    bits = [1 << k for k in range((n - 1).bit_length())]
    line = n == 4
    spread = spread_line if line else spread_cube
    early = widths[0]
    first_span = to_heads(jnp.stack([new_queries[:, p * group : p * group + early] for p in range(peers)]))
    found = [spread(first_span)]
    parts_q = parts_for_peers(peer, [new_queries], early, peers, [first_span])
    later = to_peers(parts_q)
    context_values_t = context_values.T
    parts_kv = parts_for_peers(
        peer, [new_keys, new_values], 0, peers, [*later, found[0]["early"], context_values_t]
    )

    def run_spread(c, deps):
        span = regrouped(peer, later, PIECES[c][0] * unit - early, widths[c], deps)
        found.append(spread(span))
        return span

    latest = parts_kv[0]
    for c in range(1, count):
        latest = run_spread(c, [found[c - 1]["early"], latest])
    span_k, span_v_t = joined(to_peers(parts_kv), latest)
    last = [span_k]
    outer = ((place == 0) | (place == n - 1)).astype(jnp.int32)
    low = place < n // 2

    def run_attend(c, choices, targets):
        table = jnp.stack([outer, *targets]).astype(jnp.int32)
        own = attend(
            table, kept, choices, context_keys, span_k, context_values_t, span_v_t, PIECES[c][0] // PIECES[c][1], last[0]
        )
        last[0] = own
        return own

    def run_join(c, choices, final=False, blocks=1):
        last[0] = join_parts(outer.reshape(1), choices, widths[c], last[0], final, blocks)
        return last[0]

    def run_back(c, choices):
        backs[c] = run_join(c, choices, True).reshape(peers, own_rows, widths[c])

    def run_return(*those):
        joint = jnp.concatenate([backs[c] for c in those], axis=2)
        joint = lax.all_to_all(joint, "uly", split_axis=0, concat_axis=0, tiled=False)
        at = 0
        for c in those:
            backs[c] = joint[:, :, at : at + widths[c]]
            at += widths[c]

    state = [dict() for _ in range(count)]

    def run_sent(c):
        mine = run_attend(c, found[c]["sent"], [jnp.where(low, 3, 0), jnp.where(low, 2, 1)])
        state[c].update(far=mine, edge=send(mine, (0, 1), (3, 2)))

    def run_kept(c):
        blocks = [found[c]["near"], found[c]["own"]]
        mine = run_attend(c, [blocks, blocks], [place ^ 1, place])
        state[c].update(kept=mine, edge_near=send(mine[:1], (0, 1), (3, 2)))

    def run_cross(c):
        joint = run_join(c, [[(state[c]["far"], 0), (state[c]["edge"], 0)], []], blocks=2)
        state[c]["cross"] = send(joint, (1, 2), (2, 1))

    def run_outward(c):
        joint = run_join(c, [[(state[c]["kept"], 0), (state[c]["cross"], 0)], []])
        state[c]["outward"] = send(joint, (1, 0), (2, 3))

    def run_finish(c):
        inner = [(state[c]["kept"], 1), (state[c]["edge_near"], 0), (state[c]["cross"], 1)]
        run_back(c, [inner, [(state[c]["kept"], 1), (state[c]["outward"], 0)]])

    def run_halves(c):
        inner, outer_ones = found[c]["sent"]
        near, own = found[c]["near"], found[c]["own"]
        mine = run_attend(c, [[near, inner[1]], [near, outer_ones[0]]], [place ^ 1, place ^ 3])
        state[c].update(swap=send(mine, (0, 1), (1, 0), (2, 3), (3, 2)), rest=[[own, inner[0]], [own, outer_ones[1]]])

    def run_halves_kept(c):
        state[c]["kept"] = run_attend(c, state[c]["rest"], [place, place ^ 2])

    def run_halves_join(c):
        pair = [(state[c]["kept"], 1), (state[c]["swap"], 1)]
        state[c]["across"] = send(run_join(c, [pair, pair]), (0, 2), (2, 0), (1, 3), (3, 1))

    def run_halves_finish(c):
        three = [(state[c]["kept"], 0), (state[c]["swap"], 0), (state[c]["across"], 0)]
        run_back(c, [three, three])

    if line:
        run_sent(0)
        run_kept(0)
        run_sent(1)
        run_cross(0)
        run_kept(1)
        run_halves(2)
        run_outward(0)
        run_cross(1)
        run_halves_kept(2)
        run_halves_join(2)
        run_outward(1)
        run_finish(0)
        run_return(0)
        run_finish(1)
        run_halves_finish(2)
        run_return(1, 2)
    else:
        for c in range(count):
            parts = {d: [] for d in range(n)}
            for distances in (range(1, n, 2), range(0, n, 2)):
                blocks = [found[c]["found"][d] for d in distances]
                mine = run_attend(c, [blocks, blocks], [place ^ d for d in distances])
                for slot, d in enumerate(distances):
                    parts[d].append((mine, slot))
                if 1 in distances:
                    moved = send(mine, *[(i, i ^ 1) for i in range(n)])
            for slot, d in enumerate(range(0, n, 2)):
                parts[d].append((moved, slot))
            for bit in bits[1:]:
                for d in range(bit, n, 2 * bit):
                    joint = run_join(c, [parts[d], parts[d]])
                    parts[d ^ bit].append((send(joint, *[(i, i ^ bit) for i in range(n)]), 0))
            run_back(c, [parts[0], parts[0]])
            run_return(c)

    in_order = [backs[c] for c in sorted(range(count), key=lambda c: PIECES[c][0])]
    together = jnp.concatenate(in_order, axis=2)
    return together.transpose(1, 0, 2).reshape(own_rows, peers * group)


def solution(mesh):
    in_specs = (
        P(("cfg", "blk", "uly"), None),
        P(("cfg", "blk", "uly"), None),
        P(("cfg", "blk", "uly"), None),
        P(("cfg", "blk"), "uly"),
        P(("cfg", "blk"), "uly"),
        P(),
    )
    out_specs = P(("cfg", "blk", "uly"), None)
    return jax.shard_map(shards, mesh=mesh, in_specs=in_specs, out_specs=out_specs, check_vma=False)
```

```python
import functools

import jax
import jax.numpy as jnp
from jax import lax
from jax.experimental import pallas as pl
from jax.experimental.pallas import tpu as pltpu
from jax.sharding import PartitionSpec as P

DH = 128
TILE = 128
PIECES = ((0, 1), (1, 1), (2, 1))
PIECE_UNITS = 3
HALF = 256
CHUNK = 256
LOG2E = 1.4426950408889634
TINY = 1.0e-30
ONES = 16
SCALE2 = DH ** (-0.5) * LOG2E
MASKED = -1.0e30
MIB = 1024 * 1024
QUICK = pl.CostEstimate(flops=1024, bytes_accessed=1024, transcendentals=0)


def split3(x):
    hi = x.astype(jnp.bfloat16).astype(jnp.float32)
    rest = x - hi
    mid = rest.astype(jnp.bfloat16).astype(jnp.float32)
    lo = (rest - mid).astype(jnp.bfloat16).astype(jnp.float32)
    return hi, mid, lo


def stat_rows(width):
    return -(-3 * (width // DH) // 16) * 16


def attend_kernel(choices, table_ref, kept_ref, *refs):
    count = sum(len(c) for c in choices)
    sources, at = [], 0
    for c in choices:
        sources.append(refs[at : at + len(c)])
        at += len(c)
    ck_ref, nk_ref, cv_ref, nv_ref = refs[count : count + 4]
    out_ref, q_s, s0, s1, m0, m1, stat_s = refs[-7:]
    rows = q_s.shape[0]
    width = q_s.shape[1] // 2
    heads = width // DH
    ctx, new = ck_ref.shape[0], nk_ref.shape[0]
    subs = HALF // TILE
    halves = rows // HALF
    slots = ((s0, m0), (s1, m1))
    nt = (((1,), (1,)), ((), ()))
    step_no = pl.program_id(0)
    first_tile = table_ref[1 + step_no] * (rows // TILE)
    stat_s[...] = jnp.zeros_like(stat_s)
    for c, q_refs in enumerate(sources):
        for i, q_ref in enumerate(q_refs):

            @pl.when((step_no == i) & (table_ref[0] == c))
            def _():
                for head in range(heads):
                    scaled = q_ref[:, head * DH : (head + 1) * DH].astype(jnp.float32) * SCALE2
                    hi = scaled.astype(jnp.bfloat16)
                    lo = (scaled - hi.astype(jnp.float32)).astype(jnp.bfloat16)
                    q_s[:, 2 * head * DH : (2 * head + 1) * DH] = hi
                    q_s[:, (2 * head + 1) * DH : (2 * head + 2) * DH] = lo

    def columns(head, size=DH):
        return pl.ds(pl.multiple_of(head * size, size), size)

    chunks = [(k, v, at, base) for k, v, size, base in ((ck_ref, cv_ref, ctx, 0), (nk_ref, nv_ref, new, ctx))
              for at in range(0, size, CHUNK)]

    def kept(half, sub, row):
        return kept_ref[first_tile + half * subs + sub, row // TILE] > 0

    def score(head, half, chunk, q, tops):
        s_ref = slots[half % 2][0]
        k_ref, _, at, base = chunk
        size = min(CHUNK, k_ref.shape[0] - at)
        k = k_ref[at : at + size, columns(head)]
        scores = lax.dot_general(jnp.concatenate([k, k], axis=1), q, nt, preferred_element_type=jnp.float32)
        s_ref[base + at : base + at + size, :] = scores
        for j in range(0, size, TILE):
            for sub in range(subs):
                piece = scores[j : j + TILE, sub * TILE : (sub + 1) * TILE]
                top = jnp.max(piece.reshape(TILE // 8, 8, TILE), axis=0)
                top = jnp.where(kept(half, sub, base + at + j), top, MASKED)
                tops[sub] = top if tops[sub] is None else jnp.maximum(tops[sub], top)

    def weigh(head, half, chunk, high):
        s_ref = slots[half % 2][0]
        _, v_ref, at, base = chunk
        size = min(CHUNK, v_ref.shape[1] - at)
        lows = []
        for j in range(0, size, TILE):
            row = base + at + j
            pieces = []
            for sub in range(subs):
                lanes = slice(sub * TILE, (sub + 1) * TILE)
                less = jnp.where(kept(half, sub, row), high[:, lanes], -MASKED)
                pieces.append(jnp.exp2(s_ref[row : row + TILE, lanes] - less).astype(jnp.bfloat16))
            lows.append(jnp.concatenate(pieces, axis=1))
        low = jnp.concatenate(lows, axis=0)
        values = jnp.concatenate([v_ref[columns(head), at : at + size], jnp.ones((ONES, size), jnp.bfloat16)], axis=0)
        return jnp.dot(values, low, preferred_element_type=jnp.float32)

    def step(head, half, next_head, next_half, both=True):
        q = q_s[next_half * HALF : (next_half + 1) * HALF, columns(next_head, 2 * DH)]
        tops = [None] * subs
        if both:
            high = jnp.max(slots[half % 2][1][...], axis=0, keepdims=True)
            acc = None
        for chunk in chunks:
            score(next_head, next_half, chunk, q, tops)
            if both:
                found = weigh(head, half, chunk, high)
                acc = found if acc is None else acc + found
        for sub in range(subs):
            slots[next_half % 2][1][:, sub * TILE : (sub + 1) * TILE] = tops[sub]
        if both:
            total = jnp.maximum(acc[DH : DH + 1, :], TINY)
            lanes = slice(half * HALF, (half + 1) * HALF)
            out_ref[0, columns(head), lanes] = (acc[:DH, :] * (1.0 / total)).astype(jnp.bfloat16)
            for part, value in enumerate(split3(high + jnp.log2(total))):
                stat_s[pl.ds(3 * head + part, 1), lanes] = value

    step(0, 1, 0, 0, both=False)

    @pl.loop(0, heads)
    def _(head):
        for half in range(halves):
            if half + 1 < halves:
                step(head, half, head, half + 1)
            else:
                step(head, half, jnp.minimum(head + 1, heads - 1), 0)

    out_ref[0, width:, :] = stat_s[...].astype(jnp.bfloat16)


def attend(table, kept, choices, ctx_k, new_k, ctx_v, new_v, piece, dep):
    queries = [q for choice in choices for q in choice]
    rows, width = queries[0].shape
    ctx, new = ctx_k.shape[0], new_k.shape[0]
    heads = width // DH
    keys = ctx + new
    blocks = len(choices[0])
    across = lambda i, t, b: (0, piece)
    down = lambda i, t, b: (piece, 0)
    prow = width + stat_rows(width)
    return pl.pallas_call(
        functools.partial(attend_kernel, [[None] * len(c) for c in choices]),
        out_shape=jax.ShapeDtypeStruct((blocks, prow, rows), jnp.bfloat16),
        grid_spec=pltpu.PrefetchScalarGridSpec(
            num_scalar_prefetch=2,
            grid=(blocks,),
            in_specs=[pl.BlockSpec((rows, width), lambda i, t, b: (0, 0))] * len(queries)
            + [
                pl.BlockSpec((ctx, width), across),
                pl.BlockSpec((new, width), across),
                pl.BlockSpec((width, ctx), down),
                pl.BlockSpec((width, new), down),
                pl.BlockSpec(memory_space=pl.ANY),
            ],
            out_specs=pl.BlockSpec((1, prow, rows), lambda i, t, b: (i, 0, 0)),
            scratch_shapes=[
                pltpu.VMEM((rows, 2 * width), jnp.bfloat16),
                pltpu.VMEM((keys, HALF), jnp.float32),
                pltpu.VMEM((keys, HALF), jnp.float32),
                pltpu.VMEM((8, HALF), jnp.float32),
                pltpu.VMEM((8, HALF), jnp.float32),
                pltpu.VMEM((stat_rows(width), rows), jnp.float32),
            ],
        ),
        compiler_params=pltpu.CompilerParams(vmem_limit_bytes=22 * MIB),
        cost_estimate=pl.CostEstimate(
            flops=8 * blocks * rows * keys * DH * heads,
            bytes_accessed=4 * blocks * rows * width + 4 * keys * width,
            transcendentals=blocks * rows * keys * heads,
        ),
        name="attend",
    )(table, kept, *queries, ctx_k, new_k, ctx_v, new_v, dep)


def combine(refs, width, emit):
    stats = []
    for ref in refs:
        terms = ref[0, width:, :].astype(jnp.float32)
        stats.append([terms[3 * h : 3 * h + 1] + terms[3 * h + 1 : 3 * h + 2] + terms[3 * h + 2 : 3 * h + 3]
                      for h in range(width // DH)])
    for head in range(width // DH):
        logs = [s[head] for s in stats]
        top = functools.reduce(jnp.maximum, logs)
        weights = [jnp.exp2(l - top) for l in logs]
        total = functools.reduce(jnp.add, weights)
        value = None
        for ref, weight in zip(refs, weights):
            part = ref[0, head * DH : (head + 1) * DH, :].astype(jnp.float32) * (weight / total)
            value = part if value is None else value + part
        emit(head, value, top + jnp.log2(total))


def join_kernel_of(sizes, final, table_ref, *refs):
    sources, at = [], 0
    for size in sizes:
        sources.append(refs[at : at + size])
        at += size
    if final:
        out_ref = refs[-1]
        width = out_ref.shape[1]
    else:
        out_ref, stat_ref = refs[-2:]
        width = out_ref.shape[1] - stat_ref.shape[0]

    def emit(head, value, log):
        at = slice(head * DH, (head + 1) * DH)
        if final:
            out_ref[:, at] = jnp.transpose(value).astype(jnp.bfloat16)
            return
        out_ref[0, at, :] = value.astype(jnp.bfloat16)
        for part, term in enumerate(split3(log)):
            stat_ref[3 * head + part : 3 * head + part + 1, :] = term

    for c, chosen in enumerate(sources):
        if chosen:

            @pl.when(table_ref[0] == c)
            def _():
                if not final:
                    stat_ref[...] = jnp.zeros_like(stat_ref)
                combine(chosen, width, emit)
                if not final:
                    out_ref[0, width:, :] = stat_ref[...].astype(jnp.bfloat16)


def join_parts(table, choices, width, dep, final, blocks=1):
    parts = [part for choice in choices for part in choice]
    _, prow, rows = parts[0][0].shape
    specs = [
        pl.BlockSpec((1, prow, rows), functools.partial(lambda slot, i, t: (slot + i, 0, 0), slot)) for _, slot in parts
    ]
    shape = (rows, width) if final else (blocks, prow, rows)
    out_spec = pl.BlockSpec(shape, lambda i, t: (0, 0)) if final else pl.BlockSpec((1, prow, rows), lambda i, t: (i, 0, 0))
    return pl.pallas_call(
        functools.partial(join_kernel_of, [len(c) for c in choices], final),
        out_shape=jax.ShapeDtypeStruct(shape, jnp.bfloat16),
        grid_spec=pltpu.PrefetchScalarGridSpec(
            num_scalar_prefetch=1,
            grid=(blocks,),
            in_specs=specs + [pl.BlockSpec(memory_space=pl.ANY)],
            out_specs=out_spec,
            scratch_shapes=[] if final else [pltpu.VMEM((prow - width, rows), jnp.float32)],
        ),
        compiler_params=pltpu.CompilerParams(vmem_limit_bytes=16 * MIB),
        cost_estimate=QUICK,
        name="finish" if final else "merge",
    )(table, *[array for array, _ in parts], dep)


def part_kernel(peers, count, start, peer_ref, *refs):
    rows = refs[0].shape[0]
    outs = refs[-peers:]
    for i, ref in enumerate(refs[: count * peers]):
        outs[i % peers][i // peers * rows : (i // peers + 1) * rows, :] = ref[:, start:]


def parts_for_peers(peer, arrays, start, peers, deps):
    rows, group = arrays[0].shape[0], arrays[0].shape[1] // peers
    specs = [pl.BlockSpec((rows, group), functools.partial(lambda k, i, t: (0, t[0] ^ k), k)) for k in range(peers)]
    shape = (len(arrays) * rows, group - start)
    return pl.pallas_call(
        functools.partial(part_kernel, peers, len(arrays), start),
        out_shape=[jax.ShapeDtypeStruct(shape, jnp.bfloat16)] * peers,
        grid_spec=pltpu.PrefetchScalarGridSpec(
            num_scalar_prefetch=1,
            grid=(1,),
            in_specs=specs * len(arrays) + [pl.BlockSpec(memory_space=pl.ANY)] * len(deps),
            out_specs=[pl.BlockSpec(shape, lambda i, t: (0, 0))] * peers,
        ),
        compiler_params=pltpu.CompilerParams(vmem_limit_bytes=28 * MIB),
        cost_estimate=QUICK,
        name="parts",
    )(peer.reshape(1), *[a for a in arrays for _ in range(peers)], *deps)


def regroup_kernel(peers, start, peer_ref, *refs):
    out_ref = refs[-1]
    rows, width = refs[0].shape[0], out_ref.shape[1]
    for k in range(peers):
        here = pl.ds(pl.multiple_of((peer_ref[0] ^ k) * rows, rows), rows)
        out_ref[here, :] = refs[k][:, start : start + width]


def regrouped(peer, pieces, start, width, deps):
    peers, rows = len(pieces), pieces[0].shape[0]
    whole = lambda i, t: (0, 0)
    shape = (peers * rows, width)
    return pl.pallas_call(
        functools.partial(regroup_kernel, peers, start),
        out_shape=jax.ShapeDtypeStruct(shape, jnp.bfloat16),
        grid_spec=pltpu.PrefetchScalarGridSpec(
            num_scalar_prefetch=1,
            grid=(1,),
            in_specs=[pl.BlockSpec(p.shape, whole) for p in pieces] + [pl.BlockSpec(memory_space=pl.ANY)] * len(deps),
            out_specs=pl.BlockSpec(shape, whole),
        ),
        compiler_params=pltpu.CompilerParams(vmem_limit_bytes=16 * MIB),
        cost_estimate=QUICK,
        name="regroup",
    )(peer.reshape(1), *pieces, *deps)


def join_kernel(*refs):
    pieces, (k_ref, v_ref, v_s) = refs[:-4], refs[-3:]
    rows = pieces[0].shape[0] // 2
    for i, piece in enumerate(pieces):
        k_ref[i * rows : (i + 1) * rows, :] = piece[:rows, :]
        v_s[i * rows : (i + 1) * rows, :] = piece[rows:, :]
    for at in range(0, v_s.shape[0], TILE):
        v_ref[:, at : at + TILE] = jnp.transpose(v_s[at : at + TILE, :])


def joined(pieces, dep):
    rows, group = pieces[0].shape[0] // 2 * len(pieces), pieces[0].shape[1]
    return pl.pallas_call(
        join_kernel,
        out_shape=[
            jax.ShapeDtypeStruct((rows, group), jnp.bfloat16),
            jax.ShapeDtypeStruct((group, rows), jnp.bfloat16),
        ],
        in_specs=[pl.BlockSpec(memory_space=pltpu.VMEM)] * len(pieces) + [pl.BlockSpec(memory_space=pl.ANY)],
        scratch_shapes=[pltpu.VMEM((rows, group), jnp.bfloat16)],
        compiler_params=pltpu.CompilerParams(vmem_limit_bytes=24 * MIB),
        cost_estimate=QUICK,
        name="join",
    )(*pieces, dep)


def shards(new_queries, new_keys, new_values, context_keys, context_values, keep_flags):
    n = lax.axis_size("blk")
    place = lax.axis_index("blk").astype(jnp.int32)
    peers = lax.axis_size("uly")
    own_rows = new_queries.shape[0]
    group = context_keys.shape[1]
    unit = group // PIECE_UNITS
    span_rows = own_rows * peers
    ctx_tiles, new_tiles = context_keys.shape[0] // TILE, span_rows // TILE

    peer = lax.axis_index("uly").astype(jnp.int32)
    new_order = jnp.arange(new_tiles, dtype=jnp.int32) ^ (peer * own_rows // TILE)
    new_kept = lax.dynamic_slice_in_dim(keep_flags, n * ctx_tiles + place * new_tiles, new_tiles, 1)
    kept = jnp.concatenate(
        [
            lax.dynamic_slice_in_dim(keep_flags, place * ctx_tiles, ctx_tiles, 1),
            jnp.sum(jnp.where(new_order[:, None] == jnp.arange(new_tiles), new_kept[:, None, :], 0), axis=2),
        ],
        axis=1,
    )
    kept = (kept == 1).astype(jnp.int32)
    count = len(PIECES)
    widths = [units * unit for _, units in PIECES]
    backs = [None] * count

    def to_heads(pieces):
        moved = lax.all_to_all(pieces, "uly", split_axis=0, concat_axis=0, tiled=False)
        return moved.reshape(span_rows, pieces.shape[2])

    def to_peers(pieces):
        got = {0: pieces[0]}
        for k in reversed(range(1, peers)):
            got[k] = lax.ppermute(pieces[k], "uly", [(i, i ^ k) for i in range(peers)])
        return [got[k] for k in range(peers)]

    def send(x, *pairs):
        return lax.ppermute(x, "blk", pairs)

    def spread_line(span):
        near = send(span, (0, 1), (1, 0), (2, 3), (3, 2))
        third = send(span, (1, 2), (2, 1))
        far = send(near, (1, 2), (2, 1))
        third_out = send(third, (1, 0), (2, 3))
        far_out = send(far, (1, 0), (2, 3))
        return dict(own=span, near=near, sent=[[far, third], [far_out, third_out]], early=third, after=near)

    def spread_cube(span):
        found = {0: span}
        for bit in reversed(bits):
            for d in list(found):
                found[d ^ bit] = send(found[d], *[(i, i ^ bit) for i in range(n)])
        return dict(found=found, early=found[n // 2], after=found[n // 2])

    bits = [1 << k for k in range((n - 1).bit_length())]
    line = n == 4
    spread = spread_line if line else spread_cube
    early = widths[0]
    first_span = to_heads(jnp.stack([new_queries[:, p * group : p * group + early] for p in range(peers)]))
    found = [spread(first_span)]
    parts_q = parts_for_peers(peer, [new_queries], early, peers, [first_span])
    later = to_peers(parts_q)
    parts_kv = parts_for_peers(peer, [new_keys, new_values], 0, peers, [*later, found[0]["early"]])

    def run_spread(c, deps):
        span = regrouped(peer, later, PIECES[c][0] * unit - early, widths[c], deps)
        found.append(spread(span))
        return span

    latest = parts_kv[0]
    for c in range(1, count):
        latest = run_spread(c, [found[c - 1]["after"], latest])
    span_k, span_v_t = joined(to_peers(parts_kv), latest)
    context_values_t = context_values.T
    last = [span_k]
    outer = ((place == 0) | (place == n - 1)).astype(jnp.int32)
    low = place < n // 2

    def run_attend(c, choices, targets):
        table = jnp.stack([outer, *targets]).astype(jnp.int32)
        own = attend(
            table, kept, choices, context_keys, span_k, context_values_t, span_v_t, PIECES[c][0] // PIECES[c][1], last[0]
        )
        last[0] = own
        return own

    def run_join(c, choices, final=False, blocks=1):
        last[0] = join_parts(outer.reshape(1), choices, widths[c], last[0], final, blocks)
        return last[0]

    def run_back(c, choices):
        backs[c] = run_join(c, choices, True).reshape(peers, own_rows, widths[c])

    def run_return(*those):
        joint = jnp.concatenate([backs[c] for c in those], axis=2)
        joint = lax.all_to_all(joint, "uly", split_axis=0, concat_axis=0, tiled=False)
        at = 0
        for c in those:
            backs[c] = joint[:, :, at : at + widths[c]]
            at += widths[c]

    state = [dict() for _ in range(count)]

    def run_sent(c):
        mine = run_attend(c, found[c]["sent"], [jnp.where(low, 3, 0), jnp.where(low, 2, 1)])
        state[c].update(far=mine, edge=send(mine, (0, 1), (3, 2)))

    def run_kept(c):
        blocks = [found[c]["near"], found[c]["own"]]
        mine = run_attend(c, [blocks, blocks], [place ^ 1, place])
        state[c].update(kept=mine, edge_near=send(mine[:1], (0, 1), (3, 2)))

    def run_cross(c):
        joint = run_join(c, [[(state[c]["far"], 0), (state[c]["edge"], 0)], []], blocks=2)
        state[c]["cross"] = send(joint, (1, 2), (2, 1))

    def run_outward(c):
        joint = run_join(c, [[(state[c]["kept"], 0), (state[c]["cross"], 0)], []])
        state[c]["outward"] = send(joint, (1, 0), (2, 3))

    def run_finish(c):
        inner = [(state[c]["kept"], 1), (state[c]["edge_near"], 0), (state[c]["cross"], 1)]
        run_back(c, [inner, [(state[c]["kept"], 1), (state[c]["outward"], 0)]])

    def run_halves(c):
        inner, outer_ones = found[c]["sent"]
        near, own = found[c]["near"], found[c]["own"]
        mine = run_attend(c, [[near, inner[1]], [near, outer_ones[0]]], [place ^ 1, place ^ 3])
        state[c].update(swap=send(mine, (0, 1), (1, 0), (2, 3), (3, 2)), rest=[[own, inner[0]], [own, outer_ones[1]]])

    def run_halves_kept(c):
        state[c]["kept"] = run_attend(c, state[c]["rest"], [place, place ^ 2])

    def run_halves_join(c):
        pair = [(state[c]["kept"], 1), (state[c]["swap"], 1)]
        state[c]["across"] = send(run_join(c, [pair, pair]), (0, 2), (2, 0), (1, 3), (3, 1))

    def run_halves_finish(c):
        three = [(state[c]["kept"], 0), (state[c]["swap"], 0), (state[c]["across"], 0)]
        run_back(c, [three, three])

    if line:
        run_sent(0)
        run_kept(0)
        run_sent(1)
        run_cross(0)
        run_kept(1)
        run_halves(2)
        run_outward(0)
        run_cross(1)
        run_halves_kept(2)
        run_halves_join(2)
        run_outward(1)
        run_finish(0)
        run_return(0)
        run_finish(1)
        run_halves_finish(2)
        run_return(1, 2)
    else:
        for c in range(count):
            parts = {d: [] for d in range(n)}
            for distances in (range(1, n, 2), range(0, n, 2)):
                blocks = [found[c]["found"][d] for d in distances]
                mine = run_attend(c, [blocks, blocks], [place ^ d for d in distances])
                for slot, d in enumerate(distances):
                    parts[d].append((mine, slot))
                if 1 in distances:
                    moved = send(mine, *[(i, i ^ 1) for i in range(n)])
            for slot, d in enumerate(range(0, n, 2)):
                parts[d].append((moved, slot))
            for bit in bits[1:]:
                for d in range(bit, n, 2 * bit):
                    joint = run_join(c, [parts[d], parts[d]])
                    parts[d ^ bit].append((send(joint, *[(i, i ^ bit) for i in range(n)]), 0))
            run_back(c, [parts[0], parts[0]])
            run_return(c)

    in_order = [backs[c] for c in sorted(range(count), key=lambda c: PIECES[c][0])]
    together = jnp.concatenate(in_order, axis=2)
    return together.transpose(1, 0, 2).reshape(own_rows, peers * group)


def solution(mesh):
    in_specs = (
        P(("cfg", "blk", "uly"), None),
        P(("cfg", "blk", "uly"), None),
        P(("cfg", "blk", "uly"), None),
        P(("cfg", "blk"), "uly"),
        P(("cfg", "blk"), "uly"),
        P(),
    )
    out_specs = P(("cfg", "blk", "uly"), None)
    return jax.shard_map(shards, mesh=mesh, in_specs=in_specs, out_specs=out_specs, check_vma=False)
```

```python
import functools

import jax
import jax.numpy as jnp
from jax import lax
from jax.experimental import pallas as pl
from jax.experimental.pallas import tpu as pltpu
from jax.sharding import PartitionSpec as P

DH = 128
TILE = 128
PIECES = ((0, 1), (1, 1), (2, 1))
PIECE_UNITS = 3
HALF = 256
CHUNK = 256
LOG2E = 1.4426950408889634
TINY = 1.0e-30
ONES = 16
SCALE2 = DH ** (-0.5) * LOG2E
MASKED = -1.0e30
MIB = 1024 * 1024
QUICK = pl.CostEstimate(flops=1024, bytes_accessed=1024, transcendentals=0)


def split3(x):
    hi = x.astype(jnp.bfloat16).astype(jnp.float32)
    rest = x - hi
    mid = rest.astype(jnp.bfloat16).astype(jnp.float32)
    lo = (rest - mid).astype(jnp.bfloat16).astype(jnp.float32)
    return hi, mid, lo


def stat_rows(width):
    return -(-3 * (width // DH) // 16) * 16


def attend_kernel(choices, table_ref, kept_ref, *refs):
    count = sum(len(c) for c in choices)
    sources, at = [], 0
    for c in choices:
        sources.append(refs[at : at + len(c)])
        at += len(c)
    ck_ref, nk_ref, cv_ref, nv_ref = refs[count : count + 4]
    out_ref, q_s, s0, s1, m0, m1, stat_s = refs[-7:]
    rows = q_s.shape[0]
    width = q_s.shape[1] // 2
    heads = width // DH
    ctx, new = ck_ref.shape[0], nk_ref.shape[0]
    subs = HALF // TILE
    halves = rows // HALF
    slots = ((s0, m0), (s1, m1))
    nt = (((1,), (1,)), ((), ()))
    step_no = pl.program_id(0)
    first_tile = table_ref[1 + step_no] * (rows // TILE)
    stat_s[...] = jnp.zeros_like(stat_s)
    for c, q_refs in enumerate(sources):
        for i, q_ref in enumerate(q_refs):

            @pl.when((step_no == i) & (table_ref[0] == c))
            def _():
                for head in range(heads):
                    scaled = q_ref[:, head * DH : (head + 1) * DH].astype(jnp.float32) * SCALE2
                    hi = scaled.astype(jnp.bfloat16)
                    lo = (scaled - hi.astype(jnp.float32)).astype(jnp.bfloat16)
                    q_s[:, 2 * head * DH : (2 * head + 1) * DH] = hi
                    q_s[:, (2 * head + 1) * DH : (2 * head + 2) * DH] = lo

    def columns(head, size=DH):
        return pl.ds(pl.multiple_of(head * size, size), size)

    chunks = [(k, v, at, base) for k, v, size, base in ((ck_ref, cv_ref, ctx, 0), (nk_ref, nv_ref, new, ctx))
              for at in range(0, size, CHUNK)]

    def kept(half, sub, row):
        return kept_ref[first_tile + half * subs + sub, row // TILE] > 0

    def score(head, half, chunk, q, tops):
        s_ref = slots[half % 2][0]
        k_ref, _, at, base = chunk
        size = min(CHUNK, k_ref.shape[0] - at)
        k = k_ref[at : at + size, columns(head)]
        scores = lax.dot_general(jnp.concatenate([k, k], axis=1), q, nt, preferred_element_type=jnp.float32)
        s_ref[base + at : base + at + size, :] = scores
        for j in range(0, size, TILE):
            for sub in range(subs):
                piece = scores[j : j + TILE, sub * TILE : (sub + 1) * TILE]
                top = jnp.max(piece.reshape(TILE // 8, 8, TILE), axis=0)
                top = jnp.where(kept(half, sub, base + at + j), top, MASKED)
                tops[sub] = top if tops[sub] is None else jnp.maximum(tops[sub], top)

    def weigh(head, half, chunk, high):
        s_ref = slots[half % 2][0]
        _, v_ref, at, base = chunk
        size = min(CHUNK, v_ref.shape[1] - at)
        lows = []
        for j in range(0, size, TILE):
            row = base + at + j
            pieces = []
            for sub in range(subs):
                lanes = slice(sub * TILE, (sub + 1) * TILE)
                less = jnp.where(kept(half, sub, row), high[:, lanes], -MASKED)
                pieces.append(jnp.exp2(s_ref[row : row + TILE, lanes] - less).astype(jnp.bfloat16))
            lows.append(jnp.concatenate(pieces, axis=1))
        low = jnp.concatenate(lows, axis=0)
        values = jnp.concatenate([v_ref[columns(head), at : at + size], jnp.ones((ONES, size), jnp.bfloat16)], axis=0)
        return jnp.dot(values, low, preferred_element_type=jnp.float32)

    def step(head, half, next_head, next_half, both=True):
        q = q_s[next_half * HALF : (next_half + 1) * HALF, columns(next_head, 2 * DH)]
        tops = [None] * subs
        if both:
            high = jnp.max(slots[half % 2][1][...], axis=0, keepdims=True)
            acc = None
        for chunk in chunks:
            score(next_head, next_half, chunk, q, tops)
            if both:
                found = weigh(head, half, chunk, high)
                acc = found if acc is None else acc + found
        for sub in range(subs):
            slots[next_half % 2][1][:, sub * TILE : (sub + 1) * TILE] = tops[sub]
        if both:
            total = jnp.maximum(acc[DH : DH + 1, :], TINY)
            lanes = slice(half * HALF, (half + 1) * HALF)
            out_ref[0, columns(head), lanes] = (acc[:DH, :] * (1.0 / total)).astype(jnp.bfloat16)
            for part, value in enumerate(split3(high + jnp.log2(total))):
                stat_s[pl.ds(3 * head + part, 1), lanes] = value

    step(0, 1, 0, 0, both=False)

    @pl.loop(0, heads)
    def _(head):
        for half in range(halves):
            if half + 1 < halves:
                step(head, half, head, half + 1)
            else:
                step(head, half, jnp.minimum(head + 1, heads - 1), 0)

    out_ref[0, width:, :] = stat_s[...].astype(jnp.bfloat16)


def attend(table, kept, choices, ctx_k, new_k, ctx_v, new_v, piece, dep):
    queries = [q for choice in choices for q in choice]
    rows, width = queries[0].shape
    ctx, new = ctx_k.shape[0], new_k.shape[0]
    heads = width // DH
    keys = ctx + new
    blocks = len(choices[0])
    across = lambda i, t, b: (0, piece)
    down = lambda i, t, b: (piece, 0)
    prow = width + stat_rows(width)
    return pl.pallas_call(
        functools.partial(attend_kernel, [[None] * len(c) for c in choices]),
        out_shape=jax.ShapeDtypeStruct((blocks, prow, rows), jnp.bfloat16),
        grid_spec=pltpu.PrefetchScalarGridSpec(
            num_scalar_prefetch=2,
            grid=(blocks,),
            in_specs=[pl.BlockSpec((rows, width), lambda i, t, b: (0, 0))] * len(queries)
            + [
                pl.BlockSpec((ctx, width), across),
                pl.BlockSpec((new, width), across),
                pl.BlockSpec((width, ctx), down),
                pl.BlockSpec((width, new), down),
                pl.BlockSpec(memory_space=pl.ANY),
            ],
            out_specs=pl.BlockSpec((1, prow, rows), lambda i, t, b: (i, 0, 0)),
            scratch_shapes=[
                pltpu.VMEM((rows, 2 * width), jnp.bfloat16),
                pltpu.VMEM((keys, HALF), jnp.float32),
                pltpu.VMEM((keys, HALF), jnp.float32),
                pltpu.VMEM((8, HALF), jnp.float32),
                pltpu.VMEM((8, HALF), jnp.float32),
                pltpu.VMEM((stat_rows(width), rows), jnp.float32),
            ],
        ),
        compiler_params=pltpu.CompilerParams(vmem_limit_bytes=28 * MIB),
        cost_estimate=pl.CostEstimate(
            flops=8 * blocks * rows * keys * DH * heads,
            bytes_accessed=4 * blocks * rows * width + 4 * keys * width,
            transcendentals=blocks * rows * keys * heads,
        ),
        name="attend",
    )(table, kept, *queries, ctx_k, new_k, ctx_v, new_v, dep)


def combine(refs, width, emit):
    stats = []
    for ref in refs:
        terms = ref[0, width:, :].astype(jnp.float32)
        stats.append([terms[3 * h : 3 * h + 1] + terms[3 * h + 1 : 3 * h + 2] + terms[3 * h + 2 : 3 * h + 3]
                      for h in range(width // DH)])
    for head in range(width // DH):
        logs = [s[head] for s in stats]
        top = functools.reduce(jnp.maximum, logs)
        weights = [jnp.exp2(l - top) for l in logs]
        total = functools.reduce(jnp.add, weights)
        value = None
        for ref, weight in zip(refs, weights):
            part = ref[0, head * DH : (head + 1) * DH, :].astype(jnp.float32) * (weight / total)
            value = part if value is None else value + part
        emit(head, value, top + jnp.log2(total))


def join_kernel_of(sizes, final, table_ref, *refs):
    sources, at = [], 0
    for size in sizes:
        sources.append(refs[at : at + size])
        at += size
    if final:
        out_ref = refs[-1]
        width = out_ref.shape[1]
    else:
        out_ref, stat_ref = refs[-2:]
        width = out_ref.shape[1] - stat_ref.shape[0]

    def emit(head, value, log):
        at = slice(head * DH, (head + 1) * DH)
        if final:
            out_ref[:, at] = jnp.transpose(value).astype(jnp.bfloat16)
            return
        out_ref[0, at, :] = value.astype(jnp.bfloat16)
        for part, term in enumerate(split3(log)):
            stat_ref[3 * head + part : 3 * head + part + 1, :] = term

    for c, chosen in enumerate(sources):
        if chosen:

            @pl.when(table_ref[0] == c)
            def _():
                if not final:
                    stat_ref[...] = jnp.zeros_like(stat_ref)
                combine(chosen, width, emit)
                if not final:
                    out_ref[0, width:, :] = stat_ref[...].astype(jnp.bfloat16)


def join_parts(table, choices, width, dep, final, blocks=1):
    parts = [part for choice in choices for part in choice]
    _, prow, rows = parts[0][0].shape
    specs = [
        pl.BlockSpec((1, prow, rows), functools.partial(lambda slot, i, t: (slot + i, 0, 0), slot)) for _, slot in parts
    ]
    shape = (rows, width) if final else (blocks, prow, rows)
    out_spec = pl.BlockSpec(shape, lambda i, t: (0, 0)) if final else pl.BlockSpec((1, prow, rows), lambda i, t: (i, 0, 0))
    return pl.pallas_call(
        functools.partial(join_kernel_of, [len(c) for c in choices], final),
        out_shape=jax.ShapeDtypeStruct(shape, jnp.bfloat16),
        grid_spec=pltpu.PrefetchScalarGridSpec(
            num_scalar_prefetch=1,
            grid=(blocks,),
            in_specs=specs + [pl.BlockSpec(memory_space=pl.ANY)],
            out_specs=out_spec,
            scratch_shapes=[] if final else [pltpu.VMEM((prow - width, rows), jnp.float32)],
        ),
        compiler_params=pltpu.CompilerParams(vmem_limit_bytes=16 * MIB),
        cost_estimate=QUICK,
        name="finish" if final else "merge",
    )(table, *[array for array, _ in parts], dep)


def part_kernel(peers, count, start, peer_ref, *refs):
    rows = refs[0].shape[0]
    outs = refs[-peers:]
    for i, ref in enumerate(refs[: count * peers]):
        outs[i % peers][i // peers * rows : (i // peers + 1) * rows, :] = ref[:, start:]


def parts_for_peers(peer, arrays, start, peers, deps):
    rows, group = arrays[0].shape[0], arrays[0].shape[1] // peers
    specs = [pl.BlockSpec((rows, group), functools.partial(lambda k, i, t: (0, t[0] ^ k), k)) for k in range(peers)]
    shape = (len(arrays) * rows, group - start)
    return pl.pallas_call(
        functools.partial(part_kernel, peers, len(arrays), start),
        out_shape=[jax.ShapeDtypeStruct(shape, jnp.bfloat16)] * peers,
        grid_spec=pltpu.PrefetchScalarGridSpec(
            num_scalar_prefetch=1,
            grid=(1,),
            in_specs=specs * len(arrays) + [pl.BlockSpec(memory_space=pl.ANY)] * len(deps),
            out_specs=[pl.BlockSpec(shape, lambda i, t: (0, 0))] * peers,
        ),
        compiler_params=pltpu.CompilerParams(vmem_limit_bytes=28 * MIB),
        cost_estimate=QUICK,
        name="parts",
    )(peer.reshape(1), *[a for a in arrays for _ in range(peers)], *deps)


def regroup_kernel(peers, start, peer_ref, *refs):
    out_ref = refs[-1]
    rows, width = refs[0].shape[0], out_ref.shape[1]
    for k in range(peers):
        here = pl.ds(pl.multiple_of((peer_ref[0] ^ k) * rows, rows), rows)
        out_ref[here, :] = refs[k][:, start : start + width]


def regrouped(peer, pieces, start, width, deps):
    peers, rows = len(pieces), pieces[0].shape[0]
    whole = lambda i, t: (0, 0)
    shape = (peers * rows, width)
    return pl.pallas_call(
        functools.partial(regroup_kernel, peers, start),
        out_shape=jax.ShapeDtypeStruct(shape, jnp.bfloat16),
        grid_spec=pltpu.PrefetchScalarGridSpec(
            num_scalar_prefetch=1,
            grid=(1,),
            in_specs=[pl.BlockSpec(p.shape, whole) for p in pieces] + [pl.BlockSpec(memory_space=pl.ANY)] * len(deps),
            out_specs=pl.BlockSpec(shape, whole),
        ),
        compiler_params=pltpu.CompilerParams(vmem_limit_bytes=16 * MIB),
        cost_estimate=QUICK,
        name="regroup",
    )(peer.reshape(1), *pieces, *deps)


def join_kernel(*refs):
    pieces, (k_ref, v_ref, v_s) = refs[:-4], refs[-3:]
    rows = pieces[0].shape[0] // 2
    for i, piece in enumerate(pieces):
        k_ref[i * rows : (i + 1) * rows, :] = piece[:rows, :]
        v_s[i * rows : (i + 1) * rows, :] = piece[rows:, :]
    for at in range(0, v_s.shape[0], TILE):
        v_ref[:, at : at + TILE] = jnp.transpose(v_s[at : at + TILE, :])


def joined(pieces, dep):
    rows, group = pieces[0].shape[0] // 2 * len(pieces), pieces[0].shape[1]
    return pl.pallas_call(
        join_kernel,
        out_shape=[
            jax.ShapeDtypeStruct((rows, group), jnp.bfloat16),
            jax.ShapeDtypeStruct((group, rows), jnp.bfloat16),
        ],
        in_specs=[pl.BlockSpec(memory_space=pltpu.VMEM)] * len(pieces) + [pl.BlockSpec(memory_space=pl.ANY)],
        scratch_shapes=[pltpu.VMEM((rows, group), jnp.bfloat16)],
        compiler_params=pltpu.CompilerParams(vmem_limit_bytes=24 * MIB),
        cost_estimate=QUICK,
        name="join",
    )(*pieces, dep)


def shards(new_queries, new_keys, new_values, context_keys, context_values, keep_flags):
    n = lax.axis_size("blk")
    place = lax.axis_index("blk").astype(jnp.int32)
    peers = lax.axis_size("uly")
    own_rows = new_queries.shape[0]
    group = context_keys.shape[1]
    unit = group // PIECE_UNITS
    span_rows = own_rows * peers
    ctx_tiles, new_tiles = context_keys.shape[0] // TILE, span_rows // TILE

    peer = lax.axis_index("uly").astype(jnp.int32)
    new_order = jnp.arange(new_tiles, dtype=jnp.int32) ^ (peer * own_rows // TILE)
    new_kept = lax.dynamic_slice_in_dim(keep_flags, n * ctx_tiles + place * new_tiles, new_tiles, 1)
    kept = jnp.concatenate(
        [
            lax.dynamic_slice_in_dim(keep_flags, place * ctx_tiles, ctx_tiles, 1),
            jnp.sum(jnp.where(new_order[:, None] == jnp.arange(new_tiles), new_kept[:, None, :], 0), axis=2),
        ],
        axis=1,
    )
    kept = (kept == 1).astype(jnp.int32)
    count = len(PIECES)
    widths = [units * unit for _, units in PIECES]
    backs = [None] * count

    def to_heads(pieces):
        moved = lax.all_to_all(pieces, "uly", split_axis=0, concat_axis=0, tiled=False)
        return moved.reshape(span_rows, pieces.shape[2])

    def to_peers(pieces):
        return [lax.ppermute(p, "uly", [(i, i ^ k) for i in range(peers)]) if k else p for k, p in enumerate(pieces)]

    def send(x, *pairs):
        return lax.ppermute(x, "blk", pairs)

    def spread_line(span):
        near = send(span, (0, 1), (1, 0), (2, 3), (3, 2))
        third = send(span, (1, 2), (2, 1))
        far = send(near, (1, 2), (2, 1))
        third_out = send(third, (1, 0), (2, 3))
        far_out = send(far, (1, 0), (2, 3))
        return dict(own=span, near=near, sent=[[far, third], [far_out, third_out]], early=third, mid=third_out)

    def spread_cube(span):
        found = {0: span}
        for bit in reversed(bits):
            for d in list(found):
                found[d ^ bit] = send(found[d], *[(i, i ^ bit) for i in range(n)])
        return dict(found=found, early=found[n // 2], mid=found[n // 2])

    bits = [1 << k for k in range((n - 1).bit_length())]
    line = n == 4
    spread = spread_line if line else spread_cube
    early = widths[0]
    first_span = to_heads(jnp.stack([new_queries[:, p * group : p * group + early] for p in range(peers)]))
    found = [spread(first_span)]
    parts_q = parts_for_peers(peer, [new_queries], early, peers, [first_span])
    later = to_peers(parts_q)
    parts_kv = parts_for_peers(peer, [new_keys, new_values], 0, peers, [*later, found[0]["early"]])

    def run_spread(c, deps):
        span = regrouped(peer, later, PIECES[c][0] * unit - early, widths[c], deps)
        found.append(spread(span))
        return span

    latest = parts_kv[0]
    for c in range(1, count):
        latest = run_spread(c, [found[c - 1]["early"], latest])
    span_k, span_v_t = joined(to_peers(parts_kv), latest)
    context_values_t = context_values.T
    last = [span_k]
    outer = ((place == 0) | (place == n - 1)).astype(jnp.int32)
    low = place < n // 2

    def run_attend(c, choices, targets):
        table = jnp.stack([outer, *targets]).astype(jnp.int32)
        own = attend(
            table, kept, choices, context_keys, span_k, context_values_t, span_v_t, PIECES[c][0] // PIECES[c][1], last[0]
        )
        last[0] = own
        return own

    def run_join(c, choices, final=False, blocks=1):
        last[0] = join_parts(outer.reshape(1), choices, widths[c], last[0], final, blocks)
        return last[0]

    def run_back(c, choices):
        backs[c] = run_join(c, choices, True).reshape(peers, own_rows, widths[c])

    def run_return(*those):
        joint = jnp.concatenate([backs[c] for c in those], axis=2)
        joint = lax.all_to_all(joint, "uly", split_axis=0, concat_axis=0, tiled=False)
        at = 0
        for c in those:
            backs[c] = joint[:, :, at : at + widths[c]]
            at += widths[c]

    state = [dict() for _ in range(count)]

    def run_sent(c):
        mine = run_attend(c, found[c]["sent"], [jnp.where(low, 3, 0), jnp.where(low, 2, 1)])
        state[c].update(far=mine, edge=send(mine, (0, 1), (3, 2)))

    def run_kept(c):
        blocks = [found[c]["near"], found[c]["own"]]
        mine = run_attend(c, [blocks, blocks], [place ^ 1, place])
        state[c].update(kept=mine, edge_near=send(mine[:1], (0, 1), (3, 2)))

    def run_cross(c):
        joint = run_join(c, [[(state[c]["far"], 0), (state[c]["edge"], 0)], []], blocks=2)
        state[c]["cross"] = send(joint, (1, 2), (2, 1))

    def run_outward(c):
        joint = run_join(c, [[(state[c]["kept"], 0), (state[c]["cross"], 0)], []])
        state[c]["outward"] = send(joint, (1, 0), (2, 3))

    def run_finish(c):
        inner = [(state[c]["kept"], 1), (state[c]["edge_near"], 0), (state[c]["cross"], 1)]
        run_back(c, [inner, [(state[c]["kept"], 1), (state[c]["outward"], 0)]])

    def run_halves(c):
        inner, outer_ones = found[c]["sent"]
        near, own = found[c]["near"], found[c]["own"]
        mine = run_attend(c, [[near, inner[1]], [near, outer_ones[0]]], [place ^ 1, place ^ 3])
        state[c].update(swap=send(mine, (0, 1), (1, 0), (2, 3), (3, 2)), rest=[[own, inner[0]], [own, outer_ones[1]]])

    def run_halves_kept(c):
        state[c]["kept"] = run_attend(c, state[c]["rest"], [place, place ^ 2])

    def run_halves_join(c):
        pair = [(state[c]["kept"], 1), (state[c]["swap"], 1)]
        state[c]["across"] = send(run_join(c, [pair, pair]), (0, 2), (2, 0), (1, 3), (3, 1))

    def run_halves_finish(c):
        three = [(state[c]["kept"], 0), (state[c]["swap"], 0), (state[c]["across"], 0)]
        run_back(c, [three, three])

    if line:
        run_sent(0)
        run_kept(0)
        run_sent(1)
        run_cross(0)
        run_kept(1)
        run_cross(1)
        run_halves(2)
        run_outward(0)
        run_halves_kept(2)
        run_outward(1)
        run_halves_join(2)
        run_finish(0)
        run_finish(1)
        run_return(0, 1)
        run_halves_finish(2)
        run_return(2)
    else:
        for c in range(count):
            parts = {d: [] for d in range(n)}
            for distances in (range(1, n, 2), range(0, n, 2)):
                blocks = [found[c]["found"][d] for d in distances]
                mine = run_attend(c, [blocks, blocks], [place ^ d for d in distances])
                for slot, d in enumerate(distances):
                    parts[d].append((mine, slot))
                if 1 in distances:
                    moved = send(mine, *[(i, i ^ 1) for i in range(n)])
            for slot, d in enumerate(range(0, n, 2)):
                parts[d].append((moved, slot))
            for bit in bits[1:]:
                for d in range(bit, n, 2 * bit):
                    joint = run_join(c, [parts[d], parts[d]])
                    parts[d ^ bit].append((send(joint, *[(i, i ^ bit) for i in range(n)]), 0))
            run_back(c, [parts[0], parts[0]])
            run_return(c)

    in_order = [backs[c] for c in sorted(range(count), key=lambda c: PIECES[c][0])]
    together = jnp.concatenate(in_order, axis=2)
    return together.transpose(1, 0, 2).reshape(own_rows, peers * group)


def solution(mesh):
    in_specs = (
        P(("cfg", "blk", "uly"), None),
        P(("cfg", "blk", "uly"), None),
        P(("cfg", "blk", "uly"), None),
        P(("cfg", "blk"), "uly"),
        P(("cfg", "blk"), "uly"),
        P(),
    )
    out_specs = P(("cfg", "blk", "uly"), None)
    return jax.shard_map(shards, mesh=mesh, in_specs=in_specs, out_specs=out_specs, check_vma=False)
```

```python
import functools

import jax
import jax.numpy as jnp
from jax import lax
from jax.experimental import pallas as pl
from jax.experimental.pallas import tpu as pltpu
from jax.sharding import PartitionSpec as P

DH = 128
TILE = 128
PIECES = ((0, 1), (1, 1), (2, 1))
PIECE_UNITS = 3
HALF = 256
CHUNK = 256
LOG2E = 1.4426950408889634
TINY = 1.0e-30
ONES = 16
SCALE2 = DH ** (-0.5) * LOG2E
MASKED = -1.0e30
MIB = 1024 * 1024
QUICK = pl.CostEstimate(flops=1024, bytes_accessed=1024, transcendentals=0)


def split3(x):
    hi = x.astype(jnp.bfloat16).astype(jnp.float32)
    rest = x - hi
    mid = rest.astype(jnp.bfloat16).astype(jnp.float32)
    lo = (rest - mid).astype(jnp.bfloat16).astype(jnp.float32)
    return hi, mid, lo


def stat_rows(width):
    return -(-3 * (width // DH) // 16) * 16


def attend_kernel(choices, table_ref, kept_ref, *refs):
    count = sum(len(c) for c in choices)
    sources, at = [], 0
    for c in choices:
        sources.append(refs[at : at + len(c)])
        at += len(c)
    ck_ref, nk_ref, cv_ref, nv_ref = refs[count : count + 4]
    out_ref, q_s, s0, s1, m0, m1, stat_s = refs[-7:]
    rows = q_s.shape[0]
    width = q_s.shape[1] // 2
    heads = width // DH
    ctx, new = ck_ref.shape[0], nk_ref.shape[0]
    subs = HALF // TILE
    halves = rows // HALF
    slots = ((s0, m0), (s1, m1))
    nt = (((1,), (1,)), ((), ()))
    step_no = pl.program_id(0)
    first_tile = table_ref[1 + step_no] * (rows // TILE)
    stat_s[...] = jnp.zeros_like(stat_s)
    for c, q_refs in enumerate(sources):
        for i, q_ref in enumerate(q_refs):

            @pl.when((step_no == i) & (table_ref[0] == c))
            def _():
                for head in range(heads):
                    scaled = q_ref[:, head * DH : (head + 1) * DH].astype(jnp.float32) * SCALE2
                    hi = scaled.astype(jnp.bfloat16)
                    lo = (scaled - hi.astype(jnp.float32)).astype(jnp.bfloat16)
                    q_s[:, 2 * head * DH : (2 * head + 1) * DH] = hi
                    q_s[:, (2 * head + 1) * DH : (2 * head + 2) * DH] = lo

    def columns(head, size=DH):
        return pl.ds(pl.multiple_of(head * size, size), size)

    chunks = [(k, v, at, base) for k, v, size, base in ((ck_ref, cv_ref, ctx, 0), (nk_ref, nv_ref, new, ctx))
              for at in range(0, size, CHUNK)]

    def kept(half, sub, row):
        return kept_ref[first_tile + half * subs + sub, row // TILE] > 0

    def score(head, half, chunk, q, tops):
        s_ref = slots[half % 2][0]
        k_ref, _, at, base = chunk
        size = min(CHUNK, k_ref.shape[0] - at)
        k = k_ref[at : at + size, columns(head)]
        scores = lax.dot_general(jnp.concatenate([k, k], axis=1), q, nt, preferred_element_type=jnp.float32)
        s_ref[base + at : base + at + size, :] = scores
        for j in range(0, size, TILE):
            for sub in range(subs):
                piece = scores[j : j + TILE, sub * TILE : (sub + 1) * TILE]
                top = jnp.max(piece.reshape(TILE // 8, 8, TILE), axis=0)
                top = jnp.where(kept(half, sub, base + at + j), top, MASKED)
                tops[sub] = top if tops[sub] is None else jnp.maximum(tops[sub], top)

    def weigh(head, half, chunk, high):
        s_ref = slots[half % 2][0]
        _, v_ref, at, base = chunk
        size = min(CHUNK, v_ref.shape[1] - at)
        lows = []
        for j in range(0, size, TILE):
            row = base + at + j
            pieces = []
            for sub in range(subs):
                lanes = slice(sub * TILE, (sub + 1) * TILE)
                less = jnp.where(kept(half, sub, row), high[:, lanes], -MASKED)
                pieces.append(jnp.exp2(s_ref[row : row + TILE, lanes] - less).astype(jnp.bfloat16))
            lows.append(jnp.concatenate(pieces, axis=1))
        low = jnp.concatenate(lows, axis=0)
        values = jnp.concatenate([v_ref[columns(head), at : at + size], jnp.ones((ONES, size), jnp.bfloat16)], axis=0)
        return jnp.dot(values, low, preferred_element_type=jnp.float32)

    def step(head, half, next_head, next_half, both=True):
        q = q_s[next_half * HALF : (next_half + 1) * HALF, columns(next_head, 2 * DH)]
        tops = [None] * subs
        if both:
            high = jnp.max(slots[half % 2][1][...], axis=0, keepdims=True)
            acc = None
        for chunk in chunks:
            score(next_head, next_half, chunk, q, tops)
            if both:
                found = weigh(head, half, chunk, high)
                acc = found if acc is None else acc + found
        for sub in range(subs):
            slots[next_half % 2][1][:, sub * TILE : (sub + 1) * TILE] = tops[sub]
        if both:
            total = jnp.maximum(acc[DH : DH + 1, :], TINY)
            lanes = slice(half * HALF, (half + 1) * HALF)
            out_ref[0, columns(head), lanes] = (acc[:DH, :] * (1.0 / total)).astype(jnp.bfloat16)
            for part, value in enumerate(split3(high + jnp.log2(total))):
                stat_s[pl.ds(3 * head + part, 1), lanes] = value

    step(0, 1, 0, 0, both=False)

    @pl.loop(0, heads)
    def _(head):
        for half in range(halves):
            if half + 1 < halves:
                step(head, half, head, half + 1)
            else:
                step(head, half, jnp.minimum(head + 1, heads - 1), 0)

    out_ref[0, width:, :] = stat_s[...].astype(jnp.bfloat16)


def attend(table, kept, choices, ctx_k, new_k, ctx_v, new_v, piece, dep):
    queries = [q for choice in choices for q in choice]
    rows, width = queries[0].shape
    ctx, new = ctx_k.shape[0], new_k.shape[0]
    heads = width // DH
    keys = ctx + new
    blocks = len(choices[0])
    across = lambda i, t, b: (0, piece)
    down = lambda i, t, b: (piece, 0)
    prow = width + stat_rows(width)
    return pl.pallas_call(
        functools.partial(attend_kernel, [[None] * len(c) for c in choices]),
        out_shape=jax.ShapeDtypeStruct((blocks, prow, rows), jnp.bfloat16),
        grid_spec=pltpu.PrefetchScalarGridSpec(
            num_scalar_prefetch=2,
            grid=(blocks,),
            in_specs=[pl.BlockSpec((rows, width), lambda i, t, b: (0, 0))] * len(queries)
            + [
                pl.BlockSpec((ctx, width), across),
                pl.BlockSpec((new, width), across),
                pl.BlockSpec((width, ctx), down),
                pl.BlockSpec((width, new), down),
                pl.BlockSpec(memory_space=pl.ANY),
            ],
            out_specs=pl.BlockSpec((1, prow, rows), lambda i, t, b: (i, 0, 0)),
            scratch_shapes=[
                pltpu.VMEM((rows, 2 * width), jnp.bfloat16),
                pltpu.VMEM((keys, HALF), jnp.float32),
                pltpu.VMEM((keys, HALF), jnp.float32),
                pltpu.VMEM((8, HALF), jnp.float32),
                pltpu.VMEM((8, HALF), jnp.float32),
                pltpu.VMEM((stat_rows(width), rows), jnp.float32),
            ],
        ),
        compiler_params=pltpu.CompilerParams(vmem_limit_bytes=22 * MIB),
        cost_estimate=pl.CostEstimate(
            flops=8 * blocks * rows * keys * DH * heads,
            bytes_accessed=4 * blocks * rows * width + 4 * keys * width,
            transcendentals=blocks * rows * keys * heads,
        ),
        name="attend",
    )(table, kept, *queries, ctx_k, new_k, ctx_v, new_v, dep)


def combine(refs, width, emit):
    stats = []
    for ref in refs:
        terms = ref[0, width:, :].astype(jnp.float32)
        stats.append([terms[3 * h : 3 * h + 1] + terms[3 * h + 1 : 3 * h + 2] + terms[3 * h + 2 : 3 * h + 3]
                      for h in range(width // DH)])
    for head in range(width // DH):
        logs = [s[head] for s in stats]
        top = functools.reduce(jnp.maximum, logs)
        weights = [jnp.exp2(l - top) for l in logs]
        total = functools.reduce(jnp.add, weights)
        value = None
        for ref, weight in zip(refs, weights):
            part = ref[0, head * DH : (head + 1) * DH, :].astype(jnp.float32) * (weight / total)
            value = part if value is None else value + part
        emit(head, value, top + jnp.log2(total))


def join_kernel_of(sizes, final, table_ref, *refs):
    sources, at = [], 0
    for size in sizes:
        sources.append(refs[at : at + size])
        at += size
    if final:
        out_ref = refs[-1]
        width = out_ref.shape[1]
    else:
        out_ref, stat_ref = refs[-2:]
        width = out_ref.shape[1] - stat_ref.shape[0]

    def emit(head, value, log):
        at = slice(head * DH, (head + 1) * DH)
        if final:
            out_ref[:, at] = jnp.transpose(value).astype(jnp.bfloat16)
            return
        out_ref[0, at, :] = value.astype(jnp.bfloat16)
        for part, term in enumerate(split3(log)):
            stat_ref[3 * head + part : 3 * head + part + 1, :] = term

    for c, chosen in enumerate(sources):
        if chosen:

            @pl.when(table_ref[0] == c)
            def _():
                if not final:
                    stat_ref[...] = jnp.zeros_like(stat_ref)
                combine(chosen, width, emit)
                if not final:
                    out_ref[0, width:, :] = stat_ref[...].astype(jnp.bfloat16)


def join_parts(table, choices, width, dep, final, blocks=1):
    parts = [part for choice in choices for part in choice]
    _, prow, rows = parts[0][0].shape
    specs = [
        pl.BlockSpec((1, prow, rows), functools.partial(lambda slot, i, t: (slot + i, 0, 0), slot)) for _, slot in parts
    ]
    shape = (rows, width) if final else (blocks, prow, rows)
    out_spec = pl.BlockSpec(shape, lambda i, t: (0, 0)) if final else pl.BlockSpec((1, prow, rows), lambda i, t: (i, 0, 0))
    return pl.pallas_call(
        functools.partial(join_kernel_of, [len(c) for c in choices], final),
        out_shape=jax.ShapeDtypeStruct(shape, jnp.bfloat16),
        grid_spec=pltpu.PrefetchScalarGridSpec(
            num_scalar_prefetch=1,
            grid=(blocks,),
            in_specs=specs + [pl.BlockSpec(memory_space=pl.ANY)],
            out_specs=out_spec,
            scratch_shapes=[] if final else [pltpu.VMEM((prow - width, rows), jnp.float32)],
        ),
        compiler_params=pltpu.CompilerParams(vmem_limit_bytes=16 * MIB),
        cost_estimate=QUICK,
        name="finish" if final else "merge",
    )(table, *[array for array, _ in parts], dep)


def part_kernel(peers, count, start, peer_ref, *refs):
    rows = refs[0].shape[0]
    outs = refs[-peers:]
    for i, ref in enumerate(refs[: count * peers]):
        outs[i % peers][i // peers * rows : (i // peers + 1) * rows, :] = ref[:, start:]


def parts_for_peers(peer, arrays, start, peers, deps):
    rows, group = arrays[0].shape[0], arrays[0].shape[1] // peers
    specs = [pl.BlockSpec((rows, group), functools.partial(lambda k, i, t: (0, t[0] ^ k), k)) for k in range(peers)]
    shape = (len(arrays) * rows, group - start)
    return pl.pallas_call(
        functools.partial(part_kernel, peers, len(arrays), start),
        out_shape=[jax.ShapeDtypeStruct(shape, jnp.bfloat16)] * peers,
        grid_spec=pltpu.PrefetchScalarGridSpec(
            num_scalar_prefetch=1,
            grid=(1,),
            in_specs=specs * len(arrays) + [pl.BlockSpec(memory_space=pl.ANY)] * len(deps),
            out_specs=[pl.BlockSpec(shape, lambda i, t: (0, 0))] * peers,
        ),
        compiler_params=pltpu.CompilerParams(vmem_limit_bytes=22 * MIB),
        cost_estimate=QUICK,
        name="parts",
    )(peer.reshape(1), *[a for a in arrays for _ in range(peers)], *deps)


def regroup_kernel(peers, start, peer_ref, *refs):
    out_ref = refs[-1]
    rows, width = refs[0].shape[0], out_ref.shape[1]
    for k in range(peers):
        here = pl.ds(pl.multiple_of((peer_ref[0] ^ k) * rows, rows), rows)
        out_ref[here, :] = refs[k][:, start : start + width]


def regrouped(peer, pieces, start, width, deps):
    peers, rows = len(pieces), pieces[0].shape[0]
    whole = lambda i, t: (0, 0)
    shape = (peers * rows, width)
    return pl.pallas_call(
        functools.partial(regroup_kernel, peers, start),
        out_shape=jax.ShapeDtypeStruct(shape, jnp.bfloat16),
        grid_spec=pltpu.PrefetchScalarGridSpec(
            num_scalar_prefetch=1,
            grid=(1,),
            in_specs=[pl.BlockSpec(p.shape, whole) for p in pieces] + [pl.BlockSpec(memory_space=pl.ANY)] * len(deps),
            out_specs=pl.BlockSpec(shape, whole),
        ),
        compiler_params=pltpu.CompilerParams(vmem_limit_bytes=16 * MIB),
        cost_estimate=QUICK,
        name="regroup",
    )(peer.reshape(1), *pieces, *deps)


def join_kernel(*refs):
    pieces, (k_ref, v_ref, v_s) = refs[:-4], refs[-3:]
    rows = pieces[0].shape[0] // 2
    for i, piece in enumerate(pieces):
        k_ref[i * rows : (i + 1) * rows, :] = piece[:rows, :]
        v_s[i * rows : (i + 1) * rows, :] = piece[rows:, :]
    for at in range(0, v_s.shape[0], TILE):
        v_ref[:, at : at + TILE] = jnp.transpose(v_s[at : at + TILE, :])


def joined(pieces, dep):
    rows, group = pieces[0].shape[0] // 2 * len(pieces), pieces[0].shape[1]
    return pl.pallas_call(
        join_kernel,
        out_shape=[
            jax.ShapeDtypeStruct((rows, group), jnp.bfloat16),
            jax.ShapeDtypeStruct((group, rows), jnp.bfloat16),
        ],
        in_specs=[pl.BlockSpec(memory_space=pltpu.VMEM)] * len(pieces) + [pl.BlockSpec(memory_space=pl.ANY)],
        scratch_shapes=[pltpu.VMEM((rows, group), jnp.bfloat16)],
        compiler_params=pltpu.CompilerParams(vmem_limit_bytes=24 * MIB),
        cost_estimate=QUICK,
        name="join",
    )(*pieces, dep)


def shards(new_queries, new_keys, new_values, context_keys, context_values, keep_flags):
    n = lax.axis_size("blk")
    place = lax.axis_index("blk").astype(jnp.int32)
    peers = lax.axis_size("uly")
    own_rows = new_queries.shape[0]
    group = context_keys.shape[1]
    unit = group // PIECE_UNITS
    span_rows = own_rows * peers
    ctx_tiles, new_tiles = context_keys.shape[0] // TILE, span_rows // TILE

    peer = lax.axis_index("uly").astype(jnp.int32)
    new_order = jnp.arange(new_tiles, dtype=jnp.int32) ^ (peer * own_rows // TILE)
    new_kept = lax.dynamic_slice_in_dim(keep_flags, n * ctx_tiles + place * new_tiles, new_tiles, 1)
    kept = jnp.concatenate(
        [
            lax.dynamic_slice_in_dim(keep_flags, place * ctx_tiles, ctx_tiles, 1),
            jnp.sum(jnp.where(new_order[:, None] == jnp.arange(new_tiles), new_kept[:, None, :], 0), axis=2),
        ],
        axis=1,
    )
    kept = (kept == 1).astype(jnp.int32)
    count = len(PIECES)
    widths = [units * unit for _, units in PIECES]
    backs = [None] * count

    def to_heads(pieces):
        moved = lax.all_to_all(pieces, "uly", split_axis=0, concat_axis=0, tiled=False)
        return moved.reshape(span_rows, pieces.shape[2])

    def to_peers(pieces):
        return [lax.ppermute(p, "uly", [(i, i ^ k) for i in range(peers)]) if k else p for k, p in enumerate(pieces)]

    def send(x, *pairs):
        return lax.ppermute(x, "blk", pairs)

    def spread_line(span):
        near = send(span, (0, 1), (1, 0), (2, 3), (3, 2))
        third = send(span, (1, 2), (2, 1))
        far = send(near, (1, 2), (2, 1))
        third_out = send(third, (1, 0), (2, 3))
        far_out = send(far, (1, 0), (2, 3))
        return dict(own=span, near=near, sent=[[far, third], [far_out, third_out]], early=third, mid=third_out)

    def spread_cube(span):
        found = {0: span}
        for bit in reversed(bits):
            for d in list(found):
                found[d ^ bit] = send(found[d], *[(i, i ^ bit) for i in range(n)])
        return dict(found=found, early=found[n // 2], mid=found[n // 2])

    bits = [1 << k for k in range((n - 1).bit_length())]
    line = n == 4
    spread = spread_line if line else spread_cube
    early = widths[0]
    first_span = to_heads(jnp.stack([new_queries[:, p * group : p * group + early] for p in range(peers)]))
    found = [spread(first_span)]
    parts_q = parts_for_peers(peer, [new_queries], early, peers, [first_span])
    later = to_peers(parts_q)
    parts_kv = parts_for_peers(peer, [new_keys, new_values], 0, peers, [*later, found[0]["early"]])

    def run_spread(c, deps):
        span = regrouped(peer, later, PIECES[c][0] * unit - early, widths[c], deps)
        found.append(spread(span))
        return span

    latest = parts_kv[0]
    for c in range(1, count):
        latest = run_spread(c, [found[c - 1]["early"], latest])
    span_k, span_v_t = joined(to_peers(parts_kv), latest)
    context_values_t = context_values.T
    last = [span_k]
    outer = ((place == 0) | (place == n - 1)).astype(jnp.int32)
    low = place < n // 2

    def run_attend(c, choices, targets):
        table = jnp.stack([outer, *targets]).astype(jnp.int32)
        own = attend(
            table, kept, choices, context_keys, span_k, context_values_t, span_v_t, PIECES[c][0] // PIECES[c][1], last[0]
        )
        last[0] = own
        return own

    def run_join(c, choices, final=False, blocks=1):
        last[0] = join_parts(outer.reshape(1), choices, widths[c], last[0], final, blocks)
        return last[0]

    def run_back(c, choices):
        backs[c] = run_join(c, choices, True).reshape(peers, own_rows, widths[c])

    def run_return(*those):
        joint = jnp.concatenate([backs[c] for c in those], axis=2)
        joint = lax.all_to_all(joint, "uly", split_axis=0, concat_axis=0, tiled=False)
        at = 0
        for c in those:
            backs[c] = joint[:, :, at : at + widths[c]]
            at += widths[c]

    state = [dict() for _ in range(count)]

    def run_sent(c):
        mine = run_attend(c, found[c]["sent"], [jnp.where(low, 3, 0), jnp.where(low, 2, 1)])
        state[c].update(far=mine, edge=send(mine, (0, 1), (3, 2)))

    def run_kept(c):
        blocks = [found[c]["near"], found[c]["own"]]
        mine = run_attend(c, [blocks, blocks], [place ^ 1, place])
        state[c].update(kept=mine, edge_near=send(mine[:1], (0, 1), (3, 2)))

    def run_cross(c):
        joint = run_join(c, [[(state[c]["far"], 0), (state[c]["edge"], 0)], []], blocks=2)
        state[c]["cross"] = send(joint, (1, 2), (2, 1))

    def run_outward(c):
        joint = run_join(c, [[(state[c]["kept"], 0), (state[c]["cross"], 0)], []])
        state[c]["outward"] = send(joint, (1, 0), (2, 3))

    def run_finish(c):
        inner = [(state[c]["kept"], 1), (state[c]["edge_near"], 0), (state[c]["cross"], 1)]
        run_back(c, [inner, [(state[c]["kept"], 1), (state[c]["outward"], 0)]])

    def run_halves(c):
        inner, outer_ones = found[c]["sent"]
        near, own = found[c]["near"], found[c]["own"]
        mine = run_attend(c, [[near, inner[1]], [near, outer_ones[0]]], [place ^ 1, place ^ 3])
        state[c].update(swap=send(mine, (0, 1), (1, 0), (2, 3), (3, 2)), rest=[[own, inner[0]], [own, outer_ones[1]]])

    def run_halves_kept(c):
        state[c]["kept"] = run_attend(c, state[c]["rest"], [place, place ^ 2])

    def run_halves_join(c):
        pair = [(state[c]["kept"], 1), (state[c]["swap"], 1)]
        state[c]["across"] = send(run_join(c, [pair, pair]), (0, 2), (2, 0), (1, 3), (3, 1))

    def run_halves_finish(c):
        three = [(state[c]["kept"], 0), (state[c]["swap"], 0), (state[c]["across"], 0)]
        run_back(c, [three, three])

    if line:
        run_sent(0)
        run_kept(0)
        run_sent(1)
        run_cross(0)
        run_kept(1)
        run_halves(2)
        run_outward(0)
        run_cross(1)
        run_halves_kept(2)
        run_halves_join(2)
        run_outward(1)
        run_finish(0)
        run_return(0)
        run_finish(1)
        run_halves_finish(2)
        run_return(1, 2)
    else:
        for c in range(count):
            parts = {d: [] for d in range(n)}
            for distances in (range(1, n, 2), range(0, n, 2)):
                blocks = [found[c]["found"][d] for d in distances]
                mine = run_attend(c, [blocks, blocks], [place ^ d for d in distances])
                for slot, d in enumerate(distances):
                    parts[d].append((mine, slot))
                if 1 in distances:
                    moved = send(mine, *[(i, i ^ 1) for i in range(n)])
            for slot, d in enumerate(range(0, n, 2)):
                parts[d].append((moved, slot))
            for bit in bits[1:]:
                for d in range(bit, n, 2 * bit):
                    joint = run_join(c, [parts[d], parts[d]])
                    parts[d ^ bit].append((send(joint, *[(i, i ^ bit) for i in range(n)]), 0))
            run_back(c, [parts[0], parts[0]])
            run_return(c)

    in_order = [backs[c] for c in sorted(range(count), key=lambda c: PIECES[c][0])]
    together = jnp.concatenate(in_order, axis=2)
    return together.transpose(1, 0, 2).reshape(own_rows, peers * group)


def solution(mesh):
    in_specs = (
        P(("cfg", "blk", "uly"), None),
        P(("cfg", "blk", "uly"), None),
        P(("cfg", "blk", "uly"), None),
        P(("cfg", "blk"), "uly"),
        P(("cfg", "blk"), "uly"),
        P(),
    )
    out_specs = P(("cfg", "blk", "uly"), None)
    return jax.shard_map(shards, mesh=mesh, in_specs=in_specs, out_specs=out_specs, check_vma=False)
```
